32 devices in a mesh: section: 4 (over y, x), dp: 8 (over z, core).
Axes of the slice: x: 2, y: 2, z: 4, core: 2. Of those that a mesh axis runs over, the one named last changes fastest.
Arguments:
- tokens: bfloat16 [2048, 1024], P('dp', 'section'), may hold values from -6 to 6
- cotangent: bfloat16 [2048, 1024], P('dp', 'section'), may hold values from -6 to 6
- gains: float32 [4, 1024], P('section'), may hold values from 0.5 to 1.5
- attn_in: bfloat16 [4, 1024, 1536], P('section'), may hold values from -0.1875 to 0.1875
- attn_out: bfloat16 [4, 512, 1024], P('section'), may hold values from -0.75 to 0.75
- ffn_in: bfloat16 [4, 1024, 2816], P('section'), may hold values from -0.1875 to 0.1875
- ffn_out: bfloat16 [4, 1408, 1024], P('section'), may hold values from -0.15625 to 0.15625
- mix_level: int32 [16], replicated, may hold values from 1 to 7
- seq_lengths: int32 [16, 4], P('dp'), may hold values from 0 to 128, as said below
Outputs:
- outputs: bfloat16 [2048, 1024], P('dp', 'section')
- input_grad: float32 [2048, 1024], P('dp', 'section')
- gains_grad: float32 [4, 1024], P('section')
- attn_in_grad: float32 [4, 1024, 1536], P('section')
- attn_out_grad: float32 [4, 512, 1024], P('section')
- ffn_in_grad: float32 [4, 1024, 2816], P('section')
- ffn_out_grad: float32 [4, 1408, 1024], P('section')
- value_norm: float32 [], replicated
- blend_norm: float32 [], replicated
The draws below stay inside these ranges and needn't reach their ends.
Inputs may be any that keep to these rules, and one draw needn't show every extreme that they name: `seq_lengths`: each row sums to 128; in every draw some row is a single sequence of 128 tokens; a length may be 0.
All inputs are finite; a program needn't handle non-finite values.
Results may differ from the reference program's by a relative error of at most 0.024.
Values may be sent and summed in bfloat16 or wider, within the bound.
No kernel may reach another device: no remote copies, remote signals or barrier semaphores. Data moves between devices by JAX's collectives and lax.ppermute only.
A program may use at most 256 MiB of HBM per device.

```python
import jax
import jax.numpy as jnp
from jax import lax

D = 1024
HEADS = 16
HEAD_DIM = 64
FF = 2816
SLOT = 128
PIECES = 4
SLOTS = 16
TOKENS = 2048
N_SECTION = 4


def draw_seq_lengths(key, part):
    key = jax.random.fold_in(key, 11)
    cut_key, whole_key, forced_key = jax.random.split(key, 3)
    cuts = jnp.sort(jax.random.randint(cut_key, (SLOTS, PIECES - 1), 0, SLOT + 1), axis=1)
    starts = jnp.concatenate([jnp.zeros((SLOTS, 1), jnp.int32), cuts], axis=1)
    ends = jnp.concatenate([cuts, jnp.full((SLOTS, 1), SLOT, jnp.int32)], axis=1)
    ragged = ends - starts
    single = jnp.zeros((PIECES,), jnp.int32).at[0].set(SLOT)
    whole_rows = jax.random.randint(whole_key, (SLOTS, 1), 0, 4) == 0
    forced = jnp.arange(SLOTS)[:, None] == jax.random.randint(forced_key, (), 0, SLOTS)
    return jnp.where(whole_rows | forced, single[None, :], ragged).astype(jnp.int32)


def plant(values, rng, least, top_value):
    index_at = [jax.random.randint(jax.random.fold_in(rng, axis), (), 0, length) for axis, length in enumerate(values.shape)]
    longest = values.shape.index(max(values.shape))
    beside = index_at[:longest] + [(index_at[longest] + 1) % values.shape[longest]] + index_at[longest + 1:]
    return values.at[tuple(index_at)].set(least).at[tuple(beside)].set(top_value)


def block_levels(key, shape, cuts, least, top_value):
    factor_of, own = 1.0, jax.random.fold_in(key, 6)
    for position, blocks in cuts:
        draws = jnp.exp(jax.random.uniform(jax.random.fold_in(own, position), (blocks,), jnp.float32, least / len(cuts), top_value / len(cuts)))
        factor_of = factor_of * jnp.repeat(draws, shape[position] // blocks).reshape([-1 if axis == position else 1 for axis in range(len(shape))])
    return factor_of


def normal_values(rng, shape, scale, most, cuts=(), held_as=jnp.bfloat16):
    level = block_levels(rng, shape, cuts, -0.22, 0.18) if cuts else 1.0
    drawn = jax.random.normal(rng, shape, jnp.float32) * scale * level
    return jnp.minimum(jnp.maximum(drawn, -most), most).astype(held_as)


def setup_inputs(seed: int = 0) -> dict:
    key_of = jax.random.split(jax.random.key(seed), 10)
    return {
        "tokens": normal_values(key_of[0], (TOKENS, D), 1.0, 6.0, ((0, 8), (1, 4))),
        "cotangent": normal_values(key_of[1], (TOKENS, D), 1.0, 6.0, ((0, 8), (1, 4))),
        "gains": jnp.clip(1.0 + 0.1 * jax.random.normal(key_of[2], (N_SECTION, D), jnp.float32), 0.5, 1.5),
        "attn_in": normal_values(key_of[3], (N_SECTION, D, 3 * HEADS * HEAD_DIM // 2), D ** -0.5, 0.1875, ((0, 4),)),
        "attn_out": normal_values(key_of[4], (N_SECTION, HEADS * HEAD_DIM // 2, D), (HEADS * HEAD_DIM // 16) ** -0.5, 0.75, ((0, 4),)),
        "ffn_in": normal_values(key_of[5], (N_SECTION, D, FF), D ** -0.5, 0.1875, ((0, 4),)),
        "ffn_out": normal_values(key_of[6], (N_SECTION, FF // 2, D), (FF // 2) ** -0.5, 0.15625, ((0, 4),)),
        "mix_level": plant(jax.random.randint(key_of[7], (HEADS,), 1, 8), jax.random.fold_in(key_of[7], 1), 1, 7).astype(jnp.int32),
        "seq_lengths": draw_seq_lengths(jax.random.fold_in(key_of[9], 71), 0),
    }


EPS = 1e-05
NEG = -1e+30
EXACT = lax.Precision.HIGHEST

@jax.custom_vjp
def low(v):
    return lax.optimization_barrier(v.astype(jnp.bfloat16)).astype(jnp.float32)

@jax.custom_vjp
def low_back(v):
    return v

def low_keep(v):
    return (low(v), None)

def low_pass(kept, grad):
    return (grad,)

def back_keep(v):
    return (v, None)

def back_low(kept, grad):
    return (low(grad),)
low.defvjp(low_keep, low_pass)
low_back.defvjp(back_keep, back_low)

def segment_of(lengths_row):
    ends = jnp.cumsum(lengths_row)
    places = jnp.arange(SLOT, dtype=jnp.int32)
    return lax.optimization_barrier(jnp.sum((places[:, None] >= ends[None, :]).astype(jnp.int32), axis=1))

def normalize(stream, norm_gain):
    return stream * lax.rsqrt(lax.optimization_barrier(jnp.mean(stream * stream, axis=-1, keepdims=True)) + EPS) * norm_gain

def attend(query, keys, values, segments):
    shape = (SLOT, HEADS, HEAD_DIM)
    places = jnp.arange(SLOT, dtype=jnp.int32)
    allowed = (places[None, :] <= places[:, None]) & (segments[:, None] == segments[None, :])
    scores = jnp.einsum('qhd,khd->hqk', query.reshape(shape), keys.reshape(shape), precision=EXACT) * HEAD_DIM ** (-0.5)
    scores = low_back(jnp.where(allowed[None], scores, NEG))
    attn_probs = low(jax.nn.softmax(scores, axis=-1))
    result = jnp.einsum('hqk,khd->qhd', attn_probs, values.reshape(shape), precision=EXACT)
    return result.reshape(SLOT, HEADS * HEAD_DIM)

def attention_layer(stream, attn_inward, attn_outward, norm_gain, segments, mix_weight, first_values):
    width = HEADS * HEAD_DIM
    normed_act = low(normalize(stream, norm_gain))
    projected = jnp.dot(normed_act, attn_inward, precision=EXACT)
    query = low_back(low(projected[:, :width]))
    keys = low_back(low(projected[:, width:2 * width]))
    values = low_back(low(projected[:, 2 * width:]))
    if first_values is None:
        mixed = values
    else:
        mixed = low((1.0 - mix_weight) * values + mix_weight * first_values)
    blocks = (-1, SLOT, width)
    step = jax.checkpoint(attend)
    attn = lax.map(lambda part: step(part[0], part[1], part[2], part[3]), (query.reshape(blocks), keys.reshape(blocks), mixed.reshape(blocks), segments))
    attn = low_back(low(attn.reshape(-1, width)))
    return (stream + jnp.dot(attn, attn_outward, precision=EXACT), values, mixed)

def feed_slot(stream, feed_inward, feed_outward, norm_gain):
    normed_act = low(normalize(stream, norm_gain))
    both = jnp.dot(normed_act, feed_inward, precision=EXACT)
    gate_pre = low_back(both[:, :FF])
    up_pre = low_back(both[:, FF:])
    hidden = low(jax.nn.silu(gate_pre) * up_pre)
    return stream + jnp.dot(hidden, feed_outward, precision=EXACT)

def feed_layer(stream, feed_inward, feed_outward, norm_gain):
    step = jax.checkpoint(lambda part: feed_slot(part, feed_inward, feed_outward, norm_gain))
    return lax.map(step, stream.reshape(-1, SLOT, D)).reshape(-1, D)

def attention_weights(attn_in, attn_out, layer):
    half = HEADS * HEAD_DIM // 2
    lower, upper = (attn_in[2 * layer], attn_in[2 * layer + 1])
    attn_inward = jnp.concatenate([lower[:, :half], upper[:, :half], lower[:, half:2 * half], upper[:, half:2 * half], lower[:, 2 * half:], upper[:, 2 * half:]], axis=1)
    attn_outward = jnp.concatenate([attn_out[2 * layer], attn_out[2 * layer + 1]], axis=0)
    return (attn_inward, attn_outward)

def feed_weights(ffn_in, ffn_out, layer):
    half = FF // 2
    lower, upper = (ffn_in[2 * layer], ffn_in[2 * layer + 1])
    feed_inward = jnp.concatenate([lower[:, :half], upper[:, :half], lower[:, half:], upper[:, half:]], axis=1)
    feed_outward = jnp.concatenate([ffn_out[2 * layer], ffn_out[2 * layer + 1]], axis=0)
    return (feed_inward, feed_outward)

def forward(tokens, gains, attn_in, attn_out, ffn_in, ffn_out, mix_weight, segments):
    attn_inward, attn_outward = attention_weights(attn_in, attn_out, 0)
    stream, first_values, unused = attention_layer(tokens, attn_inward, attn_outward, gains[0], segments, mix_weight, None)
    stream = low_back(low(stream))
    feed_inward, feed_outward = feed_weights(ffn_in, ffn_out, 0)
    stream = low_back(low(feed_layer(stream, feed_inward, feed_outward, gains[1])))
    attn_inward, attn_outward = attention_weights(attn_in, attn_out, 1)
    stream, unused, blended = attention_layer(stream, attn_inward, attn_outward, gains[2], segments, mix_weight, low_back(first_values))
    stream = low_back(low(stream))
    feed_inward, feed_outward = feed_weights(ffn_in, ffn_out, 1)
    norms = (jnp.mean(first_values * first_values), jnp.mean(blended * blended))
    return (low(feed_layer(stream, feed_inward, feed_outward, gains[3])), norms)

def reference(tokens, cotangent, gains, attn_in, attn_out, ffn_in, ffn_out, mix_level, seq_lengths):
    segments = jax.vmap(segment_of)(seq_lengths)
    mix_weight = jnp.repeat(mix_level.astype(jnp.float32) / 8.0, HEAD_DIM)

    def whole(x_in, g_in, ai_in, ao_in, fi_in, fo_in):
        return forward(x_in, g_in, ai_in, ao_in, fi_in, fo_in, mix_weight, segments)
    outputs, pull, norms = jax.vjp(whole, tokens.astype(jnp.float32), gains.astype(jnp.float32), attn_in.astype(jnp.float32), attn_out.astype(jnp.float32), ffn_in.astype(jnp.float32), ffn_out.astype(jnp.float32), has_aux=True)
    grads = pull(cotangent.astype(jnp.float32))
    return (outputs.astype(jnp.bfloat16), grads[0], grads[1], grads[2], grads[3], grads[4], grads[5], norms[0], norms[1])
```

```python
import functools

import jax
import jax.numpy as jnp
from jax import lax
from jax.experimental import pallas as pl
from jax.experimental.pallas import tpu as pltpu
from jax.sharding import PartitionSpec as P

HEAD_DIM = 64
EPS = 1e-05
NEG = -1e30
GROUP = 8
BF = jnp.bfloat16
F32 = jnp.float32
MIB = 1024 * 1024


def dot_nn(left, right):
    return lax.dot_general(left, right, (((1,), (0,)), ((), ())), preferred_element_type=F32)


def dot_nt(left, right):
    return lax.dot_general(left, right, (((1,), (1,)), ((), ())), preferred_element_type=F32)


def dot_tn(left, right):
    return lax.dot_general(left, right, (((0,), (0,)), ((), ())), preferred_element_type=F32)


def full(memory=pltpu.VMEM):
    return pl.BlockSpec(memory_space=memory)


def shape_of(shape, dtype):
    return jax.ShapeDtypeStruct(shape, dtype)


def normalize(stream, axis):
    rscale = lax.rsqrt(jnp.mean(stream * stream, axis=axis, keepdims=True) + EPS)
    return stream * rscale, rscale


def norm_back(stream, grad_out, dact, gain):
    normed, rscale = normalize(stream, -1)
    scaled = dact * normed
    dnorm = dact * gain
    mean = jnp.mean(scaled * gain, axis=-1, keepdims=True)
    grad = grad_out + rscale * (dnorm - normed * mean)
    return grad, jnp.sum(scaled, axis=0, keepdims=True)


def allowed_keys(ends, count):
    key = lax.broadcasted_iota(jnp.int32, (count, count), 0)
    query = lax.broadcasted_iota(jnp.int32, (count, count), 1)
    segment_key = sum((key >= end).astype(jnp.int32) for end in ends)
    segment_query = sum((query >= end).astype(jnp.int32) for end in ends)
    return (key <= query) & (segment_key == segment_query)


def head_probs(query, keys, allowed):
    scores = jnp.where(allowed, dot_tn(keys, query) * HEAD_DIM**-0.5, NEG)
    exponent = jnp.exp(scores - jnp.max(scores, axis=0, keepdims=True))
    return exponent / jnp.sum(exponent, axis=0, keepdims=True)


def head_back(query, keys, mixed, dattn, probs):
    low_probs = probs.astype(BF)
    dprobs = dot_tn(mixed, dattn)
    dscores = probs * (dprobs - jnp.sum(dprobs * probs, axis=0, keepdims=True))
    dscores = dscores.astype(BF)
    dquery = dot_nn(keys, dscores) * HEAD_DIM**-0.5
    dkeys = dot_nt(query, dscores) * HEAD_DIM**-0.5
    dmixed = dot_nt(dattn, low_probs)
    return dquery, dkeys, dmixed


def swish(gate, up):
    sigmoid = 1.0 / (1.0 + jnp.exp(-gate))
    return sigmoid, gate * sigmoid


def feed_back(gate, up, dhid):
    sigmoid, silu = swish(gate, up)
    hid = (silu * up).astype(BF)
    dgate = dhid * up * (sigmoid * (1.0 + gate * (1.0 - sigmoid)))
    dup = dhid * silu
    return hid, dgate.astype(BF), dup.astype(BF)


def attn_forward_kernel(mixing, slot, *refs):
    if mixing:
        ends_ref, x_ref, gain_ref, inward_ref, outward_ref, mix_ref, first_ref = refs[:7]
        part_ref, mixed_ref, square_ref = refs[7:]
    else:
        ends_ref, x_ref, gain_ref, inward_ref, outward_ref = refs[:5]
        part_ref, mixed_ref, square_ref = refs[5:]
    count = x_ref.shape[0]
    width = outward_ref.shape[0]
    normed, unused = normalize(x_ref[...].astype(F32), -1)
    act = (normed * gain_ref[...]).astype(BF)
    proj = dot_nn(act, inward_ref[...])
    proj = proj.T.astype(BF)
    values = proj[2 * width :]
    if mixing:
        mix = mix_ref[...]
        mixed = (1.0 - mix) * values.astype(F32) + mix * first_ref[...].astype(F32)
        values = mixed.astype(BF)
    mixed_ref[...] = values
    wide = values.astype(F32)
    square_ref[...] = jnp.sum(wide * wide, axis=0, keepdims=True)
    allowed = allowed_keys([ends_ref[slot, i] for i in range(ends_ref.shape[1])], count)
    heads = []
    for at in range(0, width, HEAD_DIM):
        probs = head_probs(proj[at : at + HEAD_DIM], proj[width + at : width + at + HEAD_DIM], allowed)
        heads.append(dot_nn(values[at : at + HEAD_DIM], probs.astype(BF)))
    attn = jnp.concatenate(heads, axis=0).T.astype(BF)
    part_ref[...] = dot_nn(attn, outward_ref[...]).astype(BF)


def feed_forward_kernel(x_ref, own_ref, got_ref, gain_ref, inward_ref, outward_ref, stream_ref, turned_ref, part_ref):
    stream = x_ref[...].astype(F32) + (own_ref[...].astype(F32) + got_ref[...].astype(F32))
    low = stream.astype(BF)
    stream_ref[...] = low
    stream = low.astype(F32)
    turned_ref[...] = stream.T.astype(BF)
    normed, unused = normalize(stream, -1)
    act = (normed * gain_ref[...]).astype(BF)
    hidden = outward_ref.shape[0]
    gate = dot_nn(act, inward_ref[:, :hidden])
    up = dot_nn(act, inward_ref[:, hidden:])
    unused, silu = swish(gate, up)
    hid = (silu * up).astype(BF)
    part_ref[...] = dot_nn(hid, outward_ref[...]).astype(BF)


def feed_backward_kernel(x_ref, grad_ref, gain_ref, inward_ref, outward_ref, part_ref):
    normed, unused = normalize(x_ref[...].astype(F32), -1)
    act = (normed * gain_ref[...]).astype(BF)
    hidden = outward_ref.shape[0]
    gate = dot_nn(act, inward_ref[:, :hidden])
    up = dot_nn(act, inward_ref[:, hidden:])
    dhid = dot_nt(grad_ref[...], outward_ref[...])
    unused, dgate, dup = feed_back(gate, up, dhid)
    dact = dot_nt(dgate, inward_ref[:, :hidden]) + dot_nt(dup, inward_ref[:, hidden:])
    part_ref[...] = dact.astype(BF)


def attn_backward_kernel(mixing, slot, *refs):
    (
        ends_ref,
        next_ref,
        grad_next_ref,
        own_ref,
        got_ref,
        gain_next_ref,
        x_ref,
        gain_ref,
        inward_ref,
        outward_ref,
        mix_ref,
        first_ref,
    ) = refs[:12]
    grad_ref, turned_ref, dgain_ref, part_ref, dfirst_ref = refs[12:]
    count = x_ref.shape[0]
    width = outward_ref.shape[0]
    dact_next = own_ref[...].astype(F32) + got_ref[...].astype(F32)
    grad, dgain = norm_back(
        next_ref[...].astype(F32), grad_next_ref[...].astype(F32), dact_next, gain_next_ref[...]
    )
    dgain_ref[...] = dgain
    low_grad = grad.astype(BF)
    grad_ref[...] = low_grad
    turned_ref[...] = low_grad.astype(F32).T.astype(BF)
    dattn = dot_nt(low_grad, outward_ref[...]).T.astype(BF)
    normed, unused = normalize(x_ref[...].astype(F32), -1)
    act = (normed * gain_ref[...]).astype(BF)
    proj = dot_nn(act, inward_ref[...]).T.astype(BF)
    values = proj[2 * width :]
    if mixing:
        mix = mix_ref[...]
        values = ((1.0 - mix) * values.astype(F32) + mix * first_ref[...].astype(F32)).astype(BF)
    allowed = allowed_keys([ends_ref[slot, i] for i in range(ends_ref.shape[1])], count)
    dquery, dkeys, dmixed = [], [], []
    for at in range(0, width, HEAD_DIM):
        query, keys = proj[at : at + HEAD_DIM], proj[width + at : width + at + HEAD_DIM]
        probs = head_probs(query, keys, allowed)
        got = head_back(query, keys, values[at : at + HEAD_DIM], dattn[at : at + HEAD_DIM], probs)
        dquery.append(got[0])
        dkeys.append(got[1])
        dmixed.append(got[2])
    dmixed = jnp.concatenate(dmixed, axis=0)
    if mixing:
        dfirst_ref[...] = (mix_ref[...] * dmixed).astype(BF)
        dvalues = (1.0 - mix_ref[...]) * dmixed
    else:
        dfirst_ref[...] = jnp.zeros_like(dfirst_ref)
        dvalues = dmixed + first_ref[...].astype(F32)
    dproj = jnp.concatenate(dquery + dkeys + [dvalues], axis=0).T.astype(BF)
    part_ref[...] = dot_nt(dproj, inward_ref[...]).astype(BF)


def combine_kernel(x_ref, grad_ref, own_ref, got_ref, gain_ref, out_ref, dgain_ref):
    dact = own_ref[...].astype(F32) + got_ref[...].astype(F32)
    grad, dgain = norm_back(x_ref[...].astype(F32), grad_ref[...].astype(F32), dact, gain_ref[...])
    out_ref[...] = grad.astype(out_ref.dtype)
    dgain_ref[...] = dgain


def call(kernel, outs, *args, smem=0, flops=0, name=None):
    moved = sum(a.size * a.dtype.itemsize for a in args) + sum(o.size * o.dtype.itemsize for o in outs)
    return pl.pallas_call(
        kernel,
        out_shape=outs,
        in_specs=[full(pltpu.SMEM)] * smem + [full()] * (len(args) - smem),
        out_specs=[full()] * len(outs),
        compiler_params=pltpu.CompilerParams(vmem_limit_bytes=40 * MIB),
        cost_estimate=pl.CostEstimate(flops=int(flops), bytes_accessed=int(moved), transcendentals=0),
        name=name,
    )(*args)


def fetch(pick, choices, target, sems, first):
    count = choices[0].shape[2]
    for which, source in enumerate(choices):

        @pl.when(pick == which)
        def _():
            for slot in range(source.shape[0]):
                pltpu.make_async_copy(
                    source.at[slot], target.at[:, slot * count : (slot + 1) * count], sems.at[first + slot]
                ).start()


def arrived(choices, target, sems, first, slots):
    count = choices[0].shape[2]
    for slot in slots:
        pltpu.make_async_copy(
            choices[0].at[0], target.at[:, pl.ds(slot * count, count)], sems.at[first + slot]
        ).wait()


def feed_weights_kernel(
    steps,
    slots,
    pick_ref,
    s0_ref,
    s1_ref,
    g0_ref,
    g1_ref,
    gain_ref,
    inward_ref,
    outward_ref,
    dinward_ref,
    doutward_ref,
    stream,
    grad,
    hid_all,
    dboth_all,
    sems,
):
    step = pl.program_id(0)
    count = s0_ref.shape[2]
    hidden = outward_ref.shape[0]
    rows, wide, across = steps

    @pl.when(step == 0)
    def _():
        fetch(pick_ref[0], (s0_ref, s1_ref), stream, sems, 0)
        fetch(pick_ref[0], (g0_ref, g1_ref), grad, sems, slots)

    @pl.when(step < rows)
    def _():
        each = slots // rows
        mine = [step * each + i for i in range(each)]
        arrived((s0_ref,), stream, sems, 0, mine)
        arrived((g0_ref,), grad, sems, slots, mine)
        here = pl.ds(pl.multiple_of(step * (each * count), each * count), each * count)
        normed, unused = normalize(stream[:, here].astype(F32), 0)
        act = (normed * gain_ref[...]).astype(BF)
        stream[:, here] = act
        both = dot_nn(inward_ref[...], act)
        dhid = dot_nn(outward_ref[...], grad[:, here])
        hid, dgate, dup = feed_back(both[:hidden], both[hidden:], dhid)
        hid_all[:, here] = hid
        dboth_all[:hidden, here] = dgate
        dboth_all[hidden:, here] = dup

    @pl.when((step >= rows) & (step < rows + wide))
    def _():
        size = dinward_ref.shape[1]
        at = pl.multiple_of((step - rows) * size, size)
        dinward_ref[...] = dot_nt(stream[...], dboth_all[pl.ds(at, size), :])

    @pl.when(step >= rows + wide)
    def _():
        size = doutward_ref.shape[1]
        at = pl.multiple_of((step - rows - wide) * size, size)
        doutward_ref[...] = dot_nt(hid_all[...], grad[pl.ds(at, size), :])


def attn_weights_kernel(
    steps,
    slots,
    pick_ref,
    ends_ref,
    s0_ref,
    s1_ref,
    g0_ref,
    g1_ref,
    first_ref,
    gain_ref,
    mix_ref,
    add_ref,
    inward_ref,
    outward_ref,
    dinward_ref,
    doutward_ref,
    stream,
    grad,
    attn_all,
    dproj_all,
    sems,
):
    step = pl.program_id(0)
    count = s0_ref.shape[2]
    width = outward_ref.shape[0]
    rows, wide, across = steps

    @pl.when(step == 0)
    def _():
        fetch(pick_ref[0], (s0_ref, s1_ref), stream, sems, 0)
        fetch(pick_ref[0], (g0_ref, g1_ref), grad, sems, slots)

    @pl.when(step < rows)
    def _():
        each = slots // rows
        mine = [step * each + i for i in range(each)]
        arrived((s0_ref,), stream, sems, 0, mine)
        arrived((g0_ref,), grad, sems, slots, mine)
        here = pl.ds(pl.multiple_of(step * (each * count), each * count), each * count)
        normed, unused = normalize(stream[:, here].astype(F32), 0)
        act = (normed * gain_ref[...]).astype(BF)
        stream[:, here] = act
        proj = dot_nn(inward_ref[...], act).astype(BF)
        dattn = dot_nn(outward_ref[...], grad[:, here]).astype(BF)
        mix = mix_ref[...]
        for i in range(each):
            cols = slice(i * count, (i + 1) * count)
            place = pl.ds(pl.multiple_of((step * each + i) * count, count), count)
            first = first_ref[i].astype(F32)
            values = proj[2 * width :, cols].astype(F32)
            values = ((1.0 - mix) * values + mix * first).astype(BF)
            allowed = allowed_keys([ends_ref[step * each + i, j] for j in range(ends_ref.shape[1])], count)
            for at in range(0, width, HEAD_DIM):
                query, keys = proj[at : at + HEAD_DIM, cols], proj[width + at : width + at + HEAD_DIM, cols]
                probs = head_probs(query, keys, allowed)
                head = slice(at, at + HEAD_DIM)
                attn_all[head, place] = dot_nn(values[head], probs.astype(BF)).astype(BF)
                dquery, dkeys, dmixed = head_back(query, keys, values[head], dattn[head, cols], probs)
                dproj_all[at : at + HEAD_DIM, place] = dquery.astype(BF)
                dproj_all[width + at : width + at + HEAD_DIM, place] = dkeys.astype(BF)
                dvalues = (1.0 - mix[head]) * dmixed + add_ref[head, :] * first[head]
                dproj_all[2 * width + at : 2 * width + at + HEAD_DIM, place] = dvalues.astype(BF)

    @pl.when((step >= rows) & (step < rows + wide))
    def _():
        size = dinward_ref.shape[1]
        at = pl.multiple_of((step - rows) * size, size)
        dinward_ref[...] = dot_nt(stream[...], dproj_all[pl.ds(at, size), :])

    @pl.when(step >= rows + wide)
    def _():
        size = doutward_ref.shape[1]
        at = pl.multiple_of((step - rows - wide) * size, size)
        doutward_ref[...] = dot_nt(attn_all[...], grad[pl.ds(at, size), :])


def weight_call(kernel, smem, gathered, extra, small, weights, name):
    slots, model, count = gathered[0].shape
    inward, outward = weights
    total = slots * count
    each = 2
    block = 256
    rows, wide, across = slots // each, inward.shape[0] // block, model // block
    steps = (rows, wide, across)
    once = dict(pipeline_mode=pl.Buffered(1))

    def whole(a):
        return pl.BlockSpec(a.shape, lambda i: (0,) * a.ndim, **once)

    in_specs = (
        [full(pltpu.SMEM)] * len(smem)
        + [full(pl.ANY)] * 4
        + [pl.BlockSpec((each,) + a.shape[1:], lambda i: (jnp.minimum(i, rows - 1), 0, 0)) for a in extra]
        + [whole(a) for a in small]
        + [whole(a) for a in weights]
    )
    out_specs = [
        pl.BlockSpec((model, block), lambda i: (0, jnp.clip(i - rows, 0, wide - 1))),
        pl.BlockSpec((outward.shape[0], block), lambda i: (0, jnp.clip(i - rows - wide, 0, across - 1))),
    ]
    flops = 4 * total * (inward.size + outward.size)
    return pl.pallas_call(
        functools.partial(kernel, steps, slots),
        grid=(rows + wide + across,),
        in_specs=in_specs,
        out_specs=out_specs,
        out_shape=[
            shape_of((model, inward.shape[0]), F32),
            shape_of((outward.shape[0], model), F32),
        ],
        scratch_shapes=[
            pltpu.VMEM((model, total), BF),
            pltpu.VMEM((model, total), BF),
            pltpu.VMEM((outward.shape[0], total), BF),
            pltpu.VMEM((inward.shape[0], total), BF),
            pltpu.SemaphoreType.DMA((2 * slots,)),
        ],
        compiler_params=pltpu.CompilerParams(
            vmem_limit_bytes=60 * MIB, dimension_semantics=("arbitrary",)
        ),
        cost_estimate=pl.CostEstimate(flops=flops, bytes_accessed=16 * MIB, transcendentals=0),
        name=name,
    )(*smem, *gathered, *extra, *small, *weights)


def section_pairs(mask):
    return [(i, i ^ mask) for i in range(lax.axis_size("section"))]


def body(tokens, cotangent, gains, attn_in, attn_out, ffn_in, ffn_out, mix_level, seq_lengths):
    section = lax.axis_index("section")
    lower = section < 2
    even = section % 2 == 0
    dp = lax.axis_size("dp")
    group = min(dp, GROUP)
    groups = [list(range(at, at + group)) for at in range(0, dp, group)]
    micro = seq_lengths.shape[0]
    count = tokens.shape[0] // micro
    piece = tokens.shape[1]
    inward, outward, feed_in, feed_out = attn_in[0], attn_out[0], ffn_in[0], ffn_out[0]
    model = inward.shape[0]
    width = outward.shape[0]
    hidden = feed_out.shape[0]

    def swap(x, mask):
        return lax.ppermute(x, "section", section_pairs(mask))

    def to_upper(x):
        return lax.ppermute(x, "section", [(0, 2), (1, 3)])

    def to_lower(x):
        return lax.ppermute(x, "section", [(2, 0), (3, 1)])

    def gathered(parts):
        return lax.all_gather(jnp.stack(parts), "dp", axis=0, tiled=True, axis_index_groups=groups)

    near = jnp.where(lower, tokens, cotangent)
    far = jnp.where(lower, cotangent, tokens)
    got_near, got_far, got_across = swap(near, 1), swap(far, 2), swap(far, 3)
    ours = [jnp.where(even, near, got_near), jnp.where(even, got_near, near)]
    theirs = [jnp.where(even, got_far, got_across), jnp.where(even, got_across, got_far)]
    given = jnp.concatenate(
        [jnp.where(lower, a, b) for a, b in zip(ours + theirs, theirs + ours)], axis=1
    )
    given = [given[m * count : (m + 1) * count] for m in range(micro)]

    got_gains = swap(gains, 1)
    gain_attn = jnp.where(even, gains, got_gains)
    gain_feed = jnp.where(even, got_gains, gains)
    ends = jnp.cumsum(seq_lengths, axis=1)
    all_ends = lax.all_gather(ends, "dp", axis=0, tiled=True, axis_index_groups=groups)
    mix_all = jnp.repeat(mix_level.astype(F32) / 8.0, HEAD_DIM)
    mix = jnp.where(even, mix_all[:width], mix_all[width:])[:, None]

    inward_turned = inward.T
    feed_in_turned = feed_in.T

    all_given = gathered([x.T for x in given])

    attn_flops = 2 * count * (inward.size + outward.size)
    feed_flops = 2 * count * (feed_in.size + feed_out.size)
    low_stream = shape_of((count, model), BF)
    low_values = shape_of((width, count), BF)
    turned_shape = shape_of((model, count), BF)
    row_sum = shape_of((1, model), F32)

    def attn_forward(slot, x, first):
        args = (ends, x, gain_attn, inward, outward)
        if first is not None:
            args += (mix, first)
        return call(
            functools.partial(attn_forward_kernel, first is not None, slot),
            [low_stream, low_values, shape_of((1, count), F32)],
            *args,
            smem=1,
            flops=attn_flops,
            name="attn_forward",
        )

    def feed_forward(x, own, got):
        return call(
            feed_forward_kernel,
            [low_stream, turned_shape, low_stream],
            x,
            own,
            got,
            gain_feed,
            feed_in,
            feed_out,
            flops=feed_flops,
            name="feed_forward",
        )

    def feed_backward(x, grad):
        return call(
            feed_backward_kernel,
            [low_stream],
            x,
            grad,
            gain_feed,
            feed_in,
            feed_out,
            flops=2 * feed_flops,
            name="feed_backward",
        )[0]

    def attn_backward(mixing, slot, x_next, grad_next, own, got, x, first):
        return call(
            functools.partial(attn_backward_kernel, mixing, slot),
            [low_stream, turned_shape, row_sum, low_stream, low_values],
            ends,
            x_next,
            grad_next,
            own,
            got,
            gain_feed,
            x,
            gain_attn,
            inward,
            outward,
            mix,
            first,
            smem=1,
            flops=2 * attn_flops,
            name="attn_backward",
        )

    def combine(x, grad, own, got, dtype):
        return call(
            combine_kernel,
            [shape_of((count, model), dtype), row_sum],
            x,
            grad,
            own,
            got,
            gain_attn,
            flops=1000,
            name="combine",
        )

    def forward_layer(xs, firsts):
        parts, mixed, squares = zip(*[attn_forward(m, xs[m], firsts[m]) for m in range(micro)])
        streams, turned, fparts = [], [], []
        for m in range(micro):
            a, b, c = feed_forward(xs[m], parts[m], swap(parts[m], 1))
            streams.append(a)
            turned.append(b)
            fparts.append(c)
        outs = []
        for m in range(micro):
            got = swap(fparts[m], 1)
            outs.append(
                (streams[m].astype(F32) + (fparts[m].astype(F32) + got.astype(F32))).astype(BF)
            )
        return streams, turned, outs, mixed, sum(jnp.sum(s) for s in squares)

    def backward_layer(mixing, mids, xs, grads, firsts, dtype):
        own = [feed_backward(mids[m], grads[m]) for m in range(micro)]
        results = [
            attn_backward(mixing, m, mids[m], grads[m], own[m], swap(own[m], 1), xs[m], firsts[m])
            for m in range(micro)
        ]
        outs = [
            combine(xs[m], results[m][0], results[m][3], swap(results[m][3], 1), dtype)
            for m in range(micro)
        ]
        dgain_feed = sum(r[2] for r in results)
        dgain_attn = sum(o[1] for o in outs)
        turned = [r[1] for r in results]
        dfirst = [r[4] for r in results]
        return [o[0] for o in outs], turned, dfirst, dgain_attn, dgain_feed

    mid0, mid0_turned, out0, first0, square0 = forward_layer(given, [None] * micro)
    first1 = [to_upper(v) for v in first0]
    x1 = [to_upper(x) for x in out0]
    all_second = gathered([jnp.where(lower, a, b.T) for a, b in zip(mid0_turned, x1)])
    mid1, mid1_turned, out1, unused, square1 = forward_layer(x1, first1)
    all_third = gathered(mid1_turned)

    grads1, turned1, dfirst1, dgain_attn1, dgain_feed1 = backward_layer(
        True, mid1, x1, given, first1, BF
    )
    dfirst0 = [to_lower(v) for v in dfirst1]
    grads_in = [to_lower(g) for g in grads1]
    all_first = gathered([jnp.where(lower, a, b) for a, b in zip(dfirst0, first1)])
    all_fourth = gathered([jnp.where(lower, a.T, b) for a, b in zip(grads_in, turned1)])
    grads0, turned0, unused, dgain_attn0, dgain_feed0 = backward_layer(
        False, mid0, given, grads_in, dfirst0, F32
    )
    all_fifth = gathered(turned0)

    pick = jnp.where(lower, 0, 1).astype(jnp.int32)[None]
    d_feed_in, d_feed_out = weight_call(
        feed_weights_kernel,
        (pick,),
        (all_second, all_third, all_fourth, all_given),
        (),
        (gain_feed.reshape(model, 1),),
        (feed_in_turned, feed_out),
        "feed_weights",
    )
    d_in, d_out = weight_call(
        attn_weights_kernel,
        (pick, all_ends),
        (all_given, all_second, all_fifth, all_fourth),
        (all_first,),
        (
            gain_attn.reshape(model, 1),
            jnp.where(lower, 0.0, mix),
            jnp.where(lower, jnp.ones_like(mix), 0.0),
        ),
        (inward_turned, outward),
        "attn_weights",
    )

    def over_groups(x):
        if dp == group:
            return x
        across = [list(range(at, dp, group)) for at in range(group)]
        return lax.psum(x.astype(BF), "dp", axis_index_groups=across).astype(F32)

    d_in, d_out, d_feed_in, d_feed_out = [
        over_groups(x)[None] for x in (d_in, d_out, d_feed_in, d_feed_out)
    ]
    dgain_attn = jnp.where(lower, dgain_attn0, dgain_attn1)
    dgain_feed = jnp.where(lower, dgain_feed0, dgain_feed1)
    d_gain = lax.psum(jnp.where(even, dgain_attn, dgain_feed), "dp")

    squares = jnp.stack([jnp.where(lower, square0, 0.0), jnp.where(lower, 0.0, square1)])
    totals = lax.psum(squares, ("section", "dp")) / (micro * count * dp * 2 * width)

    def spread(rows, own_lower):
        mine = lax.dynamic_slice_in_dim(rows, section * piece, piece, 1)
        if own_lower:
            sent = lax.dynamic_slice_in_dim(rows, ((section + 2) % 4) * piece, piece, 1)
            return jnp.where(lower, mine, to_upper(sent.astype(BF)).astype(rows.dtype))
        sent = lax.dynamic_slice_in_dim(rows, ((section + 2) % 4) * piece, piece, 1)
        return jnp.where(lower, to_lower(sent), mine)

    out = spread(jnp.concatenate(out1, axis=0), False)
    dinput = spread(jnp.concatenate(grads0, axis=0), True)
    return (out, dinput, d_gain, d_in, d_out, d_feed_in, d_feed_out, totals[0], totals[1])


def solution(mesh):
    in_specs = (
        P("dp", "section"),
        P("dp", "section"),
        P("section", None),
        P("section", None, None),
        P("section", None, None),
        P("section", None, None),
        P("section", None, None),
        P(),
        P("dp", None),
    )
    out_specs = (
        P("dp", "section"),
        P("dp", "section"),
        P("section", None),
        P("section", None, None),
        P("section", None, None),
        P("section", None, None),
        P("section", None, None),
        P(),
        P(),
    )
    return jax.shard_map(body, mesh=mesh, in_specs=in_specs, out_specs=out_specs, check_vma=False)
```

```python
import functools

import jax
import jax.numpy as jnp
from jax import lax
from jax.experimental import pallas as pl
from jax.experimental.pallas import tpu as pltpu
from jax.sharding import PartitionSpec as P

HEAD_DIM = 64
EPS = 1e-05
NEG = -1e30
GROUP = 8
BF = jnp.bfloat16
F32 = jnp.float32
MIB = 1024 * 1024


def dot_nn(left, right):
    return lax.dot_general(left, right, (((1,), (0,)), ((), ())), preferred_element_type=F32)


def dot_nt(left, right):
    return lax.dot_general(left, right, (((1,), (1,)), ((), ())), preferred_element_type=F32)


def dot_tn(left, right):
    return lax.dot_general(left, right, (((0,), (0,)), ((), ())), preferred_element_type=F32)


def shape_of(shape, dtype):
    return jax.ShapeDtypeStruct(shape, dtype)


def normalize(stream, axis):
    rscale = lax.rsqrt(jnp.mean(stream * stream, axis=axis, keepdims=True) + EPS)
    return stream * rscale, rscale


def norm_back(stream, grad_out, dact, gain):
    normed, rscale = normalize(stream, -1)
    scaled = dact * normed
    dnorm = dact * gain
    mean = jnp.mean(scaled * gain, axis=-1, keepdims=True)
    grad = grad_out + rscale * (dnorm - normed * mean)
    return grad, jnp.sum(scaled, axis=0, keepdims=True)


def turned(rows):
    return rows.astype(F32).T.astype(BF)


def allowed_keys(ends, count):
    key = lax.broadcasted_iota(jnp.int32, (count, count), 0)
    query = lax.broadcasted_iota(jnp.int32, (count, count), 1)
    segment_key = sum((key >= end).astype(jnp.int32) for end in ends)
    segment_query = sum((query >= end).astype(jnp.int32) for end in ends)
    return (key <= query) & (segment_key == segment_query)


def heads_of(array, first=0):
    return [array[at : at + HEAD_DIM] for at in range(first, array.shape[0], HEAD_DIM)]


def softmax_keys(scores, allowed):
    scores = jnp.where(allowed, scores * HEAD_DIM**-0.5, NEG)
    exponent = jnp.exp(scores - jnp.max(scores, axis=0, keepdims=True))
    return exponent * (1.0 / jnp.sum(exponent, axis=0, keepdims=True))


def attend(query, keys, values, allowed):
    query, keys, values = heads_of(query), heads_of(keys), heads_of(values)
    scores = [dot_tn(k, q) for q, k in zip(query, keys)]
    probs = [softmax_keys(s, allowed).astype(BF) for s in scores]
    return jnp.concatenate([dot_nn(v, p) for v, p in zip(values, probs)], axis=0)


def attend_back(query, keys, values, dattn, allowed, forward):
    query, keys, values, dattn = [heads_of(a) for a in (query, keys, values, dattn)]
    scores = [dot_tn(k, q) for q, k in zip(query, keys)]
    dprobs = [dot_tn(v, d) for v, d in zip(values, dattn)]
    low_probs, dscores = [], []
    for score, dprob in zip(scores, dprobs):
        probs = softmax_keys(score, allowed)
        low_probs.append(probs.astype(BF))
        dscores.append((probs * (dprob - jnp.sum(dprob * probs, axis=0, keepdims=True))).astype(BF))
    attn = None
    if forward:
        attn = jnp.concatenate([dot_nn(v, p) for v, p in zip(values, low_probs)], axis=0)
    dquery = jnp.concatenate([dot_nn(k, d) for k, d in zip(keys, dscores)], axis=0) * HEAD_DIM**-0.5
    dkeys = jnp.concatenate([dot_nt(q, d) for q, d in zip(query, dscores)], axis=0) * HEAD_DIM**-0.5
    dmixed = jnp.concatenate([dot_nt(d, p) for d, p in zip(dattn, low_probs)], axis=0)
    return dquery, dkeys, dmixed, attn


def swish(gate, up):
    sigmoid = 1.0 / (1.0 + jnp.exp(-gate))
    return sigmoid, gate * sigmoid


def feed_back(gate, up, dhid):
    sigmoid, silu = swish(gate, up)
    hid = (silu * up).astype(BF)
    dgate = dhid * up * (sigmoid * (1.0 + gate * (1.0 - sigmoid)))
    dup = dhid * silu
    return hid, dgate.astype(BF), dup.astype(BF)


def ends_at(ends_ref, slot):
    return [ends_ref[slot, i] for i in range(ends_ref.shape[1])]


def rounded_sum(left, right):
    return left.astype(F32) + right.astype(F32)


def turn_kernel(a_ref, b_ref, a_out, b_out):
    size = 256
    row = lax.broadcasted_iota(jnp.int32, (size, size), 0)
    col = lax.broadcasted_iota(jnp.int32, (size, size), 1)
    identity = jnp.where(row == col, 1.0, 0.0).astype(BF)
    for source, target in ((a_ref, a_out), (b_ref, b_out)):
        for at in range(0, source.shape[1], size):
            target[at : at + size, :] = dot_nt(identity, source[:, at : at + size]).astype(BF)


def attn_first_kernel(slot, ends_ref, x_ref, gain_ref, inward_ref, outward_ref, part_ref, values_ref, square_ref):
    count = x_ref.shape[0]
    width = outward_ref.shape[0]
    normed, unused = normalize(x_ref[...].astype(F32), -1)
    act = (normed * gain_ref[...]).astype(BF)
    proj = dot_nn(act, inward_ref[...]).T.astype(BF)
    values = proj[2 * width :]
    values_ref[...] = values
    wide = values.astype(F32)
    square_ref[...] = jnp.sum(wide * wide, axis=0, keepdims=True)
    allowed = allowed_keys(ends_at(ends_ref, slot), count)
    attn = attend(proj[:width], proj[width : 2 * width], values, allowed)
    part_ref[...] = dot_nn(attn.T.astype(BF), outward_ref[...]).astype(BF)


def feed_first_kernel(
    own_ref,
    mate_ref,
    part_own_ref,
    part_mate_ref,
    got_own_ref,
    got_mate_ref,
    gain_ref,
    inward_ref,
    outward_ref,
    mid_own_ref,
    mid_mate_ref,
    turned_ref,
    send_own_ref,
    send_mate_ref,
):
    count = own_ref.shape[0]
    own = (own_ref[...].astype(F32) + rounded_sum(part_own_ref[...], got_own_ref[...])).astype(BF)
    mate = (mate_ref[...].astype(F32) + rounded_sum(part_mate_ref[...], got_mate_ref[...])).astype(BF)
    mid_own_ref[...] = own
    mid_mate_ref[...] = mate
    turned_ref[0] = turned(own)
    turned_ref[1] = turned(mate)
    stream = jnp.concatenate([own, mate], axis=0).astype(F32)
    normed, unused = normalize(stream, -1)
    act = (normed * gain_ref[...]).astype(BF)
    hidden = outward_ref.shape[0]
    gate = dot_nn(act, inward_ref[:, :hidden])
    up = dot_nn(act, inward_ref[:, hidden:])
    unused, silu = swish(gate, up)
    part = dot_nn((silu * up).astype(BF), outward_ref[...])
    send_own_ref[...] = (stream[:count] + part[:count]).astype(BF)
    send_mate_ref[...] = part[count:].astype(BF)


def attn_second_kernel(
    ends_ref,
    a_ref,
    b_ref,
    gain_ref,
    inward_ref,
    inward_mate_ref,
    outward_ref,
    outward_mate_ref,
    mix_ref,
    mix_mate_ref,
    first_ref,
    first_mate_ref,
    x_ref,
    turned_ref,
    mid_ref,
    square_ref,
):
    count = a_ref.shape[0]
    width = outward_ref.shape[0]
    x = rounded_sum(a_ref[...], b_ref[...]).astype(BF)
    x_ref[...] = x
    turned_ref[...] = turned(x)
    stream = x.astype(F32)
    normed, unused = normalize(stream, -1)
    act = (normed * gain_ref[...]).astype(BF)
    allowed = allowed_keys(ends_at(ends_ref, 0), count)
    square = 0.0
    for w_in, w_out, m_ref, f_ref in (
        (inward_ref, outward_ref, mix_ref, first_ref),
        (inward_mate_ref, outward_mate_ref, mix_mate_ref, first_mate_ref),
    ):
        proj = dot_nn(act, w_in[...]).T.astype(BF)
        mix = m_ref[...]
        mixed = (1.0 - mix) * proj[2 * width :].astype(F32) + mix * f_ref[...].astype(F32)
        mixed = mixed.astype(BF)
        wide = mixed.astype(F32)
        square = square + jnp.sum(wide * wide, axis=0, keepdims=True)
        attn = attend(proj[:width], proj[width : 2 * width], mixed, allowed)
        stream = stream + dot_nn(attn.T.astype(BF), w_out[...])
    mid_ref[...] = stream.astype(BF)
    square_ref[...] = square


def feed_second_kernel(
    own_ref,
    mate_ref,
    grad_own_ref,
    grad_mate_ref,
    gain_ref,
    inward_ref,
    outward_ref,
    part_own_ref,
    part_mate_ref,
    turned_ref,
    out_own_ref,
    out_mate_ref,
):
    count = own_ref.shape[0]
    turned_ref[0] = turned(own_ref[...])
    turned_ref[1] = turned(mate_ref[...])
    stream = jnp.concatenate([own_ref[...], mate_ref[...]], axis=0).astype(F32)
    grad = jnp.concatenate([grad_own_ref[...], grad_mate_ref[...]], axis=0)
    normed, unused = normalize(stream, -1)
    act = (normed * gain_ref[...]).astype(BF)
    hidden = outward_ref.shape[0]
    gate = dot_nn(act, inward_ref[:, :hidden])
    up = dot_nn(act, inward_ref[:, hidden:])
    dhid = dot_nt(grad, outward_ref[...])
    hid, dgate, dup = feed_back(gate, up, dhid)
    dact = dot_nt(dgate, inward_ref[:, :hidden]) + dot_nt(dup, inward_ref[:, hidden:])
    part_own_ref[...] = dact[:count].astype(BF)
    part_mate_ref[...] = dact[count:].astype(BF)
    part = dot_nn(hid, outward_ref[...])
    out_own_ref[...] = stream[:count] + part[:count]
    out_mate_ref[...] = part[count:].astype(BF)


def feed_first_back_kernel(
    own_ref,
    mate_ref,
    grad_own_ref,
    grad_mate_ref,
    gain_ref,
    inward_ref,
    outward_ref,
    part_own_ref,
    part_mate_ref,
    turned_ref,
):
    count = own_ref.shape[0]
    turned_ref[0] = turned(grad_own_ref[...])
    turned_ref[1] = turned(grad_mate_ref[...])
    stream = jnp.concatenate([own_ref[...], mate_ref[...]], axis=0).astype(F32)
    grad = jnp.concatenate([grad_own_ref[...], grad_mate_ref[...]], axis=0)
    normed, unused = normalize(stream, -1)
    act = (normed * gain_ref[...]).astype(BF)
    hidden = outward_ref.shape[0]
    gate = dot_nn(act, inward_ref[:, :hidden])
    up = dot_nn(act, inward_ref[:, hidden:])
    dhid = dot_nt(grad, outward_ref[...])
    unused, dgate, dup = feed_back(gate, up, dhid)
    dact = dot_nt(dgate, inward_ref[:, :hidden]) + dot_nt(dup, inward_ref[:, hidden:])
    part_own_ref[...] = dact[:count].astype(BF)
    part_mate_ref[...] = dact[count:].astype(BF)


def attn_back_kernel(mixing, *refs):
    (
        ends_ref,
        mid_ref,
        grad_next_ref,
        part_ref,
        got_ref,
        gain_feed_ref,
        x_ref,
        gain_ref,
        inward_ref,
        inward_mate_ref,
        outward_ref,
        outward_mate_ref,
        mix_ref,
        mix_mate_ref,
        first_ref,
        first_mate_ref,
    ) = refs[:16]
    turned_ref, grad_ref, dgain_feed_ref, dgain_ref = refs[16:20]
    dfirst_refs = refs[20:]
    count = x_ref.shape[0]
    width = outward_ref.shape[0]
    dact_next = rounded_sum(part_ref[...], got_ref[...])
    grad, dgain = norm_back(
        mid_ref[...].astype(F32), grad_next_ref[...].astype(F32), dact_next, gain_feed_ref[...]
    )
    dgain_feed_ref[...] = dgain
    low_grad = grad.astype(BF)
    grad = low_grad.astype(F32)
    turned_ref[...] = grad.T.astype(BF)
    stream = x_ref[...].astype(F32)
    normed, unused = normalize(stream, -1)
    act = (normed * gain_ref[...]).astype(BF)
    allowed = allowed_keys(ends_at(ends_ref, 0), count)
    dact = 0.0
    for i, (w_in, w_out, m_ref, f_ref) in enumerate(
        (
            (inward_ref, outward_ref, mix_ref, first_ref),
            (inward_mate_ref, outward_mate_ref, mix_mate_ref, first_mate_ref),
        )
    ):
        dattn = dot_nt(low_grad, w_out[...]).T.astype(BF)
        proj = dot_nn(act, w_in[...]).T.astype(BF)
        values = proj[2 * width :]
        if mixing:
            mix = m_ref[...]
            values = ((1.0 - mix) * values.astype(F32) + mix * f_ref[...].astype(F32)).astype(BF)
        dquery, dkeys, dmixed, unused = attend_back(
            proj[:width], proj[width : 2 * width], values, dattn, allowed, False
        )
        if mixing:
            dfirst_refs[i][...] = (mix * dmixed).astype(BF)
            dvalues = (1.0 - mix) * dmixed
        else:
            dvalues = dmixed + f_ref[...].astype(F32)
        dproj = jnp.concatenate([dquery, dkeys, dvalues], axis=0).T.astype(BF)
        dact = dact + dot_nt(dproj, w_in[...])
    grad, dgain = norm_back(stream, grad, dact, gain_ref[...])
    grad_ref[...] = grad.astype(grad_ref.dtype)
    dgain_ref[...] = dgain


def call(kernel, outs, *args, smem=0, flops=0, name=None):
    moved = sum(a.size * a.dtype.itemsize for a in args) + sum(o.size * o.dtype.itemsize for o in outs)
    return pl.pallas_call(
        kernel,
        out_shape=outs,
        in_specs=[pl.BlockSpec(memory_space=pltpu.SMEM)] * smem
        + [pl.BlockSpec(memory_space=pltpu.VMEM)] * (len(args) - smem),
        out_specs=[pl.BlockSpec(memory_space=pltpu.VMEM)] * len(outs),
        compiler_params=pltpu.CompilerParams(vmem_limit_bytes=40 * MIB),
        cost_estimate=pl.CostEstimate(flops=int(flops), bytes_accessed=int(moved), transcendentals=0),
        name=name,
    )(*args)


def block_ref(refs, block):
    operand, index = block
    return refs[operand] if index is None else refs[operand].at[index]


def fetch(pick, refs, choices, target, sems):
    for which, blocks in enumerate(choices):

        @pl.when(pick == which)
        def _():
            for at, block in enumerate(blocks):
                source = block_ref(refs, block)
                count = source.shape[1]
                pltpu.make_async_copy(source, target.at[:, at * count : (at + 1) * count], sems.at[at]).start()


def arrived(refs, blocks, target, sems, at):
    source = block_ref(refs, blocks[0])
    count = source.shape[1]
    place = pl.ds(pl.multiple_of(at * count, count), count)
    pltpu.make_async_copy(source, target.at[:, place], sems.at[at]).wait()


def write_out(stage, sems, target, step, value):
    size = stage.shape[2]
    slot = lax.rem(step, 2)
    place = pl.ds(pl.multiple_of(step * size, size), size)
    copy = pltpu.make_async_copy(stage.at[slot], target.at[:, place], sems.at[slot])

    @pl.when(step >= 2)
    def _():
        copy.wait()

    stage[slot] = value.astype(stage.dtype)
    copy.start()


def written(stage, sems, target, steps):
    size = stage.shape[2]
    for step in range(max(steps - 2, 0), steps):
        slot = step % 2
        pltpu.make_async_copy(
            stage.at[slot], target.at[:, step * size : (step + 1) * size], sems.at[slot]
        ).wait()


def products(left, right, stage, sems, target):
    size = stage.shape[2]
    steps = right.shape[0] // size

    def one(step, unused):
        rows = pl.ds(pl.multiple_of(step * size, size), size)
        write_out(stage, sems, target, step, dot_nt(left[...], right[rows, :]))
        return 0

    lax.fori_loop(0, steps, one, 0)
    return steps


def feed_weights_kernel(layout, *refs):
    (streams, grads), operands = layout
    pick_ref = refs[0]
    blocks_refs = refs[1 : 1 + operands]
    gain_ref, inward_ref, outward_ref = refs[1 + operands : 4 + operands]
    dinward_ref, doutward_ref = refs[4 + operands : 6 + operands]
    act_all, grad_all, hid_all, dboth_all, stage_in, stage_out, sems, out_sems = refs[6 + operands :]
    hidden = outward_ref.shape[0]
    pick = pick_ref[0]
    fetch(pick, blocks_refs, streams, act_all, sems.at[0])
    fetch(pick, blocks_refs, grads, grad_all, sems.at[1])
    blocks = len(streams[0])
    wider = 2 * (act_all.shape[1] // blocks)

    def rows(step, unused):
        for at in (2 * step, 2 * step + 1):
            arrived(blocks_refs, streams[0], act_all, sems.at[0], at)
            arrived(blocks_refs, grads[0], grad_all, sems.at[1], at)
        here = pl.ds(pl.multiple_of(step * wider, wider), wider)
        normed, unused = normalize(act_all[:, here].astype(F32), 0)
        act = (normed * gain_ref[...]).astype(BF)
        act_all[:, here] = act
        both = dot_nn(inward_ref[...], act)
        dhid = dot_nn(outward_ref[...], grad_all[:, here])
        hid, dgate, dup = feed_back(both[:hidden], both[hidden:], dhid)
        hid_all[:, here] = hid
        dboth_all[:hidden, here] = dgate
        dboth_all[hidden:, here] = dup
        return 0

    lax.fori_loop(0, blocks // 2, rows, 0)
    wide = products(act_all, dboth_all, stage_in, out_sems.at[0], dinward_ref)
    across = products(hid_all, grad_all, stage_out, out_sems.at[1], doutward_ref)
    written(stage_in, out_sems.at[0], dinward_ref, wide)
    written(stage_out, out_sems.at[1], doutward_ref, across)


def attn_weights_kernel(layout, *refs):
    (streams, grads, firsts), operands = layout
    pick_ref, ends_ref = refs[:2]
    blocks_refs = refs[2 : 2 + operands]
    gain_ref, mix_ref, add_ref, inward_ref, outward_ref = refs[2 + operands : 7 + operands]
    dinward_ref, doutward_ref = refs[7 + operands : 9 + operands]
    act_all, grad_all, attn_all, dproj_all, first_all, stage_in, stage_out, sems, out_sems = refs[9 + operands :]
    width = outward_ref.shape[0]
    pick = pick_ref[0]
    fetch(pick, blocks_refs, streams, act_all, sems.at[0])
    fetch(pick, blocks_refs, grads, grad_all, sems.at[1])
    fetch(pick, blocks_refs, firsts, first_all, sems.at[2])
    blocks = len(streams[0])
    count = act_all.shape[1] // blocks
    wider = 2 * count

    def rows(step, unused):
        for at in (2 * step, 2 * step + 1):
            arrived(blocks_refs, streams[0], act_all, sems.at[0], at)
            arrived(blocks_refs, grads[0], grad_all, sems.at[1], at)
            arrived(blocks_refs, firsts[0], first_all, sems.at[2], at)
        here = pl.ds(pl.multiple_of(step * wider, wider), wider)
        normed, unused = normalize(act_all[:, here].astype(F32), 0)
        act = (normed * gain_ref[...]).astype(BF)
        act_all[:, here] = act
        proj = dot_nn(inward_ref[...], act).astype(BF)
        dattn = dot_nn(outward_ref[...], grad_all[:, here]).astype(BF)
        first = first_all[:, here].astype(F32)
        mix = mix_ref[...]
        values = ((1.0 - mix) * proj[2 * width :].astype(F32) + mix * first).astype(BF)
        for i in range(2):
            cols = slice(i * count, (i + 1) * count)
            place = pl.ds(pl.multiple_of(step * wider + i * count, count), count)
            allowed = allowed_keys(ends_at(ends_ref, step * 2 + i), count)
            dquery, dkeys, dmixed, attn = attend_back(
                proj[:width, cols],
                proj[width : 2 * width, cols],
                values[:, cols],
                dattn[:, cols],
                allowed,
                True,
            )
            dvalues = (1.0 - mix) * dmixed + add_ref[...] * first[:, cols]
            attn_all[:, place] = attn.astype(BF)
            dproj_all[:, place] = jnp.concatenate([dquery, dkeys, dvalues], axis=0).astype(BF)
        return 0

    lax.fori_loop(0, blocks // 2, rows, 0)
    wide = products(act_all, dproj_all, stage_in, out_sems.at[0], dinward_ref)
    across = products(attn_all, grad_all, stage_out, out_sems.at[1], doutward_ref)
    written(stage_in, out_sems.at[0], dinward_ref, wide)
    written(stage_out, out_sems.at[1], doutward_ref, across)


def weight_call(kernel, smem, sets, small, weights, name, block=256):
    arrays, layout = [], []
    for choices in sets:
        placed = []
        for blocks in choices:
            row = []
            for array, index in blocks:
                at = next((i for i, a in enumerate(arrays) if a is array), None)
                if at is None:
                    at = len(arrays)
                    arrays.append(array)
                row.append((at, index))
            placed.append(tuple(row))
        layout.append(tuple(placed))
    inward, outward = weights
    model = inward.shape[1]
    blocks = len(layout[0][0])
    total = blocks * arrays[0].shape[-1]
    extra = [pltpu.VMEM((outward.shape[0], total), BF)] if len(sets) == 3 else []
    flops = 4 * total * (inward.size + outward.size)
    any_spec, vmem_spec = pl.BlockSpec(memory_space=pl.ANY), pl.BlockSpec(memory_space=pltpu.VMEM)
    return pl.pallas_call(
        functools.partial(kernel, (tuple(layout), len(arrays))),
        in_specs=[pl.BlockSpec(memory_space=pltpu.SMEM)] * len(smem)
        + [any_spec] * len(arrays)
        + [vmem_spec] * (len(small) + 2),
        out_specs=[any_spec] * 2,
        out_shape=[
            shape_of((model, inward.shape[0]), BF),
            shape_of((outward.shape[0], model), BF),
        ],
        scratch_shapes=[
            pltpu.VMEM((model, total), BF),
            pltpu.VMEM((model, total), BF),
            pltpu.VMEM((outward.shape[0], total), BF),
            pltpu.VMEM((inward.shape[0], total), BF),
        ]
        + extra
        + [
            pltpu.VMEM((2, model, block), BF),
            pltpu.VMEM((2, outward.shape[0], block), BF),
            pltpu.SemaphoreType.DMA((len(sets), blocks)),
            pltpu.SemaphoreType.DMA((2, 2)),
        ],
        compiler_params=pltpu.CompilerParams(vmem_limit_bytes=44 * MIB),
        cost_estimate=pl.CostEstimate(flops=flops, bytes_accessed=16 * MIB, transcendentals=0),
        name=name,
    )(*smem, *arrays, *small, *weights)


def body(tokens, cotangent, gains, attn_in, attn_out, ffn_in, ffn_out, mix_level, seq_lengths):
    section = lax.axis_index("section")
    core = lax.axis_index("dp") % 2
    lower = section < 2
    even = section % 2 == 0
    sections = lax.axis_size("section")
    dp = lax.axis_size("dp")
    group = min(dp, GROUP)
    planes = group // 2
    micro = seq_lengths.shape[0]
    count = tokens.shape[0] // micro
    piece = tokens.shape[1]
    inward, outward, feed_in, feed_out = attn_in[0], attn_out[0], ffn_in[0], ffn_out[0]
    model = inward.shape[0]
    width = outward.shape[0]

    def send(x, mask, sources=(0, 1, 2, 3)):
        return lax.ppermute(x, "section", [(i, i ^ mask) for i in sources])

    def plane(x, by):
        pairs = [
            (i, i // group * group + (i % group // 2 + by) % planes * 2 + i % 2) for i in range(dp)
        ]
        return lax.ppermute(x, "dp", pairs)

    def planes_of(x):
        return [plane(x, by) for by in range(1, planes)]

    def other_core(x):
        return lax.ppermute(x, "dp", [(i, i ^ 1) for i in range(dp)])

    low, high = (0, 1), (2, 3)

    near = jnp.where(lower, tokens, cotangent)
    far = jnp.where(lower, cotangent, tokens)
    got_near, got_far, got_across = send(near, 1), send(far, 2), send(far, 3)
    got_gains = send(gains, 1)
    ends = jnp.cumsum(seq_lengths, axis=1)
    ends = jnp.where(even, ends, ends[::-1])
    all_ends = jnp.concatenate([ends] + planes_of(ends), axis=0)
    feed_in_turned, inward_turned = call(
        turn_kernel,
        [shape_of(feed_in.shape[::-1], BF), shape_of(inward.shape[::-1], BF)],
        feed_in,
        inward,
        flops=2 * 256 * (feed_in.size + inward.size),
        name="turn_weights",
    )

    def by_half(mine, other):
        return [jnp.where(even, mine, other), jnp.where(even, other, mine)]

    ours, theirs = by_half(near, got_near), by_half(got_far, got_across)
    given = jnp.concatenate(
        [jnp.where(lower, a, b) for a, b in zip(ours + theirs, theirs + ours)], axis=1
    )
    top, bottom = given[:count], given[count:]
    given_own, given_mate = jnp.where(even, top, bottom), jnp.where(even, bottom, top)
    given_turned = jnp.stack([given_own.T, given_mate.T])

    gain_attn = jnp.where(even, gains, got_gains)
    gain_feed = jnp.where(even, got_gains, gains)
    mix_all = jnp.repeat(mix_level.astype(F32) / 8.0, HEAD_DIM)
    mix_low, mix_high = mix_all[:width, None], mix_all[width:, None]
    mix, mix_mate = jnp.where(even, mix_low, mix_high), jnp.where(even, mix_high, mix_low)

    def swapped_weights(w_in, w_out, sources):
        def parts(w):
            half = w.shape[0] // 2
            mine = send(lax.dynamic_slice_in_dim(w, core * half, half, 0), 1, sources)
            other = other_core(mine)
            return jnp.where(
                core == 0,
                jnp.concatenate([mine, other], axis=0),
                jnp.concatenate([other, mine], axis=0),
            )

        return parts(w_in), parts(w_out)

    inward_high, outward_high = swapped_weights(inward, outward, high)

    attn_flops = 2 * count * (inward.size + outward.size)
    feed_flops = 4 * count * (feed_in.size + feed_out.size)
    slot = shape_of((count, model), BF)
    slot_wide = shape_of((count, model), F32)
    half_turned = shape_of((width, count), BF)
    slot_turned = shape_of((model, count), BF)
    pair_turned = shape_of((2, model, count), BF)
    row = shape_of((1, model), F32)
    square_row = shape_of((1, count), F32)

    def attn_first(which, x):
        return call(
            functools.partial(attn_first_kernel, which),
            [slot, half_turned, square_row],
            ends,
            x,
            gain_attn,
            inward,
            outward,
            smem=1,
            flops=attn_flops,
            name="attn_first",
        )

    part_mate, first_mate, square_mate = attn_first(1, given_mate)
    got_own = send(part_mate, 1, low)
    part_own, first_own, square_own = attn_first(0, given_own)
    got_mate = send(part_own, 1, low)
    mid0_own, mid0_mate, mid0_turned, send_own, send_mate = call(
        feed_first_kernel,
        [slot, slot, pair_turned, slot, slot],
        given_own,
        given_mate,
        part_own,
        part_mate,
        got_own,
        got_mate,
        gain_feed,
        feed_in,
        feed_out,
        flops=feed_flops,
        name="feed_first",
    )
    x_a, x_b = send(send_own, 2, low), send(send_mate, 3, low)
    first_a, first_b, first_c = (
        send(first_own, 2, low),
        send(first_mate, 3, low),
        send(first_mate, 2, low),
    )

    x1, x1_turned, mid1_own, square1 = call(
        attn_second_kernel,
        [slot, slot_turned, slot, square_row],
        ends,
        x_a,
        x_b,
        gain_attn,
        inward,
        inward_high,
        outward,
        outward_high,
        mix,
        mix_mate,
        first_a,
        first_b,
        smem=1,
        flops=2 * attn_flops,
        name="attn_second",
    )
    mid1_mate = send(mid1_own, 1, high)
    part_own, part_mate, mid1_turned, out_own, out_mate = call(
        feed_second_kernel,
        [slot, slot, pair_turned, slot_wide, slot],
        mid1_own,
        mid1_mate,
        given_own,
        given_mate,
        gain_feed,
        feed_in,
        feed_out,
        flops=3 * feed_flops,
        name="feed_second",
    )
    got_own = send(part_mate, 1, high)
    got_out = send(out_mate, 1, high)

    def attn_back(mixing, mid, grad_next, part, got, x, w_in_mate, w_out_mate, first, mate, dtype):
        return call(
            functools.partial(attn_back_kernel, mixing),
            [slot_turned, shape_of((count, model), dtype), row, row] + [half_turned] * (2 * mixing),
            ends,
            mid,
            grad_next,
            part,
            got,
            gain_feed,
            x,
            gain_attn,
            inward,
            w_in_mate,
            outward,
            w_out_mate,
            mix,
            mix_mate,
            first,
            mate,
            smem=1,
            flops=5 * attn_flops,
            name="attn_back",
        )

    grad1_turned, grad_x1, dgain_feed1, dgain_attn1, dfirst, dfirst_mate = attn_back(
        True,
        mid1_own,
        given_own,
        part_own,
        got_own,
        x1,
        inward_high,
        outward_high,
        first_a,
        first_b,
        BF,
    )
    grad_own, grad_mate = send(grad_x1, 2, high), send(grad_x1, 3, high)
    dfirst_a, dfirst_b, dfirst_c = (
        send(dfirst, 2, high),
        send(dfirst_mate, 2, high),
        send(dfirst_mate, 3, high),
    )

    late_in, late_out, unused = lax.optimization_barrier((inward, outward, send_own))
    inward_low, outward_low = swapped_weights(late_in, late_out, low)
    part_own, part_mate, grad0_turned = call(
        feed_first_back_kernel,
        [slot, slot, pair_turned],
        mid0_own,
        mid0_mate,
        grad_own,
        grad_mate,
        gain_feed,
        feed_in,
        feed_out,
        flops=2 * feed_flops,
        name="feed_first_back",
    )
    got_own = send(part_mate, 1, low)
    grad_mid0_turned, dinput, dgain_feed0, dgain_attn0 = attn_back(
        False,
        mid0_own,
        grad_own,
        part_own,
        got_own,
        given_own,
        inward_low,
        outward_low,
        dfirst_a,
        dfirst_b,
        F32,
    )

    def pairs_known(stacked):
        return [(a, i) for a in [stacked] + planes_of(stacked) for i in range(2)]

    def pairs_swapped(own, mate):
        got = planes_of(own)
        blocks = [(own, None), (mate, None)]
        for x in got:
            blocks += [(x, None), (send(x, 1), None)]
        return blocks

    set_given = pairs_known(given_turned)
    set_second = pairs_swapped(
        jnp.where(lower, mid0_turned[0], x1_turned),
        jnp.where(lower, mid0_turned[1], send(x1_turned, 1, high)),
    )
    set_first = pairs_known(
        jnp.stack([jnp.where(lower, dfirst_a, first_a), jnp.where(lower, dfirst_c, first_c)])
    )
    set_third = pairs_swapped(mid1_turned[0], mid1_turned[1])
    set_fourth = pairs_swapped(
        jnp.where(lower, grad0_turned[0], grad1_turned),
        jnp.where(lower, grad0_turned[1], send(grad1_turned, 1, high)),
    )
    set_fifth = pairs_swapped(grad_mid0_turned, send(grad_mid0_turned, 1, low))

    pick = jnp.where(lower, 0, 1).astype(jnp.int32)[None]
    d_feed_in, d_feed_out = weight_call(
        feed_weights_kernel,
        (pick,),
        ((set_second, set_third), (set_fourth, set_given)),
        (gain_feed.reshape(model, 1),),
        (feed_in_turned, feed_out),
        "feed_weights",
    )
    got_feed_in, got_feed_out = other_core(d_feed_in), other_core(d_feed_out)
    d_in, d_out = weight_call(
        attn_weights_kernel,
        (pick, all_ends),
        ((set_given, set_second), (set_fifth, set_fourth), (set_first, set_first)),
        (
            gain_attn.reshape(model, 1),
            jnp.where(lower, 0.0, mix),
            jnp.where(lower, jnp.ones_like(mix), 0.0),
        ),
        (inward_turned, outward),
        "attn_weights",
    )
    got_in, got_out_weights = other_core(d_in), other_core(d_out)

    def over_groups(x):
        if dp == group:
            return x
        across = [list(range(at, dp, group)) for at in range(group)]
        return lax.psum(x.astype(BF), "dp", axis_index_groups=across).astype(F32)

    d_in, d_out, d_feed_in, d_feed_out = [
        over_groups(rounded_sum(a, b))[None]
        for a, b in (
            (d_in, got_in),
            (d_out, got_out_weights),
            (d_feed_in, got_feed_in),
            (d_feed_out, got_feed_out),
        )
    ]

    dgain_attn = jnp.where(lower, dgain_attn0, dgain_attn1)
    dgain_feed = jnp.where(lower, dgain_feed0, dgain_feed1)
    dgain = jnp.where(even, dgain_attn, dgain_feed) + send(jnp.where(even, dgain_feed, dgain_attn), 1)
    square0 = square_own + square_mate
    squares = jnp.concatenate(
        [
            jnp.where(lower, jnp.sum(square0), 0.0)[None],
            jnp.where(lower, 0.0, jnp.sum(square1))[None],
            jnp.zeros((126,), F32),
        ]
    )[None]
    sums = jnp.concatenate([dgain, squares], axis=1)
    sums = sum(planes_of(sums), sums)
    sums = sums + other_core(sums)
    if dp > group:
        sums = lax.psum(sums, "dp") / group
    d_gain, squares = sums[:, :model], sums[0, model:]
    squares = squares + send(squares, 1) + send(squares, 2) + send(squares, 3)
    norms = squares[:2] / (micro * count * dp * 2 * width)

    def owners(rows, holders):
        def part(mask):
            return lax.dynamic_slice_in_dim(rows, (section ^ mask) * piece, piece, 1)

        held = lower if holders == low else ~lower
        beside, over, across = [send(part(mask), mask, holders) for mask in (1, 2, 3)]
        own, mate = jnp.where(held, part(0), over), jnp.where(held, beside, across)
        return jnp.where(
            even, jnp.concatenate([own, mate], axis=0), jnp.concatenate([mate, own], axis=0)
        )

    out = owners((out_own + got_out.astype(F32)).astype(BF), high)
    dinput = owners(dinput.astype(BF), low).astype(F32)
    return (out, dinput, d_gain, d_in, d_out, d_feed_in, d_feed_out, norms[0], norms[1])


def solution(mesh):
    in_specs = (
        P("dp", "section"),
        P("dp", "section"),
        P("section", None),
        P("section", None, None),
        P("section", None, None),
        P("section", None, None),
        P("section", None, None),
        P(),
        P("dp", None),
    )
    out_specs = (
        P("dp", "section"),
        P("dp", "section"),
        P("section", None),
        P("section", None, None),
        P("section", None, None),
        P("section", None, None),
        P("section", None, None),
        P(),
        P(),
    )
    return jax.shard_map(body, mesh=mesh, in_specs=in_specs, out_specs=out_specs, check_vma=False)
```

```python
import functools

import jax
import jax.numpy as jnp
from jax import lax
from jax.experimental import pallas as pl
from jax.experimental.pallas import tpu as pltpu
from jax.sharding import PartitionSpec as P

HEAD_DIM = 64
EPS = 1e-05
NEG = -1e30
GROUP = 8
BF = jnp.bfloat16
F32 = jnp.float32
MIB = 1024 * 1024
WEIGHTS_FROM = 500_000


TIMES = {
    "turn_weights": 5.9,
    "attn_mate": 3.1,
    "attn_own": 3.5,
    "feed_first": 5.3,
    "sum": 1.8,
    "attn_mixed": 3.3,
    "feed_second": 8.5,
    "middle_second_back": 3.1,
    "attn_back": 4.7,
    "input_back": 2.3,
    "late": 2.2,
    "feed_first_back": 6.8,
    "middle_first_back": 3.3,
    "split": 1.9,
    "join": 1.9,
    "add": 1.2,
}


def time_of(microseconds):
    return pl.CostEstimate(flops=int(microseconds * 1.15e9), bytes_accessed=1, transcendentals=0)


def dot_nn(left, right):
    return lax.dot_general(left, right, (((1,), (0,)), ((), ())), preferred_element_type=F32)


def dot_nt(left, right):
    return lax.dot_general(left, right, (((1,), (1,)), ((), ())), preferred_element_type=F32)


def dot_tn(left, right):
    return lax.dot_general(left, right, (((0,), (0,)), ((), ())), preferred_element_type=F32)


def shape_of(shape, dtype):
    return jax.ShapeDtypeStruct(shape, dtype)


def in_hbm(a):
    return pltpu.with_memory_space_constraint(a, pltpu.HBM)


def made_in_hbm(outs):
    return [pltpu.HBM(o.shape, o.dtype) for o in outs]


def normalize(stream, axis):
    rscale = lax.rsqrt(jnp.mean(stream * stream, axis=axis, keepdims=True) + EPS)
    return stream * rscale, rscale


def norm_back(stream, grad_out, dact, gain):
    normed, rscale = normalize(stream, -1)
    dnorm = dact * gain
    mean = jnp.mean(dnorm * normed, axis=-1, keepdims=True)
    return grad_out + rscale * (dnorm - normed * mean)


def turned(rows):
    return rows.astype(F32).T.astype(BF)


def allowed_keys(ends, count):
    key = lax.broadcasted_iota(jnp.int32, (count, count), 0)
    query = lax.broadcasted_iota(jnp.int32, (count, count), 1)
    segment_key = sum((key >= end).astype(jnp.int32) for end in ends)
    segment_query = sum((query >= end).astype(jnp.int32) for end in ends)
    return (key <= query) & (segment_key == segment_query)


def heads_of(array, first=0):
    return [array[at : at + HEAD_DIM] for at in range(first, array.shape[0], HEAD_DIM)]


def softmax_keys(scores, allowed):
    scores = jnp.where(allowed, scores * HEAD_DIM**-0.5, NEG)
    exponent = jnp.exp(scores - jnp.max(scores, axis=0, keepdims=True))
    return exponent * (1.0 / jnp.sum(exponent, axis=0, keepdims=True))


def attend(query, keys, values, allowed):
    query, keys, values = heads_of(query), heads_of(keys), heads_of(values)
    scores = [dot_tn(k, q) for q, k in zip(query, keys)]
    probs = [softmax_keys(s, allowed).astype(BF) for s in scores]
    return jnp.concatenate([dot_nn(v, p) for v, p in zip(values, probs)], axis=0)


def attend_back(query, keys, values, dattn, allowed, forward):
    query, keys, values, dattn = [heads_of(a) for a in (query, keys, values, dattn)]
    scores = [dot_tn(k, q) for q, k in zip(query, keys)]
    dprobs = [dot_tn(v, d) for v, d in zip(values, dattn)]
    low_probs, dscores = [], []
    for score, dprob in zip(scores, dprobs):
        probs = softmax_keys(score, allowed)
        low_probs.append(probs.astype(BF))
        dscores.append((probs * (dprob - jnp.sum(dprob * probs, axis=0, keepdims=True))).astype(BF))
    attn = None
    if forward:
        attn = jnp.concatenate([dot_nn(v, p) for v, p in zip(values, low_probs)], axis=0)
    dquery = jnp.concatenate([dot_nn(k, d) for k, d in zip(keys, dscores)], axis=0) * HEAD_DIM**-0.5
    dkeys = jnp.concatenate([dot_nt(q, d) for q, d in zip(query, dscores)], axis=0) * HEAD_DIM**-0.5
    dmixed = jnp.concatenate([dot_nt(d, p) for d, p in zip(dattn, low_probs)], axis=0)
    return dquery, dkeys, dmixed, attn


def swish(gate, up):
    sigmoid = 1.0 / (1.0 + jnp.exp(-gate))
    return sigmoid, gate * sigmoid


def feed_back(gate, up, dhid):
    sigmoid, silu = swish(gate, up)
    hid = (silu * up).astype(BF)
    dgate = dhid * up * (sigmoid * (1.0 + gate * (1.0 - sigmoid)))
    dup = dhid * silu
    return hid, dgate.astype(BF), dup.astype(BF)


def ends_at(ends_ref, slot):
    return [ends_ref[slot, i] for i in range(ends_ref.shape[1])]


def rounded_sum(left, right):
    return left.astype(F32) + right.astype(F32)


def turn_kernel(a_ref, b_ref, a_out, b_out):
    size = 256
    row = lax.broadcasted_iota(jnp.int32, (size, size), 0)
    col = lax.broadcasted_iota(jnp.int32, (size, size), 1)
    identity = jnp.where(row == col, 1.0, 0.0).astype(BF)
    for source, target in ((a_ref, a_out), (b_ref, b_out)):
        for at in range(0, source.shape[1], size):
            target[at : at + size, :] = dot_nt(identity, source[:, at : at + size]).astype(BF)


def attend_forward(slot, ends_ref, x, gain_ref, inward_ref, mix, first):
    width = inward_ref.shape[1] // 3
    normed, unused = normalize(x.astype(F32), -1)
    act = (normed * gain_ref[...]).astype(BF)
    proj = dot_nn(act, inward_ref[...]).T.astype(BF)
    values = proj[2 * width :]
    if mix is not None:
        values = ((1.0 - mix) * values.astype(F32) + mix * first.astype(F32)).astype(BF)
    wide = values.astype(F32)
    square = jnp.sum(wide * wide, axis=0, keepdims=True)
    allowed = allowed_keys(ends_at(ends_ref, slot), x.shape[0])
    attn = attend(proj[:width], proj[width : 2 * width], values, allowed)
    return attn.T.astype(BF), values, square


def ends_rows(ends_ref, slot, shape):
    lane = lax.broadcasted_iota(jnp.int32, shape, 1)
    ends = ends_at(ends_ref, slot)
    return sum(jnp.where(lane == i, end, 0) for i, end in enumerate(ends)).astype(F32).astype(BF)


def square_rows(square, rows):
    parts = []
    for unused in range(3):
        parts.append(square.astype(BF).astype(F32))
        square = square - parts[-1]
    return jnp.concatenate(parts + [jnp.zeros((rows - 3, square.shape[1]), F32)], axis=0).astype(BF)


def attn_mate_kernel(ends_ref, x_ref, gain_ref, inward_ref, outward_ref, part_ref, values_ref, square_ref):
    attn, values, square = attend_forward(1, ends_ref, x_ref[...], gain_ref, inward_ref, None, None)
    values_ref[...] = values
    square_ref[...] = square
    part_ref[...] = dot_nn(attn, outward_ref[...]).astype(BF)


def attn_own_kernel(
    ends_ref,
    x_ref,
    gain_ref,
    inward_ref,
    outward_ref,
    mate_ref,
    values_mate_ref,
    part_ref,
    values_ref,
    square_ref,
    turned_ref,
):
    model = x_ref.shape[1]
    width = outward_ref.shape[0]
    attn, values, square = attend_forward(0, ends_ref, x_ref[...], gain_ref, inward_ref, None, None)
    part_ref[...] = dot_nn(attn, outward_ref[...]).astype(BF)
    values_ref[:width] = values
    values_ref[width:] = values_mate_ref[...]
    square_ref[...] = square
    for slot, ref in enumerate((x_ref, mate_ref)):
        turned_ref[slot, :model] = turned(ref[...])
        turned_ref[slot, model:] = ends_rows(ends_ref, slot, (turned_ref.shape[1] - model, turned_ref.shape[2]))


def attn_mixed_kernel(
    slot, ends_ref, x_ref, gain_ref, inward_ref, outward_ref, mix_ref, first_ref, part_ref, square_ref
):
    width = outward_ref.shape[0]
    attn, unused, square = attend_forward(
        slot,
        ends_ref,
        x_ref[...],
        gain_ref,
        inward_ref,
        mix_ref[...],
        first_ref[slot * width : (slot + 1) * width],
    )
    square_ref[...] = square
    part_ref[...] = dot_nn(attn, outward_ref[...]).astype(BF)


def sum_kernel(a_ref, b_ref, out_ref):
    out_ref[...] = rounded_sum(a_ref[...], b_ref[...]).astype(BF)


def attn_sums(refs):
    own_ref, mate_ref, part_own_ref, part_mate_ref, got_own_ref, got_mate_ref = refs
    own = (own_ref[...].astype(F32) + rounded_sum(part_own_ref[...], got_own_ref[...])).astype(BF)
    mate = (mate_ref[...].astype(F32) + rounded_sum(part_mate_ref[...], got_mate_ref[...])).astype(BF)
    return own, mate


def stacked(stack_ref, own, mate, square):
    model = own.shape[1]
    stack_ref[0, :model] = turned(own)
    stack_ref[1, :model] = turned(mate)
    rows = square_rows(square, stack_ref.shape[1] - model)
    stack_ref[0, model:] = rows
    stack_ref[1, model:] = jnp.zeros_like(rows)


def feed_loads(inward_ref, outward_ref, inward, outward, sems):
    hidden = outward.shape[0]
    copies = [
        pltpu.make_async_copy(inward_ref.at[:, 0:hidden], inward.at[:, 0:hidden], sems.at[0]),
        pltpu.make_async_copy(inward_ref.at[:, hidden : 2 * hidden], inward.at[:, hidden : 2 * hidden], sems.at[1]),
        pltpu.make_async_copy(outward_ref, outward, sems.at[2]),
    ]
    for copy in copies:
        copy.start()
    return copies


def feed_first_kernel(*refs):
    gain_ref, inward_hbm, outward_hbm, square_own_ref, square_mate_ref = refs[6:11]
    mid_own_ref, mid_mate_ref, stack_ref, send_own_ref, send_mate_ref = refs[11:16]
    inward_ref, outward_ref, sems = refs[16:]
    loads = feed_loads(inward_hbm, outward_hbm, inward_ref, outward_ref, sems)
    own, mate = attn_sums(refs[:6])
    count = own.shape[0]
    mid_own_ref[...] = own
    mid_mate_ref[...] = mate
    stacked(stack_ref, own, mate, square_own_ref[...] + square_mate_ref[...])
    stream = jnp.concatenate([own, mate], axis=0).astype(F32)
    normed, unused = normalize(stream, -1)
    act = (normed * gain_ref[...]).astype(BF)
    hidden = outward_ref.shape[0]
    loads[0].wait()
    gate = dot_nn(act, inward_ref[:, :hidden])
    loads[1].wait()
    up = dot_nn(act, inward_ref[:, hidden:])
    unused, silu = swish(gate, up)
    loads[2].wait()
    part = dot_nn((silu * up).astype(BF), outward_ref[...])
    send_own_ref[...] = (stream[:count] + part[:count]).astype(BF)
    send_mate_ref[...] = part[count:].astype(BF)


def feed_second_kernel(lower_ref, *refs):
    grad_own_ref, grad_mate_ref, gain_ref, inward_hbm, outward_hbm = refs[6:11]
    square_own_ref, square_mate_ref, stack_low_ref = refs[11:14]
    part_own_ref, part_mate_ref, mid_own_ref, mid_mate_ref, stack_ref, out_own_ref, out_mate_ref = refs[14:21]
    inward_ref, outward_ref, sems = refs[21:]
    loads = feed_loads(inward_hbm, outward_hbm, inward_ref, outward_ref, sems)
    own, mate = attn_sums(refs[:6])
    count = own.shape[0]
    mid_own_ref[...] = own
    mid_mate_ref[...] = mate

    @pl.when(lower_ref[0] == 1)
    def _():
        stack_ref[...] = stack_low_ref[...]

    @pl.when(lower_ref[0] == 0)
    def _():
        stacked(stack_ref, own, mate, square_own_ref[...] + square_mate_ref[...])

    stream = jnp.concatenate([own, mate], axis=0).astype(F32)
    grad = jnp.concatenate([grad_own_ref[...], grad_mate_ref[...]], axis=0)
    normed, unused = normalize(stream, -1)
    act = (normed * gain_ref[...]).astype(BF)
    hidden = outward_ref.shape[0]
    loads[0].wait()
    gate = dot_nn(act, inward_ref[:, :hidden])
    loads[1].wait()
    up = dot_nn(act, inward_ref[:, hidden:])
    loads[2].wait()
    dhid = dot_nt(grad, outward_ref[...])
    hid, dgate, dup = feed_back(gate, up, dhid)
    dact = dot_nt(dgate, inward_ref[:, :hidden]) + dot_nt(dup, inward_ref[:, hidden:])
    part_own_ref[...] = dact[:count].astype(BF)
    part_mate_ref[...] = dact[count:].astype(BF)
    part = dot_nn(hid, outward_ref[...])
    out_own_ref[...] = (stream[:count] + part[:count]).astype(BF)
    out_mate_ref[...] = part[count:].astype(BF)


def feed_first_back_kernel(
    own_ref,
    mate_ref,
    grad_own_ref,
    grad_mate_ref,
    gain_ref,
    inward_hbm,
    outward_hbm,
    part_own_ref,
    part_mate_ref,
    inward_ref,
    outward_ref,
    sems,
):
    loads = feed_loads(inward_hbm, outward_hbm, inward_ref, outward_ref, sems)
    count = own_ref.shape[0]
    stream = jnp.concatenate([own_ref[...], mate_ref[...]], axis=0).astype(F32)
    grad = jnp.concatenate([turned(grad_own_ref[...]), turned(grad_mate_ref[...])], axis=0)
    normed, unused = normalize(stream, -1)
    act = (normed * gain_ref[...]).astype(BF)
    hidden = outward_ref.shape[0]
    loads[0].wait()
    gate = dot_nn(act, inward_ref[:, :hidden])
    loads[1].wait()
    up = dot_nn(act, inward_ref[:, hidden:])
    loads[2].wait()
    dhid = dot_nt(grad, outward_ref[...])
    unused, dgate, dup = feed_back(gate, up, dhid)
    dact = dot_nt(dgate, inward_ref[:, :hidden]) + dot_nt(dup, inward_ref[:, hidden:])
    part_own_ref[...] = dact[:count].astype(BF)
    part_mate_ref[...] = dact[count:].astype(BF)


def middle_grads(refs, gain_ref, turned_grads):
    for s_ref, g_ref, p_ref, r_ref in zip(*refs):
        grad = g_ref[...].astype(F32)
        grad = norm_back(
            s_ref[...].astype(F32),
            grad.T if turned_grads else grad,
            rounded_sum(p_ref[...], r_ref[...]),
            gain_ref[...],
        )
        yield grad.astype(BF)


def middle_first_back_kernel(lower_ref, *refs):
    gain_ref, x_own_ref, x_mate_ref, out_own_ref, out_mate_ref, turned_ref = refs[8:]
    pairs = refs[0:2], refs[2:4], refs[4:6], refs[6:8]
    grads = middle_grads(pairs, gain_ref, True)
    for i, (grad, x_ref, o_ref) in enumerate(zip(grads, (x_own_ref, x_mate_ref), (out_own_ref, out_mate_ref))):
        o_ref[...] = grad
        turned_ref[i] = turned(jnp.where(lower_ref[0] == 1, grad, x_ref[...]))


def middle_second_back_kernel(*refs):
    gain_ref, out_own_ref, out_mate_ref, turned_ref = refs[8:]
    pairs = refs[0:2], refs[2:4], refs[4:6], refs[6:8]
    for i, (grad, o_ref) in enumerate(zip(middle_grads(pairs, gain_ref, False), (out_own_ref, out_mate_ref))):
        o_ref[...] = grad
        turned_ref[i] = turned(grad)


def attn_back_kernel(mixing, slot, *refs):
    ends_ref, grad_ref, x_ref, gain_ref, inward_ref, outward_ref, first_ref = refs[:7]
    count = x_ref.shape[0]
    width = outward_ref.shape[0]
    first = first_ref[slot * width : (slot + 1) * width].astype(F32)
    normed, unused = normalize(x_ref[...].astype(F32), -1)
    act = (normed * gain_ref[...]).astype(BF)
    allowed = allowed_keys(ends_at(ends_ref, slot), count)
    dattn = dot_nt(grad_ref[...], outward_ref[...]).T.astype(BF)
    proj = dot_nn(act, inward_ref[...]).T.astype(BF)
    values = proj[2 * width :]
    if mixing:
        mix = refs[7][...]
        values = ((1.0 - mix) * values.astype(F32) + mix * first).astype(BF)
    dquery, dkeys, dmixed, unused = attend_back(
        proj[:width], proj[width : 2 * width], values, dattn, allowed, False
    )
    if mixing:
        dfirst = (mix * dmixed).astype(BF)
        dvalues = (1.0 - mix) * dmixed
        if slot == 1:
            refs[-1][...] = dfirst
        else:
            refs[-1][:width] = dfirst
            refs[-1][width:] = refs[8][...]
    else:
        dvalues = dmixed + first
    dproj = jnp.concatenate([dquery, dkeys, dvalues], axis=0).T.astype(BF)
    dact = dot_nt(dproj, inward_ref[...])
    if mixing:
        refs[-2][...] = dact.astype(BF)
    else:
        grad = 0.0 if slot else grad_ref[...].astype(F32)
        refs[-1][...] = norm_back(x_ref[...].astype(F32), grad, dact, gain_ref[...]).astype(BF)


def input_back_kernel(x_ref, grad_ref, part_ref, got_ref, gain_ref, out_ref):
    grad = norm_back(
        x_ref[...].astype(F32),
        grad_ref[...].astype(F32),
        rounded_sum(part_ref[...], got_ref[...]),
        gain_ref[...],
    )
    out_ref[...] = grad.T.astype(BF)


def split_kernel(place_ref, own_ref, mate_ref, row_ref, *refs):
    count, piece = own_ref.shape[0], refs[0].shape[1]
    for mask, ref in enumerate(refs):
        columns = pl.ds(pl.multiple_of(place_ref[mask] * piece, piece), piece)
        ref[:count] = own_ref[:, columns].astype(BF)
        ref[count : 2 * count] = mate_ref[:, columns].astype(BF)
        row = jnp.concatenate([row_ref[...], jnp.zeros((1, piece - row_ref.shape[1]), F32)], axis=1)
        ref[2 * count :] = square_rows(row, ref.shape[0] - 2 * count)


def join_kernel(flags_ref, own_ref, beside_ref, over_ref, across_ref, out_ref, row_ref):
    count = out_ref.shape[0] // 2
    holds, even = flags_ref[0] == 1, flags_ref[1] == 1
    same = jnp.where(holds, own_ref[: 2 * count], over_ref[: 2 * count]).astype(F32)
    other = jnp.where(holds, beside_ref[: 2 * count], across_ref[: 2 * count]).astype(F32)
    own, mate = same[:count] + other[count:], same[count:] + other[:count]
    out_ref[:count] = jnp.where(even, own, mate).astype(out_ref.dtype)
    out_ref[count:] = jnp.where(even, mate, own).astype(out_ref.dtype)
    lanes = row_ref.shape[1]
    rows = [r[2 * count :, :lanes].astype(F32) for r in (own_ref, beside_ref, over_ref, across_ref)]
    row_ref[...] = jnp.sum(sum(rows), axis=0, keepdims=True)


def late_kernel(lower_ref, own_ref, mate_ref, grad_high_ref, dfirst_ref, first_ref, out_ref):
    model = own_ref.shape[0]
    is_lower = lower_ref[0] == 1
    out_ref[:model] = jnp.where(is_lower, own_ref[...], grad_high_ref[0])
    out_ref[model : 2 * model] = jnp.where(is_lower, mate_ref[...], grad_high_ref[1])
    out_ref[2 * model :] = jnp.where(is_lower, dfirst_ref[...], first_ref[...])


def square_sum_kernel(lower_ref, rows_ref, out_ref):
    total = jnp.sum(rows_ref[...].astype(F32))
    lane = lax.broadcasted_iota(jnp.int32, out_ref.shape, 1)
    out_ref[...] = jnp.where(lane == 1 - lower_ref[0], total, 0.0)


def add_kernel(a_ref, b_ref, out_ref):
    out_ref[...] = a_ref[...] + b_ref[...]


def call(kernel, outs, *args, smem=0, name=None, after=(), vmem=16, loads=()):
    whole = len(args)
    held = {id(w) for w in loads}

    def run(*refs):
        kernel(*refs[:whole], *refs[whole + len(after) :])

    def whole_block(a):
        return pl.BlockSpec(a.shape, lambda i: (0,) * len(a.shape))

    def given_spec(a):
        if id(a) in held:
            return pl.BlockSpec(memory_space=pl.ANY)
        return pl.BlockSpec(memory_space=pltpu.VMEM) if a.size >= WEIGHTS_FROM else whole_block(a)

    return pl.pallas_call(
        run,
        grid=(1,),
        out_shape=made_in_hbm(outs),
        in_specs=[pl.BlockSpec(memory_space=pltpu.SMEM)] * smem
        + [given_spec(a) for a in args[smem:]]
        + [pl.BlockSpec(memory_space=pl.ANY)] * len(after),
        out_specs=[whole_block(o) for o in outs],
        scratch_shapes=[pltpu.VMEM(w.shape, w.dtype) for w in loads]
        + [pltpu.SemaphoreType.DMA((1 + len(loads),))] * bool(loads),
        compiler_params=pltpu.CompilerParams(vmem_limit_bytes=vmem * MIB),
        cost_estimate=time_of(TIMES.get(name, 1.0)),
        name=name,
    )(*args[:smem], *[a if a.size >= WEIGHTS_FROM and id(a) not in held else in_hbm(a) for a in args[smem:]], *map(in_hbm, after))


class Share:
    def __init__(self, core, segment):
        self.segment = segment
        self.own = -(-segment // 256) * 128
        self.other = segment - self.own
        self.common = 2 * self.own - segment
        self.place = core * (segment - self.own)
        self.other_source = (1 - core) * self.common
        self.other_place = (1 - core) * self.own


def aligned(start, size, unit=128):
    return pl.ds(pl.multiple_of(start, unit), size)


def block_ref(refs, block, rows, shift=0):
    operand, index, first = block
    ref = refs[operand]
    for i in index:
        ref = ref.at[i]
    return ref.at[aligned(first + shift, rows), :]


def fetch(pick_ref, refs, choices, target, sems, shift=0):
    for which, blocks in enumerate(choices):

        @pl.when(pick_ref[0] == which)
        def _():
            for at, block in enumerate(blocks):
                source = block_ref(refs, block, target.shape[0], shift)
                count = source.shape[1]
                columns = slice(at * count, (at + 1) * count)
                pltpu.make_async_copy(source, target.at[:, columns], sems.at[at]).start()


def arrived(refs, choices, target, sems, at):
    source = block_ref(refs, choices[0][0], target.shape[0])
    count = source.shape[1]
    pltpu.make_async_copy(source, target.at[:, aligned(at * count, count)], sems.at[at]).wait()


def weight_copies(share, inward_ref, outward_ref, plain_ref, inward, outward, plain, sems):
    own = share.own
    copies = []
    for s in range(inward.shape[0] // own):
        place = aligned(s * share.segment + share.place, own)
        here = slice(s * own, (s + 1) * own)
        copies.append((inward_ref.at[place, :], inward.at[here, :]))
        copies.append((plain_ref.at[:, place], plain.at[:, here]))
    copies.append((outward_ref.at[aligned(share.place, own), :], outward))
    copies = [pltpu.make_async_copy(a, b, sems.at[i]) for i, (a, b) in enumerate(copies)]
    return copies


def products(share, core, left, right, plain, refs):
    whole_ref, low_ref, dots_ref, stage, low_stage, dots, sems = refs
    own, size = share.own, stage.shape[1]
    segments = right.shape[0] // own
    steps = left.shape[0] // size
    lanes = dots.shape[1]

    def copies(step, slot):
        rows = aligned(step * size, size)
        for s in range(segments):
            place = aligned(s * share.segment + share.place, own)
            yield pltpu.make_async_copy(
                stage.at[slot, :, s * own : (s + 1) * own], whole_ref.at[0, rows, place], sems.at[slot, s]
            )
        yield pltpu.make_async_copy(low_stage.at[slot], low_ref.at[rows, :], sems.at[slot, segments])

    def one(step, unused):
        slot = lax.rem(step, 2)
        rows = aligned(step * size, size)

        @pl.when(step >= 2)
        def _():
            for copy in copies(step, slot):
                copy.wait()

        value = dot_nt(left[rows, :], right[...])
        stage[slot] = value
        low_stage[slot] = value.astype(BF)
        value = value * plain[rows, :].astype(F32)
        total = 0.0
        for at in range(0, value.shape[1], lanes):
            part = value[:, at : at + lanes]
            if at % own < share.common:
                part = jnp.where(core == 0, part, 0.0)
            total = total + part
        dots[rows, :] = total
        for copy in copies(step, slot):
            copy.start()
        return 0

    lax.fori_loop(0, steps, one, 0)
    save = pltpu.make_async_copy(dots, dots_ref, sems.at[0, segments + 1])
    save.start()
    return [save] + [copy for step in range(max(steps - 2, 0), steps) for copy in copies(step, step % 2)]


def outward_products(share, left, right, refs):
    whole_ref, low_ref, stage, low_stage, sems = refs
    value = dot_nt(left[...], right[...])
    stage[...] = value
    low_stage[...] = value.astype(BF)
    copies = [
        pltpu.make_async_copy(stage, whole_ref.at[0, aligned(share.place, share.own), :], sems.at[0]),
        pltpu.make_async_copy(low_stage, low_ref, sems.at[1]),
    ]
    for copy in copies:
        copy.start()
    return copies


def feed_weights_kernel(layout, *refs):
    (streams, grads), operands = layout
    pick_ref = refs[0]
    blocks_refs = refs[1 : 1 + operands]
    gain_ref, inward_ref, outward_ref, plain_ref = refs[1 + operands : 5 + operands]
    outs, scratch = refs[5 + operands : 10 + operands], refs[10 + operands :]
    act_all, grad_all, hid_all, dboth_all, inward, outward, plain = scratch[:7]
    stage, low_stage, dots, out_stage, out_low, sems, weight_sems, out_sems = scratch[7:]
    core = pick_ref[1]
    share = Share(core, outward_ref.shape[0])
    hidden = share.own
    weights = weight_copies(share, inward_ref, outward_ref, plain_ref, inward, outward, plain, weight_sems)
    for copy in weights:
        copy.start()
    fetch(pick_ref, blocks_refs, streams, act_all, sems.at[0])
    fetch(pick_ref, blocks_refs, grads, grad_all, sems.at[1])
    for copy in weights:
        copy.wait()
    blocks = len(streams[0])
    wider = 2 * (act_all.shape[1] // blocks)

    def rows(step, unused):
        for at in (2 * step, 2 * step + 1):
            arrived(blocks_refs, streams, act_all, sems.at[0], at)
            arrived(blocks_refs, grads, grad_all, sems.at[1], at)
        here = aligned(step * wider, wider)
        normed, unused = normalize(act_all[:, here].astype(F32), 0)
        act = (normed * gain_ref[...]).astype(BF)
        act_all[:, here] = act
        both = dot_nn(inward[...], act)
        dhid = dot_nn(outward[...], grad_all[:, here])
        hid, dgate, dup = feed_back(both[:hidden], both[hidden:], dhid)
        hid_all[:, here] = hid
        dboth_all[:hidden, here] = dgate
        dboth_all[hidden:, here] = dup
        return 0

    lax.fori_loop(0, blocks // 2, rows, 0)
    copies = outward_products(share, hid_all, grad_all, (outs[1], outs[3], out_stage, out_low, out_sems.at[2]))
    copies += products(
        share, core, act_all, dboth_all, plain, (outs[0], outs[2], outs[4], stage, low_stage, dots, out_sems)
    )
    for copy in copies:
        copy.wait()


def attn_weights_kernel(layout, *refs):
    (streams, grads, firsts), operands = layout
    pick_ref, ends_ref = refs[:2]
    blocks_refs = refs[2 : 2 + operands]
    gain_ref, mix_ref, add_ref, inward_ref, outward_ref, plain_ref = refs[2 + operands : 8 + operands]
    outs, scratch = refs[8 + operands : 13 + operands], refs[13 + operands :]
    act_all, grad_all, attn_all, dproj_all, inward, outward, plain = scratch[:7]
    stage, low_stage, dots, out_stage, out_low, first_all, sems, weight_sems, out_sems = scratch[7:]
    core = pick_ref[1]
    share = Share(core, outward_ref.shape[0])
    width = share.own
    weights = weight_copies(share, inward_ref, outward_ref, plain_ref, inward, outward, plain, weight_sems)
    for copy in weights:
        copy.start()
    fetch(pick_ref, blocks_refs, streams, act_all, sems.at[0])
    fetch(pick_ref, blocks_refs, grads, grad_all, sems.at[1])
    fetch(pick_ref, blocks_refs, firsts, first_all, sems.at[2], share.place)
    for copy in weights:
        copy.wait()
    blocks = len(streams[0])
    count = act_all.shape[1] // blocks
    wider = 2 * count

    def rows(step, unused):
        for at in (2 * step, 2 * step + 1):
            arrived(blocks_refs, streams, act_all, sems.at[0], at)
            arrived(blocks_refs, grads, grad_all, sems.at[1], at)
            arrived(blocks_refs, firsts, first_all, sems.at[2], at)
        here = aligned(step * wider, wider)
        normed, unused = normalize(act_all[:, here].astype(F32), 0)
        act = (normed * gain_ref[...]).astype(BF)
        act_all[:, here] = act
        proj = dot_nn(inward[...], act).astype(BF)
        dattn = dot_nn(outward[...], grad_all[:, here]).astype(BF)
        first = first_all[:, here].astype(F32)
        mix = mix_ref[...]
        values = ((1.0 - mix) * proj[2 * width :].astype(F32) + mix * first).astype(BF)
        for i in range(2):
            cols = slice(i * count, (i + 1) * count)
            place = aligned(step * wider + i * count, count)
            allowed = allowed_keys(ends_at(ends_ref, step * 2 + i), count)
            dquery, dkeys, dmixed, attn = attend_back(
                proj[:width, cols],
                proj[width : 2 * width, cols],
                values[:, cols],
                dattn[:, cols],
                allowed,
                True,
            )
            dvalues = (1.0 - mix) * dmixed + add_ref[...] * first[:, cols]
            attn_all[:, place] = attn.astype(BF)
            dproj_all[:, place] = jnp.concatenate([dquery, dkeys, dvalues], axis=0).astype(BF)
        return 0

    lax.fori_loop(0, blocks // 2, rows, 0)
    copies = outward_products(share, attn_all, grad_all, (outs[1], outs[3], out_stage, out_low, out_sems.at[2]))
    copies += products(
        share, core, act_all, dproj_all, plain, (outs[0], outs[2], outs[4], stage, low_stage, dots, out_sems)
    )
    for copy in copies:
        copy.wait()


def weight_call(kernel, smem, sets, small, weights, name, after=()):
    arrays, layout = [], []
    for choices in sets:
        placed = []
        for blocks in choices:
            row = []
            for array, index, first in blocks:
                at = next((i for i, a in enumerate(arrays) if a is array), None)
                if at is None:
                    at = len(arrays)
                    arrays.append(array)
                row.append((at, index, first))
            placed.append(tuple(row))
        layout.append(tuple(placed))
    inward, outward, plain = weights
    segment, model = outward.shape
    segments = inward.shape[0] // segment
    own = Share(0, segment).own
    blocks = len(layout[0][0])
    total = blocks * arrays[0].shape[-1]
    block = model // 4
    extra = [pltpu.VMEM((own, total), BF)] if len(sets) == 3 else []
    whole = len(smem) + len(arrays) + len(small) + 3
    layout = (tuple(layout), len(arrays))

    def run(*refs):
        kernel(layout, *refs[:whole], *refs[whole + len(after) :])

    any_spec, vmem_spec = pl.BlockSpec(memory_space=pl.ANY), pl.BlockSpec(memory_space=pltpu.VMEM)
    return pl.pallas_call(
        run,
        in_specs=[pl.BlockSpec(memory_space=pltpu.SMEM)] * len(smem)
        + [any_spec] * len(arrays)
        + [vmem_spec] * len(small)
        + [any_spec] * (3 + len(after)),
        out_specs=[any_spec] * 5,
        out_shape=made_in_hbm(
            [
                shape_of((1, model, inward.shape[0]), F32),
                shape_of((1,) + outward.shape, F32),
                shape_of((model, segments * own), BF),
                shape_of((own, model), BF),
                shape_of((model, 128), F32),
            ]
        ),
        scratch_shapes=[
            pltpu.VMEM((model, total), BF),
            pltpu.VMEM((model, total), BF),
            pltpu.VMEM((own, total), BF),
            pltpu.VMEM((segments * own, total), BF),
            pltpu.VMEM((segments * own, model), BF),
            pltpu.VMEM((own, model), BF),
            pltpu.VMEM((model, segments * own), BF),
            pltpu.VMEM((2, block, segments * own), F32),
            pltpu.VMEM((2, block, segments * own), BF),
            pltpu.VMEM((model, 128), F32),
            pltpu.VMEM((own, model), F32),
            pltpu.VMEM((own, model), BF),
        ]
        + extra
        + [
            pltpu.SemaphoreType.DMA((len(sets), blocks)),
            pltpu.SemaphoreType.DMA((2 * segments + 1,)),
            pltpu.SemaphoreType.DMA((3, segments + 2)),
        ],
        compiler_params=pltpu.CompilerParams(vmem_limit_bytes=56 * MIB),
        cost_estimate=time_of(27.0),
        name=name,
    )(*smem, *map(in_hbm, arrays), *small, *map(in_hbm, weights), *map(in_hbm, after))


def fill_kernel(
    segment, core_ref, low_ref, out_low_ref, unused_ref, unused_out_ref, *refs
):
    whole_ref, whole_out_ref, low, out_low, stage, out_stage, in_sems, sems = refs
    share = Share(core_ref[0], segment)
    own, other, size = share.own, share.other, stage.shape[1]
    segments = low.shape[1] // own
    reads = [
        pltpu.make_async_copy(low_ref, low, in_sems.at[0]),
        pltpu.make_async_copy(out_low_ref, out_low, in_sems.at[1]),
    ]
    for copy in reads:
        copy.start()
    reads[0].wait()
    writes = []
    for block in range(stage.shape[0]):
        rows = slice(block * size, (block + 1) * size)
        for s in range(segments):
            here = slice(s * other, (s + 1) * other)
            stage[block, :, here] = low[rows, aligned(s * own + share.other_source, other)].astype(F32)
            place = aligned(s * segment + share.other_place, other)
            copy = pltpu.make_async_copy(
                stage.at[block, :, here], whole_ref.at[0, rows, place], sems.at[block, s]
            )
            copy.start()
            writes.append(copy)
    reads[1].wait()
    out_stage[...] = out_low[aligned(share.other_source, other), :].astype(F32)
    copy = pltpu.make_async_copy(
        out_stage, whole_out_ref.at[0, aligned(share.other_place, other), :], sems.at[0, segments]
    )
    copy.start()
    for copy in writes + [copy]:
        copy.wait()


def filled(core, low, out_low, whole, whole_out, after=()):
    segment, model = whole_out.shape[1:]
    segments = whole.shape[2] // segment
    share = Share(0, segment)
    steps = 4
    any_spec = pl.BlockSpec(memory_space=pl.ANY)

    def run(*refs):
        fill_kernel(segment, *refs[:5], *refs[5 + len(after) :])

    return pl.pallas_call(
        run,
        in_specs=[pl.BlockSpec(memory_space=pltpu.SMEM)] + [any_spec] * (4 + len(after)),
        out_specs=[any_spec] * 2,
        out_shape=made_in_hbm([whole, whole_out]),
        input_output_aliases={3: 0, 4: 1},
        scratch_shapes=[
            pltpu.VMEM(low.shape, BF),
            pltpu.VMEM(out_low.shape, BF),
            pltpu.VMEM((steps, model // steps, segments * share.other), F32),
            pltpu.VMEM((share.other, model), F32),
            pltpu.SemaphoreType.DMA((2,)),
            pltpu.SemaphoreType.DMA((steps, segments + 1)),
        ],
        compiler_params=pltpu.CompilerParams(vmem_limit_bytes=32 * MIB),
        cost_estimate=time_of(5.0),
        name="fill",
    )(core, *map(in_hbm, (low, out_low, whole, whole_out)), *map(in_hbm, after))


def body(tokens, cotangent, gains, attn_in, attn_out, ffn_in, ffn_out, mix_level, seq_lengths):
    section = lax.axis_index("section")
    core = lax.axis_index("dp") % 2
    lower = section < 2
    even = section % 2 == 0
    sections = lax.axis_size("section")
    dp = lax.axis_size("dp")
    group = min(dp, GROUP)
    planes = group // 2
    micro = seq_lengths.shape[0]
    count = tokens.shape[0] // micro
    piece = tokens.shape[1]
    inward, outward, feed_in, feed_out = attn_in[0], attn_out[0], ffn_in[0], ffn_out[0]
    model = inward.shape[0]
    width = outward.shape[0]

    low, high = (0, 1), (2, 3)
    everyone = low + high

    def send(x, mask, sources=everyone):
        return lax.ppermute(x, "section", [(i, i ^ mask) for i in sources])

    def planes_of(x, sources=everyone):
        def plane(by):
            pairs = [
                (s * dp + i, s * dp + i // group * group + (i % group // 2 + by) % planes * 2 + i % 2)
                for s in sources
                for i in range(dp)
            ]
            return lax.ppermute(x, ("section", "dp"), pairs)

        return [plane(by) for by in range(1, planes)]

    def other_core(x, sources=everyone):
        pairs = [(s * dp + i, s * dp + (i ^ 1)) for s in sources for i in range(dp)]
        return lax.ppermute(x, ("section", "dp"), pairs)

    near = jnp.where(lower, tokens, cotangent)
    far = jnp.where(lower, cotangent, tokens)
    got_far, got_across, got_near = send(far, 2), send(far, 3), send(near, 1)
    got_gains = send(gains, 1)
    ends = jnp.cumsum(seq_lengths, axis=1)
    ends = jnp.where(even, ends, ends[::-1])

    def by_half(mine, other):
        return [jnp.where(even, mine, other), jnp.where(even, other, mine)]

    ours, theirs = by_half(near, got_near), by_half(got_far, got_across)
    given = jnp.concatenate(
        [jnp.where(lower, a, b) for a, b in zip(ours + theirs, theirs + ours)], axis=1
    )
    top, bottom = given[:count], given[count:]
    given_own, given_mate = jnp.where(even, top, bottom), jnp.where(even, bottom, top)

    gain_attn = jnp.where(even, gains, got_gains)
    gain_feed = jnp.where(even, got_gains, gains)
    mix_all = jnp.repeat(mix_level.astype(F32) / 8.0, HEAD_DIM)
    mix_low, mix_high = mix_all[:width, None], mix_all[width:, None]
    mix = jnp.where(even, mix_low, mix_high)

    slot = shape_of((count, model), BF)
    half_turned = shape_of((width, count), BF)
    pair_half_turned = shape_of((2 * width, count), BF)
    slot_turned = shape_of((model, count), BF)
    pair_turned = shape_of((2, model, count), BF)
    pair_and_rows = shape_of((2, model + 16, count), BF)
    square_row = shape_of((1, count), F32)
    is_lower = lower.astype(jnp.int32)[None]

    attn_call = functools.partial(call, smem=1)
    part_mate, first_mate, square_mate = attn_call(
        attn_mate_kernel,
        [slot, half_turned, square_row],
        ends,
        given_mate,
        gain_attn,
        inward,
        outward,
        name="attn_mate",
    )
    got_own = send(part_mate, 1, low)
    part_own, first_both, square_own, given_stack = attn_call(
        attn_own_kernel,
        [slot, pair_half_turned, square_row, pair_and_rows],
        ends,
        given_own,
        gain_attn,
        inward,
        outward,
        given_mate,
        first_mate,
        name="attn_own",
    )
    got_mate = send(part_own, 1, low)
    first_over = send(first_both, 2, low)
    mid0_own, mid0_mate, mid0_stack, send_own, send_mate = call(
        feed_first_kernel,
        [slot, slot, pair_and_rows, slot, slot],
        given_own,
        given_mate,
        part_own,
        part_mate,
        got_own,
        got_mate,
        gain_feed,
        feed_in,
        feed_out,
        square_own,
        square_mate,
        vmem=32,
        loads=(feed_in, feed_out),
        name="feed_first",
        after=(first_over,),
    )
    x_a, x_b = send(send_own, 2, low), send(send_mate, 3, low)
    feed_in_turned, inward_turned = call(
        turn_kernel,
        [shape_of(feed_in.shape[::-1], BF), shape_of(inward.shape[::-1], BF)],
        feed_in,
        inward,
        vmem=32,
        name="turn_weights",
        after=(send_own,),
    )

    x1_own = call(sum_kernel, [slot], x_a, x_b, name="sum", after=(inward_turned,))[0]
    x1_mate = send(x1_own, 1, high)

    def attn_mixed(which, x):
        return attn_call(
            functools.partial(attn_mixed_kernel, which),
            [slot, square_row],
            ends,
            x,
            gain_attn,
            inward,
            outward,
            mix,
            first_over,
            name="attn_mixed",
        )

    part_own, square_own = attn_mixed(0, x1_own)
    got_mate = send(part_own, 1, high)
    part_mate, square_mate = attn_mixed(1, x1_mate)
    got_own = send(part_mate, 1, high)
    def everywhere(x):
        groups = [list(range(at, at + group)) for at in range(0, dp, group)]
        return lax.all_gather(x, "dp", axis=0, axis_index_groups=groups)

    def gathered(stack):
        every = everywhere(stack)
        return every, [(every, (d, i), 0) for d in range(group) for i in range(2)]

    all_given, set_given = gathered(given_stack)
    part_own, part_mate, mid1_own, mid1_mate, middle_stack, out_own, out_mate = call(
        feed_second_kernel,
        [slot, slot, slot, slot, pair_and_rows, slot, slot],
        is_lower,
        x1_own,
        x1_mate,
        part_own,
        part_mate,
        got_own,
        got_mate,
        given_own,
        given_mate,
        gain_feed,
        feed_in,
        feed_out,
        square_own,
        square_mate,
        mid0_stack,
        smem=1,
        vmem=36,
        loads=(feed_in, feed_out),
        name="feed_second",
        after=(all_given,),
    )
    got_own, got_mate = send(part_mate, 1, high), send(part_own, 1, high)
    middle1_own, middle1_mate, grad1_stack = call(
        middle_second_back_kernel,
        [slot, slot, pair_turned],
        mid1_own,
        mid1_mate,
        given_own,
        given_mate,
        part_own,
        part_mate,
        got_own,
        got_mate,
        gain_feed,
        name="middle_second_back",
    )

    def attn_back(which, grad, x, first, *mixed, after=()):
        outs = [slot] + [half_turned if which else pair_half_turned] * bool(mixed)
        return call(
            functools.partial(attn_back_kernel, bool(mixed), which),
            outs,
            ends,
            grad,
            x,
            gain_attn,
            inward,
            outward,
            first,
            *mixed,
            smem=1,
            name="attn_back",
            after=after,
        )

    part_mate, dfirst_mate = attn_back(1, middle1_mate, x1_mate, first_over, mix)
    got_own = send(part_mate, 1, high)
    part_own, dfirst_both = attn_back(0, middle1_own, x1_own, first_over, mix, dfirst_mate)
    dfirst = send(dfirst_both, 2, high)
    grad_x1 = call(
        input_back_kernel, [slot_turned], x1_own, middle1_own, part_own, got_own, gain_attn, name="input_back"
    )[0]
    grad_own, grad_mate = send(grad_x1, 2, high), send(grad_x1, 3, high)

    all_middle, set_middle = gathered(middle_stack)

    late = call(
        late_kernel,
        [shape_of((2 * model + 2 * width, count), BF)],
        is_lower,
        grad_own,
        grad_mate,
        grad1_stack,
        dfirst,
        first_over,
        smem=1,
        name="late",
    )[0]
    part_own, part_mate = call(
        feed_first_back_kernel,
        [slot, slot],
        mid0_own,
        mid0_mate,
        grad_own,
        grad_mate,
        gain_feed,
        feed_in,
        feed_out,
        vmem=36,
        loads=(feed_in, feed_out),
        name="feed_first_back",
        after=(late, all_middle),
    )
    got_own, got_mate = send(part_mate, 1, low), send(part_own, 1, low)
    middle_own, middle_mate, late_stack = call(
        middle_first_back_kernel,
        [slot, slot, pair_turned],
        is_lower,
        mid0_own,
        mid0_mate,
        grad_own,
        grad_mate,
        part_own,
        part_mate,
        got_own,
        got_mate,
        gain_feed,
        x1_own,
        x1_mate,
        smem=1,
        name="middle_first_back",
    )

    place = jnp.stack([section ^ mask for mask in range(sections)]).astype(jnp.int32)

    def owners(own, mate, row, holders, dtype, after):
        pieces = call(
            split_kernel,
            [shape_of((2 * count + 16, piece), BF)] * sections,
            place,
            own,
            mate,
            row,
            smem=1,
            name="split",
        )
        held = lower if holders == low else ~lower
        return call(
            join_kernel,
            [shape_of((2 * count, piece), dtype), shape_of(row.shape, F32)],
            jnp.stack([held, even]).astype(jnp.int32),
            pieces[0],
            *[send(pieces[mask], mask) for mask in range(1, sections)],
            smem=1,
            name="join",
            after=after,
        )

    part_mate = attn_back(1, middle_mate, given_mate, dfirst)[0]
    part_own = attn_back(0, middle_own, given_own, dfirst)[0]

    all_ends = all_given[:, :, model, : ends.shape[1]].reshape(2 * group, -1).astype(jnp.int32)
    all_late = everywhere(late)
    set_grad = [(all_late, (d,), at) for d in range(group) for at in (0, model)]
    set_first = [(all_late, (d,), 2 * model + at) for d in range(group) for at in (0, width)]
    unused, set_last = gathered(late_stack)

    squares = pl.pallas_call(
        square_sum_kernel,
        grid_spec=pltpu.PrefetchScalarGridSpec(
            num_scalar_prefetch=1,
            grid=(1,),
            in_specs=[pl.BlockSpec((group, 1, 16, count), lambda i, unused: (0, 0, model // 16, 0))],
            out_specs=pl.BlockSpec((1, 128), lambda i, unused: (0, 0)),
        ),
        out_shape=pltpu.HBM((1, 128), F32),
        compiler_params=pltpu.CompilerParams(vmem_limit_bytes=4 * MIB),
        name="square_sum",
    )(is_lower, in_hbm(all_middle))
    dinput, squares = owners(part_own, part_mate, squares, low, F32, ())
    if dp > group:
        squares = lax.psum(squares, "dp") / group
    norms = squares[0, :2] / (micro * count * dp * 2 * width)
    out, unused = owners(out_own, out_mate, jnp.zeros((1, 128), F32), high, BF, ())

    core_at = core.astype(jnp.int32)[None]
    pick = jnp.concatenate([1 - is_lower, core_at])
    mine = Share(0, width).own

    def core_heads(column):
        return lax.dynamic_slice_in_dim(column, core * mine, mine, 0)

    d_feed_in, d_feed_out, low_in, low_out, dots_feed = weight_call(
        feed_weights_kernel,
        (pick,),
        ((set_middle, set_middle), (set_grad, set_given)),
        (gain_feed.reshape(model, 1),),
        (feed_in_turned, feed_out, feed_in),
        "feed_weights",
        after=(dinput, out),
    )
    d_feed_in, d_feed_out = filled(core_at, other_core(low_in), other_core(low_out), d_feed_in, d_feed_out)
    d_in, d_out, low_in, low_out, dots_attn = weight_call(
        attn_weights_kernel,
        (pick, all_ends),
        ((set_given, set_last), (set_last, set_grad), (set_first, set_first)),
        (
            gain_attn.reshape(model, 1),
            core_heads(jnp.where(lower, 0.0, mix)),
            core_heads(jnp.where(lower, jnp.ones_like(mix), 0.0)),
        ),
        (inward_turned, outward, inward),
        "attn_weights",
    )
    d_in, d_out = filled(core_at, other_core(low_in), other_core(low_out), d_in, d_out)

    dots_attn, dots_feed = jnp.sum(dots_attn, axis=1)[None], jnp.sum(dots_feed, axis=1)[None]
    mine, sent = jnp.where(even, dots_attn, dots_feed), jnp.where(even, dots_feed, dots_attn)
    d_gain = mine + send(sent, 1)
    d_gain = d_gain + other_core(d_gain)
    if dp > group:
        d_gain = lax.psum(d_gain, "dp") / group
        across = [list(range(at, dp, group)) for at in range(group)]
        d_in, d_out, d_feed_in, d_feed_out = [
            lax.psum(x.astype(BF), "dp", axis_index_groups=across).astype(F32)
            for x in (d_in, d_out, d_feed_in, d_feed_out)
        ]
    d_gain = d_gain / gains
    return (out, dinput, d_gain, d_in, d_out, d_feed_in, d_feed_out, norms[0], norms[1])


def solution(mesh):
    in_specs = (
        P("dp", "section"),
        P("dp", "section"),
        P("section", None),
        P("section", None, None),
        P("section", None, None),
        P("section", None, None),
        P("section", None, None),
        P(),
        P("dp", None),
    )
    out_specs = (
        P("dp", "section"),
        P("dp", "section"),
        P("section", None),
        P("section", None, None),
        P("section", None, None),
        P("section", None, None),
        P("section", None, None),
        P(),
        P(),
    )
    return jax.shard_map(body, mesh=mesh, in_specs=in_specs, out_specs=out_specs, check_vma=False)
```

```python
import functools

import jax
import jax.numpy as jnp
from jax import lax
from jax.experimental import pallas as pl
from jax.experimental.pallas import tpu as pltpu
from jax.sharding import PartitionSpec as P

HEAD_DIM = 64
EPS = 1e-05
NEG = -1e30
GROUP = 8
BF = jnp.bfloat16
F32 = jnp.float32
MIB = 1024 * 1024
WEIGHTS_FROM = 500_000


TIMES = {
    "turn_weights": 5.9,
    "attn_mate": 3.1,
    "attn_own": 3.5,
    "feed_first": 5.3,
    "sum": 1.8,
    "stack": 1.9,
    "attn_mixed": 3.3,
    "feed_second": 8.5,
    "middle_second_back": 3.1,
    "attn_back": 4.7,
    "input_back": 2.3,
    "late": 2.2,
    "feed_first_back": 6.8,
    "middle_first_back": 3.3,
    "split": 1.9,
    "join": 1.9,
    "add": 1.2,
}


def time_of(microseconds):
    return pl.CostEstimate(flops=int(microseconds * 1.15e9), bytes_accessed=1, transcendentals=0)


def dot_nn(left, right):
    return lax.dot_general(left, right, (((1,), (0,)), ((), ())), preferred_element_type=F32)


def dot_nt(left, right):
    return lax.dot_general(left, right, (((1,), (1,)), ((), ())), preferred_element_type=F32)


def dot_tn(left, right):
    return lax.dot_general(left, right, (((0,), (0,)), ((), ())), preferred_element_type=F32)


def shape_of(shape, dtype):
    return jax.ShapeDtypeStruct(shape, dtype)


def in_hbm(a):
    return pltpu.with_memory_space_constraint(a, pltpu.HBM)


def made_in_hbm(outs):
    return [pltpu.HBM(o.shape, o.dtype) for o in outs]


def normalize(stream, axis):
    rscale = lax.rsqrt(jnp.mean(stream * stream, axis=axis, keepdims=True) + EPS)
    return stream * rscale, rscale


def norm_back(stream, grad_out, dact, gain):
    normed, rscale = normalize(stream, -1)
    dnorm = dact * gain
    mean = jnp.mean(dnorm * normed, axis=-1, keepdims=True)
    return grad_out + rscale * (dnorm - normed * mean)


def turned(rows):
    return rows.astype(F32).T.astype(BF)


def allowed_keys(ends, count):
    key = lax.broadcasted_iota(jnp.int32, (count, count), 0)
    query = lax.broadcasted_iota(jnp.int32, (count, count), 1)
    segment_key = sum((key >= end).astype(jnp.int32) for end in ends)
    segment_query = sum((query >= end).astype(jnp.int32) for end in ends)
    return (key <= query) & (segment_key == segment_query)


def heads_of(array, first=0):
    return [array[at : at + HEAD_DIM] for at in range(first, array.shape[0], HEAD_DIM)]


def softmax_keys(scores, allowed):
    scores = jnp.where(allowed, scores * HEAD_DIM**-0.5, NEG)
    exponent = jnp.exp(scores - jnp.max(scores, axis=0, keepdims=True))
    return exponent * (1.0 / jnp.sum(exponent, axis=0, keepdims=True))


def attend(query, keys, values, allowed):
    query, keys, values = heads_of(query), heads_of(keys), heads_of(values)
    scores = [dot_tn(k, q) for q, k in zip(query, keys)]
    probs = [softmax_keys(s, allowed).astype(BF) for s in scores]
    return jnp.concatenate([dot_nn(v, p) for v, p in zip(values, probs)], axis=0)


def attend_back(query, keys, values, dattn, allowed):
    scores = [dot_tn(k, q) for q, k in zip(heads_of(query), heads_of(keys))]
    return attend_back_from(query, keys, values, dattn, lambda: [softmax_keys(s, allowed) for s in scores], False)


def attend_back_from(query, keys, values, dattn, probs_of, forward):
    query, keys, values, dattn = [heads_of(a) for a in (query, keys, values, dattn)]
    dprobs = [dot_tn(v, d) for v, d in zip(values, dattn)]
    low_probs, dscores = [], []
    for probs, dprob in zip(probs_of(), dprobs):
        low_probs.append(probs.astype(BF))
        probs = probs.astype(F32)
        dscores.append((probs * (dprob - jnp.sum(dprob * probs, axis=0, keepdims=True))).astype(BF))
    attn = None
    if forward:
        attn = jnp.concatenate([dot_nn(v, p) for v, p in zip(values, low_probs)], axis=0)
    dquery = jnp.concatenate([dot_nn(k, d) for k, d in zip(keys, dscores)], axis=0) * HEAD_DIM**-0.5
    dkeys = jnp.concatenate([dot_nt(q, d) for q, d in zip(query, dscores)], axis=0) * HEAD_DIM**-0.5
    dmixed = jnp.concatenate([dot_nt(d, p) for d, p in zip(dattn, low_probs)], axis=0)
    return dquery, dkeys, dmixed, attn


def swish(gate, up):
    sigmoid = 1.0 / (1.0 + jnp.exp(-gate))
    return sigmoid, gate * sigmoid


def feed_back(gate, up, dhid):
    sigmoid, silu = swish(gate, up)
    hid = (silu * up).astype(BF)
    dgate = dhid * up * (sigmoid * (1.0 + gate * (1.0 - sigmoid)))
    dup = dhid * silu
    return hid, dgate.astype(BF), dup.astype(BF)


def ends_at(ends_ref, slot):
    return [ends_ref[slot, i] for i in range(ends_ref.shape[1])]


def rounded_sum(left, right):
    return left.astype(F32) + right.astype(F32)


def turn_kernel(a_ref, b_ref, a_out, b_out):
    size = 256
    row = lax.broadcasted_iota(jnp.int32, (size, size), 0)
    col = lax.broadcasted_iota(jnp.int32, (size, size), 1)
    identity = jnp.where(row == col, 1.0, 0.0).astype(BF)
    for source, target in ((a_ref, a_out), (b_ref, b_out)):
        for at in range(0, source.shape[1], size):
            target[at : at + size, :] = dot_nt(identity, source[:, at : at + size]).astype(BF)


def attend_forward(slot, ends_ref, x, gain_ref, inward_ref, mix, first):
    width = inward_ref.shape[1] // 3
    normed, unused = normalize(x.astype(F32), -1)
    act = (normed * gain_ref[...]).astype(BF)
    proj = dot_nn(act, inward_ref[...]).T.astype(BF)
    values = proj[2 * width :]
    if mix is not None:
        values = ((1.0 - mix) * values.astype(F32) + mix * first.astype(F32)).astype(BF)
    wide = values.astype(F32)
    square = jnp.sum(wide * wide, axis=0, keepdims=True)
    allowed = allowed_keys(ends_at(ends_ref, slot), x.shape[0])
    attn = attend(proj[:width], proj[width : 2 * width], values, allowed)
    return attn.T.astype(BF), values, square


def ends_rows(ends_ref, slot, shape):
    lane = lax.broadcasted_iota(jnp.int32, shape, 1)
    ends = ends_at(ends_ref, slot)
    return sum(jnp.where(lane == i, end, 0) for i, end in enumerate(ends)).astype(F32).astype(BF)


def square_rows(square, rows):
    parts = []
    for unused in range(3):
        parts.append(square.astype(BF).astype(F32))
        square = square - parts[-1]
    return jnp.concatenate(parts + [jnp.zeros((rows - 3, square.shape[1]), F32)], axis=0).astype(BF)


def attn_mate_kernel(ends_ref, x_ref, gain_ref, inward_ref, outward_ref, part_ref, values_ref, square_ref):
    attn, values, square = attend_forward(1, ends_ref, x_ref[...], gain_ref, inward_ref, None, None)
    values_ref[...] = values
    square_ref[...] = square
    part_ref[...] = dot_nn(attn, outward_ref[...]).astype(BF)


def attn_own_kernel(
    ends_ref,
    x_ref,
    gain_ref,
    inward_ref,
    outward_ref,
    mate_ref,
    values_mate_ref,
    part_ref,
    values_ref,
    square_ref,
    turned_ref,
):
    model = x_ref.shape[1]
    width = outward_ref.shape[0]
    attn, values, square = attend_forward(0, ends_ref, x_ref[...], gain_ref, inward_ref, None, None)
    part_ref[...] = dot_nn(attn, outward_ref[...]).astype(BF)
    values_ref[:width] = values
    values_ref[width:] = values_mate_ref[...]
    square_ref[...] = square
    for slot, ref in enumerate((x_ref, mate_ref)):
        turned_ref[slot, :model] = turned(ref[...])
        turned_ref[slot, model:] = ends_rows(ends_ref, slot, (turned_ref.shape[1] - model, turned_ref.shape[2]))


def attn_mixed_kernel(slot, ends_ref, x_ref, gain_ref, inward_ref, outward_ref, mix_ref, first_ref, *refs):
    part_ref, square_ref = refs[-2:]
    width = outward_ref.shape[0]
    attn, unused, square = attend_forward(
        slot,
        ends_ref,
        x_ref[...],
        gain_ref,
        inward_ref,
        mix_ref[...],
        first_ref[slot * width : (slot + 1) * width],
    )
    part_ref[...] = dot_nn(attn, outward_ref[...]).astype(BF)
    if slot == 0:
        square_ref[...] = square
        return
    lower_ref, low_ref, own_ref, square_own_ref, square_low_own, square_low_mate = refs[:6]
    stack_ref = square_ref
    model = x_ref.shape[1]
    is_lower = lower_ref[0, 0] == 1
    square = jnp.where(is_lower, square_low_own[...] + square_low_mate[...], square + square_own_ref[...])
    rows = square_rows(square, stack_ref.shape[1] - model)
    stack_ref[0, model:] = rows
    stack_ref[1, model:] = jnp.zeros_like(rows)
    stack_ref[0, :model] = jnp.where(is_lower, low_ref[0], turned(own_ref[...]))
    stack_ref[1, :model] = jnp.where(is_lower, low_ref[1], turned(x_ref[...]))


def sum_kernel(a_ref, b_ref, out_ref):
    out_ref[...] = rounded_sum(a_ref[...], b_ref[...]).astype(BF)


def attn_sums(refs):
    own_ref, mate_ref, part_own_ref, part_mate_ref, got_own_ref, got_mate_ref = refs
    own = (own_ref[...].astype(F32) + rounded_sum(part_own_ref[...], got_own_ref[...])).astype(BF)
    mate = (mate_ref[...].astype(F32) + rounded_sum(part_mate_ref[...], got_mate_ref[...])).astype(BF)
    return own, mate


def feed_loads(inward_ref, outward_ref, inward, outward, sems):
    hidden = outward.shape[0]
    copies = [
        pltpu.make_async_copy(inward_ref.at[:, 0:hidden], inward.at[:, 0:hidden], sems.at[0]),
        pltpu.make_async_copy(inward_ref.at[:, hidden : 2 * hidden], inward.at[:, hidden : 2 * hidden], sems.at[1]),
        pltpu.make_async_copy(outward_ref, outward, sems.at[2]),
    ]
    for copy in copies:
        copy.start()
    return copies


def feed_first_kernel(*refs):
    gain_ref, inward_hbm, outward_hbm = refs[6:9]
    mid_own_ref, mid_mate_ref, stack_ref, send_own_ref, send_mate_ref = refs[9:14]
    inward_ref, outward_ref, sems = refs[14:]
    loads = feed_loads(inward_hbm, outward_hbm, inward_ref, outward_ref, sems)
    own, mate = attn_sums(refs[:6])
    count = own.shape[0]
    mid_own_ref[...] = own
    mid_mate_ref[...] = mate
    stack_ref[0] = turned(own)
    stack_ref[1] = turned(mate)
    stream = jnp.concatenate([own, mate], axis=0).astype(F32)
    normed, unused = normalize(stream, -1)
    act = (normed * gain_ref[...]).astype(BF)
    hidden = outward_ref.shape[0]
    loads[0].wait()
    gate = dot_nn(act, inward_ref[:, :hidden])
    loads[1].wait()
    up = dot_nn(act, inward_ref[:, hidden:])
    unused, silu = swish(gate, up)
    loads[2].wait()
    part = dot_nn((silu * up).astype(BF), outward_ref[...])
    send_own_ref[...] = (stream[:count] + part[:count]).astype(BF)
    send_mate_ref[...] = part[count:].astype(BF)


def feed_second_kernel(*refs):
    grad_own_ref, grad_mate_ref, gain_ref, inward_hbm, outward_hbm = refs[6:11]
    part_own_ref, part_mate_ref, mid_own_ref, mid_mate_ref, turned_ref, out_own_ref, out_mate_ref = refs[11:18]
    inward_ref, outward_ref, sems = refs[18:]
    loads = feed_loads(inward_hbm, outward_hbm, inward_ref, outward_ref, sems)
    own, mate = attn_sums(refs[:6])
    count = own.shape[0]
    mid_own_ref[...] = own
    mid_mate_ref[...] = mate
    turned_ref[...] = turned(own)
    stream = jnp.concatenate([own, mate], axis=0).astype(F32)
    grad = jnp.concatenate([grad_own_ref[...], grad_mate_ref[...]], axis=0)
    normed, unused = normalize(stream, -1)
    act = (normed * gain_ref[...]).astype(BF)
    hidden = outward_ref.shape[0]
    loads[0].wait()
    gate = dot_nn(act, inward_ref[:, :hidden])
    loads[1].wait()
    up = dot_nn(act, inward_ref[:, hidden:])
    loads[2].wait()
    dhid = dot_nt(grad, outward_ref[...])
    hid, dgate, dup = feed_back(gate, up, dhid)
    dact = dot_nt(dgate, inward_ref[:, :hidden]) + dot_nt(dup, inward_ref[:, hidden:])
    part_own_ref[...] = dact[:count].astype(BF)
    part_mate_ref[...] = dact[count:].astype(BF)
    part = dot_nn(hid, outward_ref[...])
    out_own_ref[...] = (stream[:count] + part[:count]).astype(BF)
    out_mate_ref[...] = part[count:].astype(BF)


def feed_first_back_kernel(
    own_ref,
    mate_ref,
    grad_own_ref,
    grad_mate_ref,
    gain_ref,
    inward_hbm,
    outward_hbm,
    part_own_ref,
    part_mate_ref,
    inward_ref,
    outward_ref,
    sems,
):
    loads = feed_loads(inward_hbm, outward_hbm, inward_ref, outward_ref, sems)
    count = own_ref.shape[0]
    stream = jnp.concatenate([own_ref[...], mate_ref[...]], axis=0).astype(F32)
    grad = jnp.concatenate([turned(grad_own_ref[...]), turned(grad_mate_ref[...])], axis=0)
    normed, unused = normalize(stream, -1)
    act = (normed * gain_ref[...]).astype(BF)
    hidden = outward_ref.shape[0]
    loads[0].wait()
    gate = dot_nn(act, inward_ref[:, :hidden])
    loads[1].wait()
    up = dot_nn(act, inward_ref[:, hidden:])
    loads[2].wait()
    dhid = dot_nt(grad, outward_ref[...])
    unused, dgate, dup = feed_back(gate, up, dhid)
    dact = dot_nt(dgate, inward_ref[:, :hidden]) + dot_nt(dup, inward_ref[:, hidden:])
    part_own_ref[...] = dact[:count].astype(BF)
    part_mate_ref[...] = dact[count:].astype(BF)


def middle_grads(refs, gain_ref, turned_grads):
    for s_ref, g_ref, p_ref, r_ref in zip(*refs):
        grad = g_ref[...].astype(F32)
        grad = norm_back(
            s_ref[...].astype(F32),
            grad.T if turned_grads else grad,
            rounded_sum(p_ref[...], r_ref[...]),
            gain_ref[...],
        )
        yield grad.astype(BF)


def middle_first_back_kernel(lower_ref, *refs):
    gain_ref, grad_high_ref, dfirst_ref, first_ref = refs[8:12]
    out_own_ref, out_mate_ref, last_ref = refs[12:]
    pairs = refs[0:2], refs[2:4], refs[4:6], refs[6:8]
    own, mate = middle_grads(pairs, gain_ref, True)
    out_own_ref[...] = own
    out_mate_ref[...] = mate
    model = own.shape[1]
    is_lower = lower_ref[0] == 1
    last_ref[:model] = jnp.where(is_lower, turned(own), grad_high_ref[0])
    last_ref[model : 2 * model] = jnp.where(is_lower, turned(mate), grad_high_ref[1])
    last_ref[2 * model :] = jnp.where(is_lower, dfirst_ref[...], first_ref[...])


def middle_second_back_kernel(*refs):
    gain_ref, out_own_ref, out_mate_ref, turned_ref = refs[8:]
    pairs = refs[0:2], refs[2:4], refs[4:6], refs[6:8]
    own, mate = middle_grads(pairs, gain_ref, False)
    out_own_ref[...] = own
    out_mate_ref[...] = mate
    turned_ref[0] = turned(own)
    turned_ref[1] = turned(mate)


def attn_back_kernel(mixing, slot, *refs):
    ends_ref, grad_ref, x_ref, gain_ref, inward_ref, outward_ref, first_ref = refs[:7]
    count = x_ref.shape[0]
    width = outward_ref.shape[0]
    first = first_ref[slot * width : (slot + 1) * width].astype(F32)
    normed, unused = normalize(x_ref[...].astype(F32), -1)
    act = (normed * gain_ref[...]).astype(BF)
    allowed = allowed_keys(ends_at(ends_ref, slot), count)
    dattn = dot_nt(grad_ref[...], outward_ref[...]).T.astype(BF)
    proj = dot_nn(act, inward_ref[...]).T.astype(BF)
    values = proj[2 * width :]
    if mixing:
        mix = refs[7][...]
        values = ((1.0 - mix) * values.astype(F32) + mix * first).astype(BF)
    dquery, dkeys, dmixed, unused = attend_back(proj[:width], proj[width : 2 * width], values, dattn, allowed)
    if mixing:
        dfirst = (mix * dmixed).astype(BF)
        dvalues = (1.0 - mix) * dmixed
        if slot == 1:
            refs[-1][...] = dfirst
        else:
            refs[-1][:width] = dfirst
            refs[-1][width:] = refs[8][...]
    else:
        dvalues = dmixed + first
    dproj = jnp.concatenate([dquery, dkeys, dvalues], axis=0).T.astype(BF)
    dact = dot_nt(dproj, inward_ref[...])
    if mixing:
        refs[-2][...] = dact.astype(BF)
    else:
        grad = 0.0 if slot else grad_ref[...].astype(F32)
        refs[-1][...] = norm_back(x_ref[...].astype(F32), grad, dact, gain_ref[...]).astype(BF)


def input_back_kernel(x_ref, grad_ref, part_ref, got_ref, gain_ref, out_ref):
    grad = norm_back(
        x_ref[...].astype(F32),
        grad_ref[...].astype(F32),
        rounded_sum(part_ref[...], got_ref[...]),
        gain_ref[...],
    )
    out_ref[...] = grad.T.astype(BF)


def split_kernel(place_ref, a_own_ref, a_mate_ref, b_own_ref, b_mate_ref, row_ref, *refs):
    count, piece = a_own_ref.shape[0], refs[0].shape[1]
    for mask, ref in enumerate(refs):
        columns = aligned(place_ref[mask] * piece, piece)
        for i, source in enumerate((a_own_ref, a_mate_ref, b_own_ref, b_mate_ref)):
            ref[i * count : (i + 1) * count] = source[:, columns]
        row = jnp.concatenate([row_ref[...], jnp.zeros((1, piece - row_ref.shape[1]), F32)], axis=1)
        ref[4 * count :] = square_rows(row, ref.shape[0] - 4 * count)


def join_kernel(flags_ref, own_ref, beside_ref, over_ref, across_ref, a_ref, b_ref, row_ref):
    count = a_ref.shape[0] // 2
    lower, even = flags_ref[0] == 1, flags_ref[1] == 1
    for first, out_ref, holds in ((0, a_ref, lower), (2 * count, b_ref, jnp.logical_not(lower))):
        rows = slice(first, first + 2 * count)
        same = jnp.where(holds, own_ref[rows], over_ref[rows]).astype(F32)
        other = jnp.where(holds, beside_ref[rows], across_ref[rows]).astype(F32)
        own, mate = same[:count] + other[count:], same[count:] + other[:count]
        out_ref[:count] = jnp.where(even, own, mate).astype(out_ref.dtype)
        out_ref[count:] = jnp.where(even, mate, own).astype(out_ref.dtype)
    lanes = row_ref.shape[1]
    rows = [r[4 * count :, :lanes].astype(F32) for r in (own_ref, beside_ref, over_ref, across_ref)]
    row_ref[...] = jnp.sum(sum(rows), axis=0, keepdims=True)


def late_kernel(lower_ref, low_ref, high_ref, out_ref):
    out_ref[...] = jnp.where(lower_ref[0] == 1, low_ref[...], high_ref[...])


def square_sum_kernel(lower_ref, rows_ref, out_ref):
    total = jnp.sum(rows_ref[...].astype(F32))
    lane = lax.broadcasted_iota(jnp.int32, out_ref.shape, 1)
    out_ref[...] = jnp.where(lane == 1 - lower_ref[0], total, 0.0)


def add_kernel(a_ref, b_ref, out_ref):
    out_ref[...] = a_ref[...] + b_ref[...]


def call(kernel, outs, *args, smem=0, name=None, after=(), vmem=16, loads=()):
    whole = len(args)
    held = {id(w) for w in loads}

    def run(*refs):
        kernel(*refs[:whole], *refs[whole + len(after) :])

    def whole_block(a):
        return pl.BlockSpec(a.shape, lambda i: (0,) * len(a.shape))

    def given_spec(a):
        if id(a) in held:
            return pl.BlockSpec(memory_space=pl.ANY)
        return pl.BlockSpec(memory_space=pltpu.VMEM) if a.size >= WEIGHTS_FROM else whole_block(a)

    return pl.pallas_call(
        run,
        grid=(1,),
        out_shape=made_in_hbm(outs),
        in_specs=[pl.BlockSpec(memory_space=pltpu.SMEM)] * smem
        + [given_spec(a) for a in args[smem:]]
        + [pl.BlockSpec(memory_space=pl.ANY)] * len(after),
        out_specs=[whole_block(o) for o in outs],
        scratch_shapes=[pltpu.VMEM(w.shape, w.dtype) for w in loads]
        + [pltpu.SemaphoreType.DMA((1 + len(loads),))] * bool(loads),
        compiler_params=pltpu.CompilerParams(vmem_limit_bytes=vmem * MIB),
        cost_estimate=time_of(TIMES.get(name, 1.0)),
        name=name,
    )(*args[:smem], *[a if a.size >= WEIGHTS_FROM and id(a) not in held else in_hbm(a) for a in args[smem:]], *map(in_hbm, after))


def gate(array, after):
    spec = pl.BlockSpec(memory_space=pl.ANY)
    return pl.pallas_call(
        lambda *refs: None,
        out_shape=pltpu.HBM(array.shape, array.dtype),
        in_specs=[spec] * (1 + len(after)),
        out_specs=spec,
        input_output_aliases={0: 0},
        compiler_params=pltpu.CompilerParams(vmem_limit_bytes=MIB),
        cost_estimate=time_of(0.1),
        name="gate",
    )(in_hbm(array), *map(in_hbm, after))


class Share:
    def __init__(self, core, segment):
        self.segment = segment
        self.own = -(-segment // 256) * 128
        self.other = segment - self.own
        self.common = 2 * self.own - segment
        self.place = core * (segment - self.own)
        self.other_source = (1 - core) * self.common
        self.other_place = (1 - core) * self.own


def aligned(start, size, unit=128):
    return pl.ds(pl.multiple_of(start, unit), size)


def block_ref(refs, block, rows, shift=0):
    operand, index, first = block[:3]
    ref = refs[operand]
    for i in index:
        ref = ref.at[i]
    return ref.at[aligned(first + shift, rows), :]


def fetch(pick_ref, refs, choices, target, sems, shift=0):
    for which, blocks in enumerate(choices):

        @pl.when(pick_ref[0] == which)
        def _():
            for at, block in enumerate(blocks):
                source = block_ref(refs, block, target.shape[0], shift)
                count = source.shape[1]
                if block[3] is not None:
                    plane, other, slot = block[3]
                    core = 1 - pick_ref[1] if other else pick_ref[1]
                    at = (2 * plane + core) * 2 + slot
                columns = aligned(at * count, count)
                pltpu.make_async_copy(source, target.at[:, columns], sems.at[at]).start()


def arrived(refs, choices, target, sems, at):
    source = block_ref(refs, choices[0][0], target.shape[0])
    count = source.shape[1]
    pltpu.make_async_copy(source, target.at[:, aligned(at * count, count)], sems.at[at]).wait()


def weight_copies(share, inward_ref, outward_ref, plain_ref, inward, outward, plain, sems):
    own = share.own
    first, last = [(outward_ref.at[aligned(share.place, own), :], outward)], []
    for s in range(inward.shape[0] // own):
        place = aligned(s * share.segment + share.place, own)
        here = slice(s * own, (s + 1) * own)
        first.append((inward_ref.at[place, :], inward.at[here, :]))
        last.append((plain_ref.at[:, place], plain.at[:, here]))
    copies = [pltpu.make_async_copy(a, b, sems.at[i]) for i, (a, b) in enumerate(first + last)]
    return copies[: len(first)], copies[len(first) :]


def products(share, core, left, right, plain, refs):
    whole_ref, low_ref, dots_ref, stage, low_stage, dots, sems = refs
    size, lanes = stage.shape[2], dots.shape[1]
    each = share.own // size
    steps = right.shape[0] // size

    def copies(step, slot):
        place = lax.div(step, each) * share.segment + share.place + lax.rem(step, each) * size
        columns = aligned(place, size)
        yield pltpu.make_async_copy(stage.at[slot], whole_ref.at[0, :, columns], sems.at[slot, 0])
        yield pltpu.make_async_copy(low_stage.at[slot], low_ref.at[:, aligned(step * size, size)], sems.at[slot, 1])

    dots[...] = jnp.zeros_like(dots)

    def one(step, unused):
        slot = lax.rem(step, 2)
        here = aligned(step * size, size)

        @pl.when(step >= 2)
        def _():
            for copy in copies(step, slot):
                copy.wait()

        value = dot_nt(left[...], right[here, :])
        stage[slot] = value
        low_stage[slot] = value.astype(BF)
        value = value * plain[:, here].astype(F32)
        total = 0.0
        for at in range(0, size, lanes):
            part = value[:, at : at + lanes]
            if at < share.common:
                part = jnp.where((core == 0) | (lax.rem(step, each) > 0), part, 0.0)
            total = total + part
        dots[...] += total
        for copy in copies(step, slot):
            copy.start()
        return 0

    lax.fori_loop(0, steps, one, 0)
    save = pltpu.make_async_copy(dots, dots_ref, sems.at[0, 2])
    save.start()
    return [save] + [copy for step in range(max(steps - 2, 0), steps) for copy in copies(step, step % 2)]


def outward_products(share, left, right, refs):
    whole_ref, low_ref, stage, low_stage, sems = refs
    value = dot_nt(left[...], right[...])
    stage[...] = value
    low_stage[...] = value.astype(BF)
    copies = [
        pltpu.make_async_copy(stage, whole_ref.at[0, aligned(share.place, share.own), :], sems.at[0]),
        pltpu.make_async_copy(low_stage, low_ref, sems.at[1]),
    ]
    for copy in copies:
        copy.start()
    return copies


def feed_weights_kernel(layout, *refs):
    (streams, grads), operands = layout
    pick_ref = refs[0]
    blocks_refs = refs[1 : 1 + operands]
    gain_ref, inward_ref, outward_ref, plain_ref = refs[1 + operands : 5 + operands]
    outs, scratch = refs[5 + operands : 10 + operands], refs[10 + operands :]
    act_all, grad_all, hid_all, dboth_all, inward, outward, plain = scratch[:7]
    stage, low_stage, dots, out_stage, out_low, sems, weight_sems, out_sems = scratch[7:]
    core = pick_ref[1]
    share = Share(core, outward_ref.shape[0])
    hidden = share.own
    weights, plain_copies = weight_copies(
        share, inward_ref, outward_ref, plain_ref, inward, outward, plain, weight_sems
    )
    for copy in weights:
        copy.start()
    for copy in weights:
        copy.wait()
    fetch(pick_ref, blocks_refs, streams, act_all, sems.at[0])
    fetch(pick_ref, blocks_refs, grads, grad_all, sems.at[1])
    for copy in plain_copies:
        copy.start()
    blocks = len(streams[0])
    wider = 2 * (act_all.shape[1] // blocks)

    def rows(step, unused):
        for at in (2 * step, 2 * step + 1):
            arrived(blocks_refs, streams, act_all, sems.at[0], at)
            arrived(blocks_refs, grads, grad_all, sems.at[1], at)
        here = aligned(step * wider, wider)
        normed, unused = normalize(act_all[:, here].astype(F32), 0)
        act = (normed * gain_ref[...]).astype(BF)
        act_all[:, here] = act
        both = dot_nn(inward[...], act)
        dhid = dot_nn(outward[...], grad_all[:, here])
        hid, dgate, dup = feed_back(both[:hidden], both[hidden:], dhid)
        hid_all[:, here] = hid
        dboth_all[:hidden, here] = dgate
        dboth_all[hidden:, here] = dup
        return 0

    lax.fori_loop(0, blocks // 2, rows, 0)
    for copy in plain_copies:
        copy.wait()
    copies = outward_products(share, hid_all, grad_all, (outs[1], outs[3], out_stage, out_low, out_sems.at[2]))
    copies += products(
        share, core, act_all, dboth_all, plain, (outs[0], outs[2], outs[4], stage, low_stage, dots, out_sems)
    )
    for copy in copies:
        copy.wait()


def attn_scores_kernel(layout, *refs):
    (streams,), operands = layout
    pick_ref, ends_ref = refs[:2]
    blocks_refs = refs[2 : 2 + operands]
    gain_ref, inward_ref = refs[2 + operands : 4 + operands]
    outs, scratch = refs[4 + operands : 7 + operands], refs[7 + operands :]
    act_all, proj_all, probs_all, inward, sems, weight_sems, out_sems = scratch
    own = inward.shape[0] // 3
    share = Share(pick_ref[1], inward_ref.shape[0] // 3)
    copies = []
    for s in range(3):
        place = aligned(s * share.segment + share.place, own)
        copies.append(
            pltpu.make_async_copy(inward_ref.at[place, :], inward.at[s * own : (s + 1) * own, :], weight_sems.at[s])
        )
    for copy in copies:
        copy.start()
    for copy in copies:
        copy.wait()
    fetch(pick_ref, blocks_refs, streams, act_all, sems)
    blocks = len(streams[0])
    count = act_all.shape[1] // blocks
    wider = 2 * count

    def saves(step):
        here = aligned(step * wider, wider)
        for i, (source, target) in enumerate(zip((act_all, proj_all, probs_all), outs)):
            yield pltpu.make_async_copy(source.at[:, here], target.at[:, here], out_sems.at[i, step])

    def rows(step, unused):
        for at in (2 * step, 2 * step + 1):
            arrived(blocks_refs, streams, act_all, sems, at)
        here = aligned(step * wider, wider)
        normed, unused = normalize(act_all[:, here].astype(F32), 0)
        act = (normed * gain_ref[...]).astype(BF)
        act_all[:, here] = act
        proj = dot_nn(inward[...], act).astype(BF)
        proj_all[:, here] = proj
        for i in range(2):
            cols = slice(i * count, (i + 1) * count)
            allowed = allowed_keys(ends_at(ends_ref, step * 2 + i), count)
            query, keys = heads_of(proj[:own, cols]), heads_of(proj[own : 2 * own, cols])
            scores = [dot_tn(k, q) for q, k in zip(query, keys)]
            probs = [softmax_keys(s, allowed).astype(BF) for s in scores]
            probs_all[:, aligned(step * wider + i * count, count)] = jnp.concatenate(probs, axis=0)
        for copy in saves(step):
            copy.start()
        return 0

    lax.fori_loop(0, blocks // 2, rows, 0)
    for step in range(blocks // 2):
        for copy in saves(step):
            copy.wait()


def attn_scores(smem, streams, gain, inward, model, after):
    arrays, layout = gather_layout((streams,))
    segment = inward.shape[0] // 3
    own = Share(0, segment).own
    blocks = len(layout[0][0])
    count = arrays[0].shape[-1]
    total = blocks * count
    shapes = [(model, total), (3 * own, total), (own // HEAD_DIM * count, total)]
    layout = (layout, len(arrays))
    whole = len(smem) + len(arrays) + 2

    def run(*refs):
        attn_scores_kernel(layout, *refs[:whole], *refs[whole + len(after) :])

    any_spec, vmem_spec = pl.BlockSpec(memory_space=pl.ANY), pl.BlockSpec(memory_space=pltpu.VMEM)
    return pl.pallas_call(
        run,
        in_specs=[pl.BlockSpec(memory_space=pltpu.SMEM)] * len(smem)
        + [any_spec] * len(arrays)
        + [vmem_spec, any_spec]
        + [any_spec] * len(after),
        out_specs=[any_spec] * 3,
        out_shape=made_in_hbm([shape_of(s, BF) for s in shapes]),
        scratch_shapes=[pltpu.VMEM(s, BF) for s in shapes]
        + [
            pltpu.VMEM((3 * own, model), BF),
            pltpu.SemaphoreType.DMA((blocks,)),
            pltpu.SemaphoreType.DMA((3,)),
            pltpu.SemaphoreType.DMA((3, blocks // 2)),
        ],
        compiler_params=pltpu.CompilerParams(vmem_limit_bytes=24 * MIB),
        cost_estimate=time_of(14.0),
        name="attn_scores",
    )(*smem, *map(in_hbm, arrays), gain, in_hbm(inward), *map(in_hbm, after))


def attn_weights_kernel(layout, *refs):
    (grads, firsts), operands = layout
    pick_ref = refs[0]
    blocks_refs = refs[1 : 1 + operands]
    act_ref, proj_ref, probs_ref, mix_ref, add_ref, outward_ref, plain_ref = refs[1 + operands : 8 + operands]
    outs, scratch = refs[8 + operands : 13 + operands], refs[13 + operands :]
    act_all, grad_all, attn_all, dproj_all, outward, plain = scratch[:6]
    stage, low_stage, dots, out_stage, out_low, first_all, proj_all, probs_all = scratch[6:14]
    sems, weight_sems, kept_sems, out_sems = scratch[14:]
    core = pick_ref[1]
    share = Share(core, outward_ref.shape[0])
    width = share.own
    load = pltpu.make_async_copy(outward_ref.at[aligned(share.place, width), :], outward, weight_sems.at[0])
    load.start()
    fetch(pick_ref, blocks_refs, grads, grad_all, sems.at[0])
    fetch(pick_ref, blocks_refs, firsts, first_all, sems.at[1], share.place)
    blocks = len(grads[0])
    count = act_all.shape[1] // blocks
    wider = 2 * count

    def kept(step):
        here = aligned(step * wider, wider)
        for i, (source, target) in enumerate(((proj_ref, proj_all), (probs_ref, probs_all), (act_ref, act_all))):
            yield pltpu.make_async_copy(source.at[:, here], target.at[:, here], kept_sems.at[i, step])

    for step in range(blocks // 2):
        for copy in kept(step):
            copy.start()
    plain_copies = []
    for s in range(3):
        place = aligned(s * share.segment + share.place, width)
        here = slice(s * width, (s + 1) * width)
        plain_copies.append(
            pltpu.make_async_copy(plain_ref.at[:, place], plain.at[:, here], weight_sems.at[1 + s])
        )
    for copy in plain_copies:
        copy.start()
    load.wait()

    def rows(step, unused):
        for at in (2 * step, 2 * step + 1):
            arrived(blocks_refs, grads, grad_all, sems.at[0], at)
            arrived(blocks_refs, firsts, first_all, sems.at[1], at)
        for copy in kept(step):
            copy.wait()
        here = aligned(step * wider, wider)
        proj = proj_all[:, here]
        dattn = dot_nn(outward[...], grad_all[:, here]).astype(BF)
        first = first_all[:, here].astype(F32)
        mix = mix_ref[...]
        values = ((1.0 - mix) * proj[2 * width :].astype(F32) + mix * first).astype(BF)
        for i in range(2):
            cols = slice(i * count, (i + 1) * count)
            place = aligned(step * wider + i * count, count)
            probs = probs_all[:, place]
            dquery, dkeys, dmixed, attn = attend_back_from(
                proj[:width, cols],
                proj[width : 2 * width, cols],
                values[:, cols],
                dattn[:, cols],
                lambda: [probs[at : at + count] for at in range(0, probs.shape[0], count)],
                True,
            )
            dvalues = (1.0 - mix) * dmixed + add_ref[...] * first[:, cols]
            attn_all[:, place] = attn.astype(BF)
            dproj_all[:, place] = jnp.concatenate([dquery, dkeys, dvalues], axis=0).astype(BF)
        return 0

    lax.fori_loop(0, blocks // 2, rows, 0)
    for copy in plain_copies:
        copy.wait()
    copies = outward_products(share, attn_all, grad_all, (outs[1], outs[3], out_stage, out_low, out_sems.at[2]))
    copies += products(
        share, core, act_all, dproj_all, plain, (outs[0], outs[2], outs[4], stage, low_stage, dots, out_sems)
    )
    for copy in copies:
        copy.wait()


def gather_layout(sets):
    arrays, layout = [], []
    for choices in sets:
        placed = []
        for blocks in choices:
            row = []
            for array, index, first, where in blocks:
                at = next((i for i, a in enumerate(arrays) if a is array), None)
                if at is None:
                    at = len(arrays)
                    arrays.append(array)
                row.append((at, index, first, where))
            placed.append(tuple(row))
        layout.append(tuple(placed))
    return arrays, tuple(layout)


def weight_call(kernel, smem, sets, kept, small, weights, name, after=()):
    arrays, layout = gather_layout(sets)
    *turned_in, outward, plain = weights
    segment, model = outward.shape
    segments = plain.shape[1] // segment
    own = Share(0, segment).own
    blocks = len(layout[0][0])
    total = blocks * arrays[0].shape[-1]
    block = 256
    whole = len(smem) + len(arrays) + len(kept) + len(small) + len(weights)
    layout = (layout, len(arrays))

    def run(*refs):
        kernel(layout, *refs[:whole], *refs[whole + len(after) :])

    any_spec, vmem_spec = pl.BlockSpec(memory_space=pl.ANY), pl.BlockSpec(memory_space=pltpu.VMEM)
    scratch = [
        pltpu.VMEM((model, total), BF),
        pltpu.VMEM((model, total), BF),
        pltpu.VMEM((own, total), BF),
        pltpu.VMEM((segments * own, total), BF),
    ]
    scratch += [pltpu.VMEM((segments * own, model), BF)] * len(turned_in)
    scratch += [
        pltpu.VMEM((own, model), BF),
        pltpu.VMEM((model, segments * own), BF),
        pltpu.VMEM((2, model, block), F32),
        pltpu.VMEM((2, model, block), BF),
        pltpu.VMEM((model, 128), F32),
        pltpu.VMEM((own, model), F32),
        pltpu.VMEM((own, model), BF),
    ]
    if kept:
        scratch += [pltpu.VMEM((own, total), BF)] + [pltpu.VMEM(a.shape, BF) for a in kept[1:]]
    scratch += [
        pltpu.SemaphoreType.DMA((len(sets), blocks)),
        pltpu.SemaphoreType.DMA((2 * segments + 1,)),
    ]
    if kept:
        scratch += [pltpu.SemaphoreType.DMA((3, blocks // 2))]
    scratch += [pltpu.SemaphoreType.DMA((3, 3))]
    return pl.pallas_call(
        run,
        in_specs=[pl.BlockSpec(memory_space=pltpu.SMEM)] * len(smem)
        + [any_spec] * (len(arrays) + len(kept))
        + [vmem_spec] * len(small)
        + [any_spec] * (len(weights) + len(after)),
        out_specs=[any_spec] * 5,
        out_shape=made_in_hbm(
            [
                shape_of((1, model, segments * segment), F32),
                shape_of((1,) + outward.shape, F32),
                shape_of((model, segments * own), BF),
                shape_of((own, model), BF),
                shape_of((model, 128), F32),
            ]
        ),
        scratch_shapes=scratch,
        compiler_params=pltpu.CompilerParams(vmem_limit_bytes=56 * MIB),
        cost_estimate=time_of(27.0),
        name=name,
    )(*smem, *map(in_hbm, arrays), *map(in_hbm, kept), *small, *map(in_hbm, weights), *map(in_hbm, after))


def fill_kernel(segment, core_ref, low, out_low, unused_ref, unused_out_ref, *refs):
    whole_ref, whole_out_ref, stage, out_stage, sems = refs
    share = Share(core_ref[0], segment)
    own, other, size = share.own, share.other, stage.shape[1]
    segments = low.shape[1] // own
    writes = []
    for block in range(stage.shape[0]):
        rows = slice(block * size, (block + 1) * size)
        for s in range(segments):
            here = slice(s * other, (s + 1) * other)
            stage[block, :, here] = low[rows, aligned(s * own + share.other_source, other)].astype(F32)
            place = aligned(s * segment + share.other_place, other)
            copy = pltpu.make_async_copy(
                stage.at[block, :, here], whole_ref.at[0, rows, place], sems.at[block, s]
            )
            copy.start()
            writes.append(copy)
    out_stage[...] = out_low[aligned(share.other_source, other), :].astype(F32)
    copy = pltpu.make_async_copy(
        out_stage, whole_out_ref.at[0, aligned(share.other_place, other), :], sems.at[0, segments]
    )
    copy.start()
    for copy in writes + [copy]:
        copy.wait()


def filled(core, low, out_low, whole, whole_out, after=()):
    segment, model = whole_out.shape[1:]
    segments = whole.shape[2] // segment
    share = Share(0, segment)
    steps = 4
    any_spec = pl.BlockSpec(memory_space=pl.ANY)

    def run(*refs):
        fill_kernel(segment, *refs[:5], *refs[5 + len(after) :])

    return pl.pallas_call(
        run,
        in_specs=[pl.BlockSpec(memory_space=pltpu.SMEM)]
        + [pl.BlockSpec(memory_space=pltpu.VMEM)] * 2
        + [any_spec] * (2 + len(after)),
        out_specs=[any_spec] * 2,
        out_shape=made_in_hbm([whole, whole_out]),
        input_output_aliases={3: 0, 4: 1},
        scratch_shapes=[
            pltpu.VMEM((steps, model // steps, segments * share.other), F32),
            pltpu.VMEM((share.other, model), F32),
            pltpu.SemaphoreType.DMA((steps, segments + 1)),
        ],
        compiler_params=pltpu.CompilerParams(vmem_limit_bytes=32 * MIB),
        cost_estimate=time_of(5.0),
        name="fill",
    )(core, low, out_low, in_hbm(whole), in_hbm(whole_out), *map(in_hbm, after))


def body(tokens, cotangent, gains, attn_in, attn_out, ffn_in, ffn_out, mix_level, seq_lengths):
    section = lax.axis_index("section")
    core = lax.axis_index("dp") % 2
    lower = section < 2
    even = section % 2 == 0
    sections = lax.axis_size("section")
    dp = lax.axis_size("dp")
    group = min(dp, GROUP)
    planes = group // 2
    micro = seq_lengths.shape[0]
    count = tokens.shape[0] // micro
    piece = tokens.shape[1]
    inward, outward, feed_in, feed_out = attn_in[0], attn_out[0], ffn_in[0], ffn_out[0]
    model = inward.shape[0]
    width = outward.shape[0]

    low, high = (0, 1), (2, 3)
    everyone = low + high

    def send(x, mask, sources=everyone):
        return lax.ppermute(x, "section", [(i, i ^ mask) for i in sources])

    def planes_of(x, sources=everyone):
        def plane(by):
            pairs = [
                (s * dp + i, s * dp + i // group * group + (i % group // 2 + by) % planes * 2 + i % 2)
                for s in sources
                for i in range(dp)
            ]
            return lax.ppermute(x, ("section", "dp"), pairs)

        return [plane(by) for by in range(1, planes)]

    def other_core(x, sources=everyone):
        pairs = [(s * dp + i, s * dp + (i ^ 1)) for s in sources for i in range(dp)]
        return lax.ppermute(x, ("section", "dp"), pairs)

    near = jnp.where(lower, tokens, cotangent)
    far = jnp.where(lower, cotangent, tokens)
    got_far, got_across, got_near = send(far, 2), send(far, 3), send(near, 1)
    got_gains = send(gains, 1)
    ends = jnp.cumsum(seq_lengths, axis=1)
    ends = jnp.where(even, ends, ends[::-1])

    def by_half(mine, other):
        return [jnp.where(even, mine, other), jnp.where(even, other, mine)]

    ours, theirs = by_half(near, got_near), by_half(got_far, got_across)
    given = jnp.concatenate(
        [jnp.where(lower, a, b) for a, b in zip(ours + theirs, theirs + ours)], axis=1
    )
    top, bottom = given[:count], given[count:]
    given_own, given_mate = jnp.where(even, top, bottom), jnp.where(even, bottom, top)

    gain_attn = jnp.where(even, gains, got_gains)
    gain_feed = jnp.where(even, got_gains, gains)
    mix_all = jnp.repeat(mix_level.astype(F32) / 8.0, HEAD_DIM)
    mix_low, mix_high = mix_all[:width, None], mix_all[width:, None]
    mix = jnp.where(even, mix_low, mix_high)

    slot = shape_of((count, model), BF)
    half_turned = shape_of((width, count), BF)
    pair_half_turned = shape_of((2 * width, count), BF)
    slot_turned = shape_of((model, count), BF)
    pair_turned = shape_of((2, model, count), BF)
    pair_and_rows = shape_of((2, model + 16, count), BF)
    square_row = shape_of((1, count), F32)
    is_lower = lower.astype(jnp.int32)[None]

    attn_call = functools.partial(call, smem=1)
    part_mate, first_mate, square_mate = attn_call(
        attn_mate_kernel,
        [slot, half_turned, square_row],
        ends,
        given_mate,
        gain_attn,
        inward,
        outward,
        name="attn_mate",
    )
    got_own = send(part_mate, 1, low)
    part_own, first_both, square_own, given_stack = attn_call(
        attn_own_kernel,
        [slot, pair_half_turned, square_row, pair_and_rows],
        ends,
        given_own,
        gain_attn,
        inward,
        outward,
        given_mate,
        first_mate,
        name="attn_own",
    )
    got_mate = send(part_own, 1, low)
    first_over = send(first_both, 2, low)
    square0 = square_own, square_mate
    mid0_own, mid0_mate, mid0_stack, send_own, send_mate = call(
        feed_first_kernel,
        [slot, slot, pair_turned, slot, slot],
        given_own,
        given_mate,
        part_own,
        part_mate,
        got_own,
        got_mate,
        gain_feed,
        feed_in,
        feed_out,
        vmem=32,
        loads=(feed_in, feed_out),
        name="feed_first",
        after=(first_over,),
    )
    x_a, x_b = send(send_own, 2, low), send(send_mate, 3, low)
    feed_in_turned, inward_turned = call(
        turn_kernel,
        [shape_of(feed_in.shape[::-1], BF), shape_of(inward.shape[::-1], BF)],
        feed_in,
        inward,
        vmem=32,
        name="turn_weights",
        after=(send_own,),
    )

    x1_own = call(sum_kernel, [slot], x_a, x_b, name="sum", after=(inward_turned,))[0]
    x1_mate = send(x1_own, 1, high)

    def attn_mixed(which, x, out, *more):
        return attn_call(
            functools.partial(attn_mixed_kernel, which),
            [slot, out],
            ends,
            x,
            gain_attn,
            inward,
            outward,
            mix,
            first_over,
            *more,
            name="attn_mixed",
        )

    part_own, square_own = attn_mixed(0, x1_own, square_row)
    got_mate = send(part_own, 1, high)
    part_mate, middle_stack = attn_mixed(
        1,
        x1_mate,
        pair_and_rows,
        jnp.full((1, count), is_lower[0], jnp.int32),
        mid0_stack,
        x1_own,
        square_own,
        *square0,
    )
    got_own = send(part_mate, 1, high)
    def everywhere(x):
        groups = [list(range(at, at + group)) for at in range(0, dp, group)]
        return lax.all_gather(x, "dp", axis=0, axis_index_groups=groups)

    def gathered(stack):
        every = everywhere(stack)
        return every, [(every, (d, i), 0, None) for d in range(group) for i in range(2)]

    def own_gathered(own, after):
        same_core = [
            [at + 2 * z + c for z in range(planes)] for at in range(0, dp, group) for c in range(2)
        ]
        every = gate(lax.all_gather(own, "dp", axis=0, axis_index_groups=same_core), after)
        return every, send(every, 1)

    def own_blocks(every, mate):
        arrays = ((every, False, 0), (other_core(every), True, 0), (mate, False, 1), (other_core(mate), True, 1))
        return [(a, (z,), 0, (z, other, i)) for a, other, i in arrays for z in range(planes)]

    all_given, set_given = gathered(given_stack)
    all_middle, set_middle = gathered(middle_stack)
    part_own, part_mate, mid1_own, mid1_mate, mid1_turned, out_own, out_mate = call(
        feed_second_kernel,
        [slot, slot, slot, slot, slot_turned, slot, slot],
        x1_own,
        x1_mate,
        part_own,
        part_mate,
        got_own,
        got_mate,
        given_own,
        given_mate,
        gain_feed,
        feed_in,
        feed_out,
        vmem=36,
        loads=(feed_in, feed_out),
        name="feed_second",
        after=(all_given,),
    )
    got_own, got_mate = send(part_mate, 1, high), send(part_own, 1, high)
    middle1_own, middle1_mate, grad1_turned = call(
        middle_second_back_kernel,
        [slot, slot, pair_turned],
        mid1_own,
        mid1_mate,
        given_own,
        given_mate,
        part_own,
        part_mate,
        got_own,
        got_mate,
        gain_feed,
        name="middle_second_back",
    )

    def attn_back(which, grad, x, first, *mixed, after=()):
        outs = [slot] + [half_turned if which else pair_half_turned] * bool(mixed)
        return call(
            functools.partial(attn_back_kernel, bool(mixed), which),
            outs,
            ends,
            grad,
            x,
            gain_attn,
            inward,
            outward,
            first,
            *mixed,
            smem=1,
            name="attn_back",
            after=after,
        )

    part_mate, dfirst_mate = attn_back(1, middle1_mate, x1_mate, first_over, mix)
    got_own = send(part_mate, 1, high)
    part_own, dfirst_both = attn_back(0, middle1_own, x1_own, first_over, mix, dfirst_mate)
    dfirst = send(dfirst_both, 2, high)
    grad_x1 = call(
        input_back_kernel, [slot_turned], x1_own, middle1_own, part_own, got_own, gain_attn, name="input_back"
    )[0]
    grad_own, grad_mate = send(grad_x1, 2, high), send(grad_x1, 3, high)

    late = call(late_kernel, [slot_turned], is_lower, grad_own, mid1_turned, smem=1, name="late")[0]
    part_own, part_mate = call(
        feed_first_back_kernel,
        [slot, slot],
        mid0_own,
        mid0_mate,
        grad_own,
        grad_mate,
        gain_feed,
        feed_in,
        feed_out,
        vmem=36,
        loads=(feed_in, feed_out),
        name="feed_first_back",
        after=(late, all_middle),
    )
    got_own, got_mate = send(part_mate, 1, low), send(part_own, 1, low)
    middle_own, middle_mate, last = call(
        middle_first_back_kernel,
        [slot, slot, shape_of((2 * model + 2 * width, count), BF)],
        is_lower,
        mid0_own,
        mid0_mate,
        grad_own,
        grad_mate,
        part_own,
        part_mate,
        got_own,
        got_mate,
        gain_feed,
        grad1_turned,
        dfirst,
        first_over,
        smem=1,
        name="middle_first_back",
    )

    place = jnp.stack([section ^ mask for mask in range(sections)]).astype(jnp.int32)

    late_every, late_mate = own_gathered(late, [middle_own])
    part_mate = attn_back(1, middle_mate, given_mate, dfirst, after=(late_every,))[0]
    part_own = attn_back(0, middle_own, given_own, dfirst, after=(part_mate,))[0]

    all_ends = all_given[:, :, model, : ends.shape[1]].reshape(2 * group, -1).astype(jnp.int32)
    core_at = core.astype(jnp.int32)[None]
    pick = jnp.concatenate([1 - is_lower, core_at])
    squares = pl.pallas_call(
        square_sum_kernel,
        grid_spec=pltpu.PrefetchScalarGridSpec(
            num_scalar_prefetch=1,
            grid=(1,),
            in_specs=[pl.BlockSpec((group, 1, 16, count), lambda i, unused: (0, 0, model // 16, 0))],
            out_specs=pl.BlockSpec((1, 128), lambda i, unused: (0, 0)),
        ),
        out_shape=pltpu.HBM((1, 128), F32),
        compiler_params=pltpu.CompilerParams(vmem_limit_bytes=4 * MIB),
        name="square_sum",
    )(is_lower, in_hbm(all_middle))
    mine = Share(0, width).own

    def core_heads(column):
        return lax.dynamic_slice_in_dim(column, core * mine, mine, 0)

    pieces = call(
        split_kernel,
        [shape_of((4 * count + 16, piece), BF)] * sections,
        place,
        part_own,
        part_mate,
        out_own,
        out_mate,
        squares,
        smem=1,
        name="split",
    )
    scores = attn_scores(
        (pick, all_ends),
        (set_given, set_middle),
        gain_attn.reshape(model, 1),
        inward_turned,
        model,
        (late_every,),
    )
    set_late = own_blocks(late_every, gate(late_mate, [pieces[0], scores[2]]))
    all_last = everywhere(last)
    set_last = [(all_last, (d,), at, None) for d in range(group) for at in (0, model)]
    set_first = [(all_last, (d,), 2 * model + at, None) for d in range(group) for at in (0, width)]
    d_feed_in, d_feed_out, low_in, low_out, dots_feed = weight_call(
        feed_weights_kernel,
        (pick,),
        ((set_middle, set_late), (set_late, set_given)),
        (),
        (gain_feed.reshape(model, 1),),
        (feed_in_turned, feed_out, feed_in),
        "feed_weights",
        after=(pieces[0], scores[2]),
    )
    dinput, out, squares = call(
        join_kernel,
        [shape_of((2 * count, piece), F32), shape_of((2 * count, piece), BF), shape_of((1, 128), F32)],
        jnp.stack([lower, even]).astype(jnp.int32),
        pieces[0],
        *[send(pieces[mask], mask) for mask in range(1, sections)],
        smem=1,
        name="join",
        after=(low_in,),
    )
    if dp > group:
        squares = lax.psum(squares, "dp") / group
    norms = squares[0, :2] / (micro * count * dp * 2 * width)
    d_feed_in, d_feed_out = filled(core_at, other_core(low_in), other_core(low_out), d_feed_in, d_feed_out)
    d_in, d_out, low_in, low_out, dots_attn = weight_call(
        attn_weights_kernel,
        (pick,),
        ((set_last, set_last), (set_first, set_first)),
        scores,
        (
            core_heads(jnp.where(lower, 0.0, mix)),
            core_heads(jnp.where(lower, jnp.ones_like(mix), 0.0)),
        ),
        (outward, inward),
        "attn_weights",
        after=(dinput,),
    )
    d_in, d_out = filled(core_at, other_core(low_in), other_core(low_out), d_in, d_out, (d_feed_in,))

    dots_attn, dots_feed = jnp.sum(dots_attn, axis=1)[None], jnp.sum(dots_feed, axis=1)[None]
    mine, sent = jnp.where(even, dots_attn, dots_feed), jnp.where(even, dots_feed, dots_attn)
    d_gain = mine + send(sent, 1)
    d_gain = d_gain + other_core(d_gain)
    if dp > group:
        d_gain = lax.psum(d_gain, "dp") / group
        across = [list(range(at, dp, group)) for at in range(group)]
        d_in, d_out, d_feed_in, d_feed_out = [
            lax.psum(x.astype(BF), "dp", axis_index_groups=across).astype(F32)
            for x in (d_in, d_out, d_feed_in, d_feed_out)
        ]
    d_gain = d_gain / gains
    return (out, dinput, d_gain, d_in, d_out, d_feed_in, d_feed_out, norms[0], norms[1])


def solution(mesh):
    in_specs = (
        P("dp", "section"),
        P("dp", "section"),
        P("section", None),
        P("section", None, None),
        P("section", None, None),
        P("section", None, None),
        P("section", None, None),
        P(),
        P("dp", None),
    )
    out_specs = (
        P("dp", "section"),
        P("dp", "section"),
        P("section", None),
        P("section", None, None),
        P("section", None, None),
        P("section", None, None),
        P("section", None, None),
        P(),
        P(),
    )
    return jax.shard_map(body, mesh=mesh, in_specs=in_specs, out_specs=out_specs, check_vma=False)
```

```python
import functools

import jax
import jax.numpy as jnp
from jax import lax
from jax.experimental import pallas as pl
from jax.experimental.pallas import tpu as pltpu
from jax.sharding import PartitionSpec as P

HEAD_DIM = 64
EPS = 1e-05
NEG = -1e30
GROUP = 8
BF = jnp.bfloat16
F32 = jnp.float32
MIB = 1024 * 1024
WEIGHTS_FROM = 500_000


TIMES = {
    "turn_weights": 5.9,
    "attn_mate": 3.1,
    "attn_own": 3.5,
    "feed_first": 5.3,
    "sum": 1.8,
    "stack": 1.9,
    "attn_mixed": 3.3,
    "feed_second": 8.5,
    "middle_second_back": 3.1,
    "attn_back": 4.7,
    "input_back": 2.3,
    "late": 2.2,
    "feed_first_back": 6.8,
    "middle_first_back": 3.3,
    "split": 1.9,
    "join": 1.9,
    "add": 1.2,
}


def time_of(microseconds):
    return pl.CostEstimate(flops=int(microseconds * 1.15e9), bytes_accessed=1, transcendentals=0)


def dot_nn(left, right):
    return lax.dot_general(left, right, (((1,), (0,)), ((), ())), preferred_element_type=F32)


def dot_nt(left, right):
    return lax.dot_general(left, right, (((1,), (1,)), ((), ())), preferred_element_type=F32)


def dot_tn(left, right):
    return lax.dot_general(left, right, (((0,), (0,)), ((), ())), preferred_element_type=F32)


def shape_of(shape, dtype):
    return jax.ShapeDtypeStruct(shape, dtype)


def in_hbm(a):
    return pltpu.with_memory_space_constraint(a, pltpu.HBM)


def made_in_hbm(outs):
    return [pltpu.HBM(o.shape, o.dtype) for o in outs]


def normalize(stream, axis):
    rscale = lax.rsqrt(jnp.mean(stream * stream, axis=axis, keepdims=True) + EPS)
    return stream * rscale, rscale


def norm_back(stream, grad_out, dact, gain):
    normed, rscale = normalize(stream, -1)
    dnorm = dact * gain
    mean = jnp.mean(dnorm * normed, axis=-1, keepdims=True)
    return grad_out + rscale * (dnorm - normed * mean)


def column_of(row_ref):
    return jnp.broadcast_to(row_ref[...], (8, row_ref.shape[1])).T[:, 0:1]


def turned(rows):
    return rows.astype(F32).T.astype(BF)


def allowed_keys(ends, count):
    key = lax.broadcasted_iota(jnp.int32, (count, count), 0)
    query = lax.broadcasted_iota(jnp.int32, (count, count), 1)
    segment_key = sum((key >= end).astype(jnp.int32) for end in ends)
    segment_query = sum((query >= end).astype(jnp.int32) for end in ends)
    return (key <= query) & (segment_key == segment_query)


def heads_of(array, first=0):
    return [array[at : at + HEAD_DIM] for at in range(first, array.shape[0], HEAD_DIM)]


def softmax_keys(scores, allowed):
    scores = jnp.where(allowed, scores * HEAD_DIM**-0.5, NEG)
    exponent = jnp.exp(scores - jnp.max(scores, axis=0, keepdims=True))
    return exponent * (1.0 / jnp.sum(exponent, axis=0, keepdims=True))


def attend(query, keys, values, allowed):
    query, keys, values = heads_of(query), heads_of(keys), heads_of(values)
    scores = [dot_tn(k, q) for q, k in zip(query, keys)]
    probs = [softmax_keys(s, allowed).astype(BF) for s in scores]
    return jnp.concatenate([dot_nn(v, p) for v, p in zip(values, probs)], axis=0)


def attend_back(query, keys, values, dattn, allowed):
    scores = [dot_tn(k, q) for q, k in zip(heads_of(query), heads_of(keys))]
    return attend_back_from(query, keys, values, dattn, lambda: [softmax_keys(s, allowed) for s in scores], False)


def attend_back_from(query, keys, values, dattn, probs_of, forward):
    query, keys, values, dattn = [heads_of(a) for a in (query, keys, values, dattn)]
    dprobs = [dot_tn(v, d) for v, d in zip(values, dattn)]
    low_probs, dscores = [], []
    for probs, dprob in zip(probs_of(), dprobs):
        low_probs.append(probs.astype(BF))
        probs = probs.astype(F32)
        dscores.append((probs * (dprob - jnp.sum(dprob * probs, axis=0, keepdims=True))).astype(BF))
    attn = None
    if forward:
        attn = jnp.concatenate([dot_nn(v, p) for v, p in zip(values, low_probs)], axis=0)
    dquery = jnp.concatenate([dot_nn(k, d) for k, d in zip(keys, dscores)], axis=0) * HEAD_DIM**-0.5
    dkeys = jnp.concatenate([dot_nt(q, d) for q, d in zip(query, dscores)], axis=0) * HEAD_DIM**-0.5
    dmixed = jnp.concatenate([dot_nt(d, p) for d, p in zip(dattn, low_probs)], axis=0)
    return dquery, dkeys, dmixed, attn


def swish(gate, up):
    sigmoid = 1.0 / (1.0 + jnp.exp(-gate))
    return sigmoid, gate * sigmoid


def feed_back(gate, up, dhid):
    sigmoid, silu = swish(gate, up)
    hid = (silu * up).astype(BF)
    dgate = dhid * up * (sigmoid * (1.0 + gate * (1.0 - sigmoid)))
    dup = dhid * silu
    return hid, dgate.astype(BF), dup.astype(BF)


def ends_at(ends_ref, slot):
    return [ends_ref[slot, i] for i in range(ends_ref.shape[1])]


def rounded_sum(left, right):
    return left.astype(F32) + right.astype(F32)


def turn_kernel(a_ref, b_ref, a_out, b_out):
    size = 256
    row = lax.broadcasted_iota(jnp.int32, (size, size), 0)
    col = lax.broadcasted_iota(jnp.int32, (size, size), 1)
    identity = jnp.where(row == col, 1.0, 0.0).astype(BF)
    for source, target in ((a_ref, a_out), (b_ref, b_out)):
        for at in range(0, source.shape[1], size):
            target[at : at + size, :] = dot_nt(identity, source[:, at : at + size]).astype(BF)


def attend_forward(slot, ends_ref, x, gain_ref, inward_ref, mix, first):
    width = inward_ref.shape[1] // 3
    normed, unused = normalize(x.astype(F32), -1)
    act = (normed * gain_ref[...]).astype(BF)
    proj = dot_nn(act, inward_ref[...]).T.astype(BF)
    values = proj[2 * width :]
    if mix is not None:
        values = ((1.0 - mix) * values.astype(F32) + mix * first.astype(F32)).astype(BF)
    wide = values.astype(F32)
    square = jnp.sum(wide * wide, axis=0, keepdims=True)
    allowed = allowed_keys(ends_at(ends_ref, slot), x.shape[0])
    attn = attend(proj[:width], proj[width : 2 * width], values, allowed)
    return attn.T.astype(BF), values, square


def ends_rows(ends_ref, slot, shape):
    lane = lax.broadcasted_iota(jnp.int32, shape, 1)
    ends = ends_at(ends_ref, slot)
    return sum(jnp.where(lane == i, end, 0) for i, end in enumerate(ends)).astype(F32).astype(BF)


def square_rows(square, rows):
    parts = []
    for unused in range(3):
        parts.append(square.astype(BF).astype(F32))
        square = square - parts[-1]
    return jnp.concatenate(parts + [jnp.zeros((rows - 3, square.shape[1]), F32)], axis=0).astype(BF)


def attn_mate_kernel(ends_ref, x_ref, gain_ref, inward_ref, outward_ref, part_ref, values_ref, square_ref):
    attn, values, square = attend_forward(1, ends_ref, x_ref[...], gain_ref, inward_ref, None, None)
    values_ref[...] = values
    square_ref[...] = square
    part_ref[...] = dot_nn(attn, outward_ref[...]).astype(BF)


def attn_own_kernel(
    ends_ref,
    x_ref,
    gain_ref,
    inward_ref,
    outward_ref,
    mate_ref,
    values_mate_ref,
    part_ref,
    values_ref,
    square_ref,
    turned_ref,
):
    model = x_ref.shape[1]
    width = outward_ref.shape[0]
    attn, values, square = attend_forward(0, ends_ref, x_ref[...], gain_ref, inward_ref, None, None)
    part_ref[...] = dot_nn(attn, outward_ref[...]).astype(BF)
    values_ref[:width] = values
    values_ref[width:] = values_mate_ref[...]
    square_ref[...] = square
    for slot, ref in enumerate((x_ref, mate_ref)):
        turned_ref[slot, :model] = turned(ref[...])
        turned_ref[slot, model:] = ends_rows(ends_ref, slot, (turned_ref.shape[1] - model, turned_ref.shape[2]))


def attn_mixed_kernel(slot, ends_ref, x_ref, gain_ref, inward_ref, outward_ref, mix_ref, first_ref, *refs):
    part_ref, square_ref = refs[-2:]
    width = outward_ref.shape[0]
    attn, unused, square = attend_forward(
        slot,
        ends_ref,
        x_ref[...],
        gain_ref,
        inward_ref,
        mix_ref[...],
        first_ref[slot * width : (slot + 1) * width],
    )
    part_ref[...] = dot_nn(attn, outward_ref[...]).astype(BF)
    if slot == 0:
        square_ref[...] = square
        return
    lower_ref, low_ref, own_ref, square_own_ref, square_low_own, square_low_mate = refs[:6]
    stack_ref = square_ref
    model = x_ref.shape[1]
    is_lower = lower_ref[0, 0] == 1
    square = jnp.where(is_lower, square_low_own[...] + square_low_mate[...], square + square_own_ref[...])
    rows = square_rows(square, stack_ref.shape[1] - model)
    stack_ref[0, model:] = rows
    stack_ref[1, model:] = jnp.zeros_like(rows)
    stack_ref[0, :model] = jnp.where(is_lower, low_ref[0], turned(own_ref[...]))
    stack_ref[1, :model] = jnp.where(is_lower, low_ref[1], turned(x_ref[...]))


def sum_kernel(a_ref, b_ref, out_ref):
    out_ref[...] = rounded_sum(a_ref[...], b_ref[...]).astype(BF)


def attn_sums(refs):
    own_ref, mate_ref, part_own_ref, part_mate_ref, got_own_ref, got_mate_ref = refs
    own = (own_ref[...].astype(F32) + rounded_sum(part_own_ref[...], got_own_ref[...])).astype(BF)
    mate = (mate_ref[...].astype(F32) + rounded_sum(part_mate_ref[...], got_mate_ref[...])).astype(BF)
    return own, mate


def feed_loads(inward_ref, outward_ref, inward, outward, sems):
    hidden = outward.shape[0]
    copies = [
        pltpu.make_async_copy(inward_ref.at[:, 0:hidden], inward.at[:, 0:hidden], sems.at[0]),
        pltpu.make_async_copy(inward_ref.at[:, hidden : 2 * hidden], inward.at[:, hidden : 2 * hidden], sems.at[1]),
        pltpu.make_async_copy(outward_ref, outward, sems.at[2]),
    ]
    for copy in copies:
        copy.start()
    return copies


def feed_first_kernel(*refs):
    gain_ref, inward_hbm, outward_hbm = refs[6:9]
    mid_own_ref, mid_mate_ref, stack_ref, send_own_ref, send_mate_ref = refs[9:14]
    inward_ref, outward_ref, sems = refs[14:]
    loads = feed_loads(inward_hbm, outward_hbm, inward_ref, outward_ref, sems)
    own, mate = attn_sums(refs[:6])
    count = own.shape[0]
    mid_own_ref[...] = own
    mid_mate_ref[...] = mate
    stack_ref[0] = turned(own)
    stack_ref[1] = turned(mate)
    stream = jnp.concatenate([own, mate], axis=0).astype(F32)
    normed, unused = normalize(stream, -1)
    act = (normed * gain_ref[...]).astype(BF)
    hidden = outward_ref.shape[0]
    loads[0].wait()
    gate = dot_nn(act, inward_ref[:, :hidden])
    loads[1].wait()
    up = dot_nn(act, inward_ref[:, hidden:])
    unused, silu = swish(gate, up)
    loads[2].wait()
    part = dot_nn((silu * up).astype(BF), outward_ref[...])
    send_own_ref[...] = (stream[:count] + part[:count]).astype(BF)
    send_mate_ref[...] = part[count:].astype(BF)


def feed_second_kernel(*refs):
    grad_own_ref, grad_mate_ref, gain_ref, inward_hbm, outward_hbm = refs[6:11]
    part_own_ref, part_mate_ref, mid_own_ref, mid_mate_ref, turned_ref, out_own_ref, out_mate_ref = refs[11:18]
    inward_ref, outward_ref, sems = refs[18:]
    loads = feed_loads(inward_hbm, outward_hbm, inward_ref, outward_ref, sems)
    own, mate = attn_sums(refs[:6])
    count = own.shape[0]
    mid_own_ref[...] = own
    mid_mate_ref[...] = mate
    turned_ref[...] = turned(own)
    stream = jnp.concatenate([own, mate], axis=0).astype(F32)
    grad = jnp.concatenate([grad_own_ref[...], grad_mate_ref[...]], axis=0)
    normed, unused = normalize(stream, -1)
    act = (normed * gain_ref[...]).astype(BF)
    hidden = outward_ref.shape[0]
    loads[0].wait()
    gate = dot_nn(act, inward_ref[:, :hidden])
    loads[1].wait()
    up = dot_nn(act, inward_ref[:, hidden:])
    loads[2].wait()
    dhid = dot_nt(grad, outward_ref[...])
    hid, dgate, dup = feed_back(gate, up, dhid)
    dact = dot_nt(dgate, inward_ref[:, :hidden]) + dot_nt(dup, inward_ref[:, hidden:])
    part_own_ref[...] = dact[:count].astype(BF)
    part_mate_ref[...] = dact[count:].astype(BF)
    part = dot_nn(hid, outward_ref[...])
    out_own_ref[...] = (stream[:count] + part[:count]).astype(BF)
    out_mate_ref[...] = part[count:].astype(BF)


def feed_first_back_kernel(
    own_ref,
    mate_ref,
    grad_own_ref,
    grad_mate_ref,
    gain_ref,
    inward_hbm,
    outward_hbm,
    part_own_ref,
    part_mate_ref,
    inward_ref,
    outward_ref,
    sems,
):
    loads = feed_loads(inward_hbm, outward_hbm, inward_ref, outward_ref, sems)
    count = own_ref.shape[0]
    stream = jnp.concatenate([own_ref[...], mate_ref[...]], axis=0).astype(F32)
    grad = jnp.concatenate([turned(grad_own_ref[...]), turned(grad_mate_ref[...])], axis=0)
    normed, unused = normalize(stream, -1)
    act = (normed * gain_ref[...]).astype(BF)
    hidden = outward_ref.shape[0]
    loads[0].wait()
    gate = dot_nn(act, inward_ref[:, :hidden])
    loads[1].wait()
    up = dot_nn(act, inward_ref[:, hidden:])
    loads[2].wait()
    dhid = dot_nt(grad, outward_ref[...])
    unused, dgate, dup = feed_back(gate, up, dhid)
    dact = dot_nt(dgate, inward_ref[:, :hidden]) + dot_nt(dup, inward_ref[:, hidden:])
    part_own_ref[...] = dact[:count].astype(BF)
    part_mate_ref[...] = dact[count:].astype(BF)


def middle_grads(refs, gain_ref, turned_grads):
    for s_ref, g_ref, p_ref, r_ref in zip(*refs):
        grad = g_ref[...].astype(F32)
        grad = norm_back(
            s_ref[...].astype(F32),
            grad.T if turned_grads else grad,
            rounded_sum(p_ref[...], r_ref[...]),
            gain_ref[...],
        )
        yield grad.astype(BF)


def middle_first_back_kernel(lower_ref, *refs):
    gain_ref, grad_high_ref, dfirst_ref, first_ref = refs[8:12]
    out_own_ref, out_mate_ref, last_ref = refs[12:]
    pairs = refs[0:2], refs[2:4], refs[4:6], refs[6:8]
    own, mate = middle_grads(pairs, gain_ref, True)
    out_own_ref[...] = own
    out_mate_ref[...] = mate
    model = own.shape[1]
    is_lower = lower_ref[0] == 1
    last_ref[:model] = jnp.where(is_lower, turned(own), grad_high_ref[0])
    last_ref[model : 2 * model] = jnp.where(is_lower, turned(mate), grad_high_ref[1])
    last_ref[2 * model :] = jnp.where(is_lower, dfirst_ref[...], first_ref[...])


def middle_second_back_kernel(*refs):
    gain_ref, out_own_ref, out_mate_ref, turned_ref = refs[8:]
    pairs = refs[0:2], refs[2:4], refs[4:6], refs[6:8]
    own, mate = middle_grads(pairs, gain_ref, False)
    out_own_ref[...] = own
    out_mate_ref[...] = mate
    turned_ref[0] = turned(own)
    turned_ref[1] = turned(mate)


def attn_back_kernel(mixing, slot, *refs):
    ends_ref, grad_ref, x_ref, gain_ref, inward_ref, outward_ref, first_ref = refs[:7]
    count = x_ref.shape[0]
    width = outward_ref.shape[0]
    first = first_ref[slot * width : (slot + 1) * width].astype(F32)
    normed, unused = normalize(x_ref[...].astype(F32), -1)
    act = (normed * gain_ref[...]).astype(BF)
    allowed = allowed_keys(ends_at(ends_ref, slot), count)
    dattn = dot_nt(grad_ref[...], outward_ref[...]).T.astype(BF)
    proj = dot_nn(act, inward_ref[...]).T.astype(BF)
    values = proj[2 * width :]
    if mixing:
        mix = refs[7][...]
        values = ((1.0 - mix) * values.astype(F32) + mix * first).astype(BF)
    dquery, dkeys, dmixed, unused = attend_back(proj[:width], proj[width : 2 * width], values, dattn, allowed)
    if mixing:
        dfirst = (mix * dmixed).astype(BF)
        dvalues = (1.0 - mix) * dmixed
        if slot == 1:
            refs[-1][...] = dfirst
        else:
            refs[-1][:width] = dfirst
            refs[-1][width:] = refs[8][...]
    else:
        dvalues = dmixed + first
    dproj = jnp.concatenate([dquery, dkeys, dvalues], axis=0).T.astype(BF)
    dact = dot_nt(dproj, inward_ref[...])
    if mixing:
        refs[-2][...] = dact.astype(BF)
    else:
        grad = 0.0 if slot else grad_ref[...].astype(F32)
        refs[-1][...] = norm_back(x_ref[...].astype(F32), grad, dact, gain_ref[...]).astype(BF)


def input_back_kernel(x_ref, grad_ref, part_ref, got_ref, gain_ref, out_ref):
    grad = norm_back(
        x_ref[...].astype(F32),
        grad_ref[...].astype(F32),
        rounded_sum(part_ref[...], got_ref[...]),
        gain_ref[...],
    )
    out_ref[...] = grad.T.astype(BF)


def split_kernel(place_ref, a_own_ref, a_mate_ref, b_own_ref, b_mate_ref, row_ref, *refs):
    count, piece = a_own_ref.shape[0], refs[0].shape[1]
    for mask, ref in enumerate(refs):
        columns = aligned(place_ref[mask] * piece, piece)
        for i, source in enumerate((a_own_ref, a_mate_ref, b_own_ref, b_mate_ref)):
            ref[i * count : (i + 1) * count] = source[:, columns]
        row = jnp.concatenate([row_ref[...], jnp.zeros((1, piece - row_ref.shape[1]), F32)], axis=1)
        ref[4 * count :] = square_rows(row, ref.shape[0] - 4 * count)


def join_kernel(flags_ref, own_ref, beside_ref, over_ref, across_ref, a_ref, b_ref, row_ref):
    count = a_ref.shape[0] // 2
    lower, even = flags_ref[0] == 1, flags_ref[1] == 1
    for first, out_ref, holds in ((0, a_ref, lower), (2 * count, b_ref, jnp.logical_not(lower))):
        rows = slice(first, first + 2 * count)
        same = jnp.where(holds, own_ref[rows], over_ref[rows]).astype(F32)
        other = jnp.where(holds, beside_ref[rows], across_ref[rows]).astype(F32)
        own, mate = same[:count] + other[count:], same[count:] + other[:count]
        out_ref[:count] = jnp.where(even, own, mate).astype(out_ref.dtype)
        out_ref[count:] = jnp.where(even, mate, own).astype(out_ref.dtype)
    lanes = row_ref.shape[1]
    rows = [r[4 * count :, :lanes].astype(F32) for r in (own_ref, beside_ref, over_ref, across_ref)]
    row_ref[...] = jnp.sum(sum(rows), axis=0, keepdims=True)


def late_kernel(lower_ref, low_ref, high_ref, out_ref):
    out_ref[...] = jnp.where(lower_ref[0] == 1, low_ref[...], high_ref[...])


def square_sum_kernel(lower_ref, rows_ref, out_ref):
    total = jnp.sum(rows_ref[...].astype(F32))
    lane = lax.broadcasted_iota(jnp.int32, out_ref.shape, 1)
    out_ref[...] = jnp.where(lane == 1 - lower_ref[0], total, 0.0)


def add_kernel(a_ref, b_ref, out_ref):
    out_ref[...] = a_ref[...] + b_ref[...]


def call(kernel, outs, *args, smem=0, name=None, after=(), vmem=16, loads=(), free=()):
    whole = len(args)
    held = {id(w) for w in loads}
    either = {id(a) for a in free}

    def run(*refs):
        kernel(*refs[:whole], *refs[whole + len(after) :])

    def whole_block(a):
        return pl.BlockSpec(a.shape, lambda i: (0,) * len(a.shape))

    def given_spec(a):
        if id(a) in held:
            return pl.BlockSpec(memory_space=pl.ANY)
        return pl.BlockSpec(memory_space=pltpu.VMEM) if a.size >= WEIGHTS_FROM else whole_block(a)

    return pl.pallas_call(
        run,
        grid=(1,),
        out_shape=made_in_hbm(outs),
        in_specs=[pl.BlockSpec(memory_space=pltpu.SMEM)] * smem
        + [given_spec(a) for a in args[smem:]]
        + [pl.BlockSpec(memory_space=pl.ANY)] * len(after),
        out_specs=[whole_block(o) for o in outs],
        scratch_shapes=[pltpu.VMEM(w.shape, w.dtype) for w in loads]
        + [pltpu.SemaphoreType.DMA((1 + len(loads),))] * bool(loads),
        compiler_params=pltpu.CompilerParams(vmem_limit_bytes=vmem * MIB),
        cost_estimate=time_of(TIMES.get(name, 1.0)),
        name=name,
    )(*args[:smem], *[a if id(a) in either or a.size >= WEIGHTS_FROM and id(a) not in held else in_hbm(a) for a in args[smem:]], *[a if id(a) in either else in_hbm(a) for a in after])


def gate(array, after):
    spec = pl.BlockSpec(memory_space=pl.ANY)
    return pl.pallas_call(
        lambda *refs: None,
        out_shape=pltpu.HBM(array.shape, array.dtype),
        in_specs=[spec] * (1 + len(after)),
        out_specs=spec,
        input_output_aliases={0: 0},
        compiler_params=pltpu.CompilerParams(vmem_limit_bytes=MIB),
        cost_estimate=time_of(0.1),
        name="gate",
    )(in_hbm(array), *map(in_hbm, after))


class Share:
    def __init__(self, core, segment):
        self.segment = segment
        self.own = -(-segment // 256) * 128
        self.other = segment - self.own
        self.common = 2 * self.own - segment
        self.place = core * (segment - self.own)
        self.other_source = (1 - core) * self.common
        self.other_place = (1 - core) * self.own


def aligned(start, size, unit=128):
    return pl.ds(pl.multiple_of(start, unit), size)


def block_ref(refs, block, rows, shift=0):
    operand, index, first = block[:3]
    ref = refs[operand]
    for i in index:
        ref = ref.at[i]
    return ref.at[aligned(first + shift, rows), :]


def fetch(pick_ref, refs, choices, target, sems, shift=0):
    for which, blocks in enumerate(choices):

        @pl.when(pick_ref[0] == which)
        def _():
            for at, block in enumerate(blocks):
                source = block_ref(refs, block, target.shape[0], shift)
                count = source.shape[1]
                if block[3] is not None:
                    plane, other, slot = block[3]
                    core = 1 - pick_ref[1] if other else pick_ref[1]
                    at = (2 * plane + core) * 2 + slot
                columns = aligned(at * count, count)
                pltpu.make_async_copy(source, target.at[:, columns], sems.at[at]).start()


def arrived(refs, choices, target, sems, at):
    source = block_ref(refs, choices[0][0], target.shape[0])
    count = source.shape[1]
    pltpu.make_async_copy(source, target.at[:, aligned(at * count, count)], sems.at[at]).wait()


def weight_copies(share, inward_ref, outward_ref, plain_ref, inward, outward, plain, sems):
    own = share.own
    first, last = [(outward_ref.at[aligned(share.place, own), :], outward)], []
    for s in range(inward.shape[0] // own):
        place = aligned(s * share.segment + share.place, own)
        here = slice(s * own, (s + 1) * own)
        first.append((inward_ref.at[place, :], inward.at[here, :]))
        last.append((plain_ref.at[:, place], plain.at[:, here]))
    copies = [pltpu.make_async_copy(a, b, sems.at[i]) for i, (a, b) in enumerate(first + last)]
    return copies[: len(first)], copies[len(first) :]


def products(share, core, left, right, plain, refs):
    whole_ref, low_ref, dots_ref, stage, low_stage, dots, dots_row, sems = refs
    size, lanes = stage.shape[2], dots.shape[1]
    each = share.own // size
    steps = right.shape[0] // size

    def copies(step, slot):
        place = lax.div(step, each) * share.segment + share.place + lax.rem(step, each) * size
        columns = aligned(place, size)
        yield pltpu.make_async_copy(stage.at[slot], whole_ref.at[0, :, columns], sems.at[slot, 0])
        yield pltpu.make_async_copy(low_stage.at[slot], low_ref.at[:, aligned(step * size, size)], sems.at[slot, 1])

    dots[...] = jnp.zeros_like(dots)

    def one(step, unused):
        slot = lax.rem(step, 2)
        here = aligned(step * size, size)

        @pl.when(step >= 2)
        def _():
            for copy in copies(step, slot):
                copy.wait()

        value = dot_nt(left[...], right[here, :])
        stage[slot] = value
        low_stage[slot] = value.astype(BF)
        value = value * plain[:, here].astype(F32)
        total = 0.0
        for at in range(0, size, lanes):
            part = value[:, at : at + lanes]
            if at < share.common:
                part = jnp.where((core == 0) | (lax.rem(step, each) > 0), part, 0.0)
            total = total + part
        dots[...] += total
        for copy in copies(step, slot):
            copy.start()
        return 0

    lax.fori_loop(0, steps, one, 0)
    dots_row[...] = jnp.sum(dots[...].T, axis=0, keepdims=True)
    save = pltpu.make_async_copy(dots_row, dots_ref, sems.at[0, 2])
    save.start()
    return [save] + [copy for step in range(max(steps - 2, 0), steps) for copy in copies(step, step % 2)]


def outward_products(share, left, right, refs):
    whole_ref, low_ref, stage, low_stage, sems = refs
    value = dot_nt(left[...], right[...])
    stage[...] = value
    low_stage[...] = value.astype(BF)
    copies = [
        pltpu.make_async_copy(stage, whole_ref.at[0, aligned(share.place, share.own), :], sems.at[0]),
        pltpu.make_async_copy(low_stage, low_ref, sems.at[1]),
    ]
    for copy in copies:
        copy.start()
    return copies


def feed_weights_kernel(layout, *refs):
    (streams, grads), operands = layout
    pick_ref = refs[0]
    blocks_refs = refs[1 : 1 + operands]
    gain_ref, inward_ref, outward_ref, plain_ref = refs[1 + operands : 5 + operands]
    outs, scratch = refs[5 + operands : 10 + operands], refs[10 + operands :]
    act_all, grad_all, hid_all, dboth_all, inward, outward, plain = scratch[:7]
    stage, low_stage, dots, dots_row, out_stage, out_low, sems, weight_sems, out_sems = scratch[7:]
    core = pick_ref[1]
    share = Share(core, outward_ref.shape[0])
    hidden = share.own
    weights, plain_copies = weight_copies(
        share, inward_ref, outward_ref, plain_ref, inward, outward, plain, weight_sems
    )
    for copy in weights:
        copy.start()
    for copy in weights:
        copy.wait()
    fetch(pick_ref, blocks_refs, streams, act_all, sems.at[0])
    fetch(pick_ref, blocks_refs, grads, grad_all, sems.at[1])
    for copy in plain_copies:
        copy.start()
    blocks = len(streams[0])
    wider = 2 * (act_all.shape[1] // blocks)

    gain = column_of(gain_ref)

    def rows(step, unused):
        for at in (2 * step, 2 * step + 1):
            arrived(blocks_refs, streams, act_all, sems.at[0], at)
            arrived(blocks_refs, grads, grad_all, sems.at[1], at)
        here = aligned(step * wider, wider)
        normed, unused = normalize(act_all[:, here].astype(F32), 0)
        act = (normed * gain).astype(BF)
        act_all[:, here] = act
        both = dot_nn(inward[...], act)
        dhid = dot_nn(outward[...], grad_all[:, here])
        hid, dgate, dup = feed_back(both[:hidden], both[hidden:], dhid)
        hid_all[:, here] = hid
        dboth_all[:hidden, here] = dgate
        dboth_all[hidden:, here] = dup
        return 0

    lax.fori_loop(0, blocks // 2, rows, 0)
    for copy in plain_copies:
        copy.wait()
    copies = outward_products(share, hid_all, grad_all, (outs[1], outs[3], out_stage, out_low, out_sems.at[2]))
    copies += products(
        share, core, act_all, dboth_all, plain, (outs[0], outs[2], outs[4], stage, low_stage, dots, dots_row, out_sems)
    )
    for copy in copies:
        copy.wait()


def attn_scores_kernel(layout, *refs):
    (streams,), operands = layout
    pick_ref, ends_ref = refs[:2]
    blocks_refs = refs[2 : 2 + operands]
    gain_ref, inward_ref = refs[2 + operands : 4 + operands]
    outs, scratch = refs[4 + operands : 7 + operands], refs[7 + operands :]
    act_all, proj_all, probs_all, inward, sems, weight_sems, out_sems = scratch
    own = inward.shape[0] // 3
    share = Share(pick_ref[1], inward_ref.shape[0] // 3)
    copies = []
    for s in range(3):
        place = aligned(s * share.segment + share.place, own)
        copies.append(
            pltpu.make_async_copy(inward_ref.at[place, :], inward.at[s * own : (s + 1) * own, :], weight_sems.at[s])
        )
    for copy in copies:
        copy.start()
    for copy in copies:
        copy.wait()
    fetch(pick_ref, blocks_refs, streams, act_all, sems)
    blocks = len(streams[0])
    count = act_all.shape[1] // blocks
    wider = 2 * count

    def saves(step):
        here = aligned(step * wider, wider)
        for i, (source, target) in enumerate(zip((act_all, proj_all, probs_all), outs)):
            yield pltpu.make_async_copy(source.at[:, here], target.at[:, here], out_sems.at[i, step])

    gain = column_of(gain_ref)

    def rows(step, unused):
        for at in (2 * step, 2 * step + 1):
            arrived(blocks_refs, streams, act_all, sems, at)
        here = aligned(step * wider, wider)
        normed, unused = normalize(act_all[:, here].astype(F32), 0)
        act = (normed * gain).astype(BF)
        act_all[:, here] = act
        proj = dot_nn(inward[...], act).astype(BF)
        proj_all[:, here] = proj
        for i in range(2):
            cols = slice(i * count, (i + 1) * count)
            allowed = allowed_keys(ends_at(ends_ref, step * 2 + i), count)
            query, keys = heads_of(proj[:own, cols]), heads_of(proj[own : 2 * own, cols])
            scores = [dot_tn(k, q) for q, k in zip(query, keys)]
            probs = [softmax_keys(s, allowed).astype(BF) for s in scores]
            probs_all[:, aligned(step * wider + i * count, count)] = jnp.concatenate(probs, axis=0)
        for copy in saves(step):
            copy.start()
        return 0

    lax.fori_loop(0, blocks // 2, rows, 0)
    for step in range(blocks // 2):
        for copy in saves(step):
            copy.wait()


def attn_scores(smem, streams, gain, inward, model, after):
    arrays, layout = gather_layout((streams,))
    segment = inward.shape[0] // 3
    own = Share(0, segment).own
    blocks = len(layout[0][0])
    count = arrays[0].shape[-1]
    total = blocks * count
    shapes = [(model, total), (3 * own, total), (own // HEAD_DIM * count, total)]
    layout = (layout, len(arrays))
    whole = len(smem) + len(arrays) + 2

    def run(*refs):
        attn_scores_kernel(layout, *refs[:whole], *refs[whole + len(after) :])

    any_spec, vmem_spec = pl.BlockSpec(memory_space=pl.ANY), pl.BlockSpec(memory_space=pltpu.VMEM)
    return pl.pallas_call(
        run,
        in_specs=[pl.BlockSpec(memory_space=pltpu.SMEM)] * len(smem)
        + [any_spec] * len(arrays)
        + [vmem_spec, any_spec]
        + [any_spec] * len(after),
        out_specs=[any_spec] * 3,
        out_shape=made_in_hbm([shape_of(s, BF) for s in shapes]),
        scratch_shapes=[pltpu.VMEM(s, BF) for s in shapes]
        + [
            pltpu.VMEM((3 * own, model), BF),
            pltpu.SemaphoreType.DMA((blocks,)),
            pltpu.SemaphoreType.DMA((3,)),
            pltpu.SemaphoreType.DMA((3, blocks // 2)),
        ],
        compiler_params=pltpu.CompilerParams(vmem_limit_bytes=24 * MIB),
        cost_estimate=time_of(14.0),
        name="attn_scores",
    )(*smem, *map(in_hbm, arrays), gain, in_hbm(inward), *map(in_hbm, after))


def attn_weights_kernel(layout, *refs):
    (grads, firsts), operands = layout
    pick_ref, level_ref = refs[:2]
    blocks_refs = refs[2 : 2 + operands]
    act_ref, proj_ref, probs_ref, outward_ref, plain_ref = refs[2 + operands : 7 + operands]
    outs, scratch = refs[7 + operands : 12 + operands], refs[12 + operands :]
    act_all, grad_all, attn_all, dproj_all, outward, plain = scratch[:6]
    stage, low_stage, dots, dots_row, out_stage, out_low, first_all, proj_all, probs_all = scratch[6:15]
    sems, weight_sems, kept_sems, out_sems = scratch[15:]
    core = pick_ref[1]
    share = Share(core, outward_ref.shape[0])
    width = share.own
    load = pltpu.make_async_copy(outward_ref.at[aligned(share.place, width), :], outward, weight_sems.at[0])
    load.start()
    fetch(pick_ref, blocks_refs, grads, grad_all, sems.at[0])
    fetch(pick_ref, blocks_refs, firsts, first_all, sems.at[1], share.place)
    blocks = len(grads[0])
    count = act_all.shape[1] // blocks
    wider = 2 * count

    def kept(step):
        here = aligned(step * wider, wider)
        for i, (source, target) in enumerate(((proj_ref, proj_all), (probs_ref, probs_all), (act_ref, act_all))):
            yield pltpu.make_async_copy(source.at[:, here], target.at[:, here], kept_sems.at[i, step])

    for step in range(blocks // 2):
        for copy in kept(step):
            copy.start()
    plain_copies = []
    for s in range(3):
        place = aligned(s * share.segment + share.place, width)
        here = slice(s * width, (s + 1) * width)
        plain_copies.append(
            pltpu.make_async_copy(plain_ref.at[:, place], plain.at[:, here], weight_sems.at[1 + s])
        )
    for copy in plain_copies:
        copy.start()
    load.wait()

    upper = pick_ref[0].astype(F32)
    heads = width // HEAD_DIM
    first_head = pick_ref[3] * (share.segment // HEAD_DIM) + core * (share.segment - width) // HEAD_DIM
    levels = [level_ref[first_head + i].astype(F32) / 8.0 * upper for i in range(heads)]
    mix = jnp.concatenate([jnp.full((HEAD_DIM, 1), level, F32) for level in levels], axis=0)

    def rows(step, unused):
        for at in (2 * step, 2 * step + 1):
            arrived(blocks_refs, grads, grad_all, sems.at[0], at)
            arrived(blocks_refs, firsts, first_all, sems.at[1], at)
        for copy in kept(step):
            copy.wait()
        here = aligned(step * wider, wider)
        proj = proj_all[:, here]
        dattn = dot_nn(outward[...], grad_all[:, here]).astype(BF)
        first = first_all[:, here].astype(F32)
        values = ((1.0 - mix) * proj[2 * width :].astype(F32) + mix * first).astype(BF)
        for i in range(2):
            cols = slice(i * count, (i + 1) * count)
            place = aligned(step * wider + i * count, count)
            probs = probs_all[:, place]
            dquery, dkeys, dmixed, attn = attend_back_from(
                proj[:width, cols],
                proj[width : 2 * width, cols],
                values[:, cols],
                dattn[:, cols],
                lambda: [probs[at : at + count] for at in range(0, probs.shape[0], count)],
                True,
            )
            dvalues = (1.0 - mix) * dmixed + (1.0 - upper) * first[:, cols]
            attn_all[:, place] = attn.astype(BF)
            dproj_all[:, place] = jnp.concatenate([dquery, dkeys, dvalues], axis=0).astype(BF)
        return 0

    lax.fori_loop(0, blocks // 2, rows, 0)
    for copy in plain_copies:
        copy.wait()
    copies = outward_products(share, attn_all, grad_all, (outs[1], outs[3], out_stage, out_low, out_sems.at[2]))
    copies += products(
        share, core, act_all, dproj_all, plain, (outs[0], outs[2], outs[4], stage, low_stage, dots, dots_row, out_sems)
    )
    for copy in copies:
        copy.wait()


def gather_layout(sets):
    arrays, layout = [], []
    for choices in sets:
        placed = []
        for blocks in choices:
            row = []
            for array, index, first, where in blocks:
                at = next((i for i, a in enumerate(arrays) if a is array), None)
                if at is None:
                    at = len(arrays)
                    arrays.append(array)
                row.append((at, index, first, where))
            placed.append(tuple(row))
        layout.append(tuple(placed))
    return arrays, tuple(layout)


def weight_call(kernel, smem, sets, kept, small, weights, name, after=()):
    arrays, layout = gather_layout(sets)
    *turned_in, outward, plain = weights
    segment, model = outward.shape
    segments = plain.shape[1] // segment
    own = Share(0, segment).own
    blocks = len(layout[0][0])
    total = blocks * arrays[0].shape[-1]
    block = 256
    whole = len(smem) + len(arrays) + len(kept) + len(small) + len(weights)
    layout = (layout, len(arrays))

    def run(*refs):
        kernel(layout, *refs[:whole], *refs[whole + len(after) :])

    any_spec, vmem_spec = pl.BlockSpec(memory_space=pl.ANY), pl.BlockSpec(memory_space=pltpu.VMEM)
    scratch = [
        pltpu.VMEM((model, total), BF),
        pltpu.VMEM((model, total), BF),
        pltpu.VMEM((own, total), BF),
        pltpu.VMEM((segments * own, total), BF),
    ]
    scratch += [pltpu.VMEM((segments * own, model), BF)] * len(turned_in)
    scratch += [
        pltpu.VMEM((own, model), BF),
        pltpu.VMEM((model, segments * own), BF),
        pltpu.VMEM((2, model, block), F32),
        pltpu.VMEM((2, model, block), BF),
        pltpu.VMEM((model, 128), F32),
        pltpu.VMEM((1, model), F32),
        pltpu.VMEM((own, model), F32),
        pltpu.VMEM((own, model), BF),
    ]
    if kept:
        scratch += [pltpu.VMEM((own, total), BF)] + [pltpu.VMEM(a.shape, BF) for a in kept[1:]]
    scratch += [
        pltpu.SemaphoreType.DMA((len(sets), blocks)),
        pltpu.SemaphoreType.DMA((2 * segments + 1,)),
    ]
    if kept:
        scratch += [pltpu.SemaphoreType.DMA((3, blocks // 2))]
    scratch += [pltpu.SemaphoreType.DMA((3, 3))]
    return pl.pallas_call(
        run,
        in_specs=[pl.BlockSpec(memory_space=pltpu.SMEM)] * len(smem)
        + [any_spec] * (len(arrays) + len(kept))
        + [vmem_spec] * len(small)
        + [any_spec] * (len(weights) + len(after)),
        out_specs=[any_spec] * 5,
        out_shape=made_in_hbm(
            [
                shape_of((1, model, segments * segment), F32),
                shape_of((1,) + outward.shape, F32),
                shape_of((model, segments * own), BF),
                shape_of((own, model), BF),
                shape_of((1, model), F32),
            ]
        ),
        scratch_shapes=scratch,
        compiler_params=pltpu.CompilerParams(vmem_limit_bytes=56 * MIB),
        cost_estimate=time_of(27.0),
        name=name,
    )(*smem, *map(in_hbm, arrays), *map(in_hbm, kept), *small, *map(in_hbm, weights), *map(in_hbm, after))


def fill_kernel(segment, core_ref, low, out_low, unused_ref, unused_out_ref, *refs):
    whole_ref, whole_out_ref, stage, out_stage, sems = refs
    share = Share(core_ref[0], segment)
    own, other, size = share.own, share.other, stage.shape[1]
    segments = low.shape[1] // own
    writes = []
    for block in range(stage.shape[0]):
        rows = slice(block * size, (block + 1) * size)
        for s in range(segments):
            here = slice(s * other, (s + 1) * other)
            stage[block, :, here] = low[rows, aligned(s * own + share.other_source, other)].astype(F32)
            place = aligned(s * segment + share.other_place, other)
            copy = pltpu.make_async_copy(
                stage.at[block, :, here], whole_ref.at[0, rows, place], sems.at[block, s]
            )
            copy.start()
            writes.append(copy)
    out_stage[...] = out_low[aligned(share.other_source, other), :].astype(F32)
    copy = pltpu.make_async_copy(
        out_stage, whole_out_ref.at[0, aligned(share.other_place, other), :], sems.at[0, segments]
    )
    copy.start()
    for copy in writes + [copy]:
        copy.wait()


def filled(core, low, out_low, whole, whole_out, after=()):
    segment, model = whole_out.shape[1:]
    segments = whole.shape[2] // segment
    share = Share(0, segment)
    steps = 4
    any_spec = pl.BlockSpec(memory_space=pl.ANY)

    def run(*refs):
        fill_kernel(segment, *refs[:5], *refs[5 + len(after) :])

    return pl.pallas_call(
        run,
        in_specs=[pl.BlockSpec(memory_space=pltpu.SMEM)]
        + [pl.BlockSpec(memory_space=pltpu.VMEM)] * 2
        + [any_spec] * (2 + len(after)),
        out_specs=[any_spec] * 2,
        out_shape=made_in_hbm([whole, whole_out]),
        input_output_aliases={3: 0, 4: 1},
        scratch_shapes=[
            pltpu.VMEM((steps, model // steps, segments * share.other), F32),
            pltpu.VMEM((share.other, model), F32),
            pltpu.SemaphoreType.DMA((steps, segments + 1)),
        ],
        compiler_params=pltpu.CompilerParams(vmem_limit_bytes=32 * MIB),
        cost_estimate=time_of(5.0),
        name="fill",
    )(core, low, out_low, in_hbm(whole), in_hbm(whole_out), *map(in_hbm, after))


def body(tokens, cotangent, gains, attn_in, attn_out, ffn_in, ffn_out, mix_level, seq_lengths):
    section = lax.axis_index("section")
    core = lax.axis_index("dp") % 2
    lower = section < 2
    even = section % 2 == 0
    sections = lax.axis_size("section")
    dp = lax.axis_size("dp")
    group = min(dp, GROUP)
    planes = group // 2
    micro = seq_lengths.shape[0]
    count = tokens.shape[0] // micro
    piece = tokens.shape[1]
    inward, outward, feed_in, feed_out = attn_in[0], attn_out[0], ffn_in[0], ffn_out[0]
    model = inward.shape[0]
    width = outward.shape[0]

    low, high = (0, 1), (2, 3)
    everyone = low + high

    def send(x, mask, sources=everyone):
        return lax.ppermute(x, "section", [(i, i ^ mask) for i in sources])

    def planes_of(x, sources=everyone):
        def plane(by):
            pairs = [
                (s * dp + i, s * dp + i // group * group + (i % group // 2 + by) % planes * 2 + i % 2)
                for s in sources
                for i in range(dp)
            ]
            return lax.ppermute(x, ("section", "dp"), pairs)

        return [plane(by) for by in range(1, planes)]

    def other_core(x, sources=everyone):
        pairs = [(s * dp + i, s * dp + (i ^ 1)) for s in sources for i in range(dp)]
        return lax.ppermute(x, ("section", "dp"), pairs)

    near = jnp.where(lower, tokens, cotangent)
    far = jnp.where(lower, cotangent, tokens)
    got_far, got_across, got_near = send(far, 2), send(far, 3), send(near, 1)
    got_gains = send(gains, 1)
    ends = jnp.cumsum(seq_lengths, axis=1)
    ends = jnp.where(even, ends, ends[::-1])

    def by_half(mine, other):
        return [jnp.where(even, mine, other), jnp.where(even, other, mine)]

    ours, theirs = by_half(near, got_near), by_half(got_far, got_across)
    given = jnp.concatenate(
        [jnp.where(lower, a, b) for a, b in zip(ours + theirs, theirs + ours)], axis=1
    )
    top, bottom = given[:count], given[count:]
    given_own, given_mate = jnp.where(even, top, bottom), jnp.where(even, bottom, top)

    gain_attn = jnp.where(even, gains, got_gains)
    gain_feed = jnp.where(even, got_gains, gains)
    mix_all = jnp.repeat(mix_level.astype(F32) / 8.0, HEAD_DIM)
    mix_low, mix_high = mix_all[:width, None], mix_all[width:, None]
    mix = jnp.where(even, mix_low, mix_high)

    slot = shape_of((count, model), BF)
    half_turned = shape_of((width, count), BF)
    pair_half_turned = shape_of((2 * width, count), BF)
    slot_turned = shape_of((model, count), BF)
    pair_turned = shape_of((2, model, count), BF)
    pair_and_rows = shape_of((2, model + 16, count), BF)
    square_row = shape_of((1, count), F32)
    is_lower = lower.astype(jnp.int32)[None]

    attn_call = functools.partial(call, smem=1)
    part_mate, first_mate, square_mate = attn_call(
        attn_mate_kernel,
        [slot, half_turned, square_row],
        ends,
        given_mate,
        gain_attn,
        inward,
        outward,
        name="attn_mate",
    )
    got_own = send(part_mate, 1, low)
    part_own, first_both, square_own, given_stack = attn_call(
        attn_own_kernel,
        [slot, pair_half_turned, square_row, pair_and_rows],
        ends,
        given_own,
        gain_attn,
        inward,
        outward,
        given_mate,
        first_mate,
        name="attn_own",
    )
    got_mate = send(part_own, 1, low)
    first_over = send(first_both, 2, low)
    square0 = square_own, square_mate
    mid0_own, mid0_mate, mid0_stack, send_own, send_mate = call(
        feed_first_kernel,
        [slot, slot, pair_turned, slot, slot],
        given_own,
        given_mate,
        part_own,
        part_mate,
        got_own,
        got_mate,
        gain_feed,
        feed_in,
        feed_out,
        vmem=32,
        loads=(feed_in, feed_out),
        free=(first_over,),
        name="feed_first",
        after=(first_over,),
    )
    x_a, x_b = send(send_own, 2, low), send(send_mate, 3, low)
    feed_in_turned, inward_turned = call(
        turn_kernel,
        [shape_of(feed_in.shape[::-1], BF), shape_of(inward.shape[::-1], BF)],
        feed_in,
        inward,
        vmem=32,
        name="turn_weights",
        after=(send_own,),
    )

    x1_own = call(sum_kernel, [slot], x_a, x_b, name="sum", after=(inward_turned,), free=(x_a, x_b))[0]
    x1_mate = send(x1_own, 1, high)

    def attn_mixed(which, x, out, *more):
        return attn_call(
            functools.partial(attn_mixed_kernel, which),
            [slot, out],
            ends,
            x,
            gain_attn,
            inward,
            outward,
            mix,
            first_over,
            *more,
            name="attn_mixed",
            free=(first_over,),
        )

    part_own, square_own = attn_mixed(0, x1_own, square_row)
    got_mate = send(part_own, 1, high)
    part_mate, middle_stack = attn_mixed(
        1,
        x1_mate,
        pair_and_rows,
        jnp.full((1, count), is_lower[0], jnp.int32),
        mid0_stack,
        x1_own,
        square_own,
        *square0,
    )
    got_own = send(part_mate, 1, high)
    def everywhere(x):
        groups = [list(range(at, at + group)) for at in range(0, dp, group)]
        return lax.all_gather(x, "dp", axis=0, axis_index_groups=groups)

    def gathered(stack):
        every = everywhere(stack)
        return every, [(every, (d, i), 0, None) for d in range(group) for i in range(2)]

    def own_gathered(own, after):
        same_core = [
            [at + 2 * z + c for z in range(planes)] for at in range(0, dp, group) for c in range(2)
        ]
        every = gate(lax.all_gather(own, "dp", axis=0, axis_index_groups=same_core), after)
        return every, send(every, 1)

    def own_blocks(every, mate):
        arrays = ((every, False, 0), (other_core(every), True, 0), (mate, False, 1), (other_core(mate), True, 1))
        return [(a, (z,), 0, (z, other, i)) for a, other, i in arrays for z in range(planes)]

    all_given, set_given = gathered(given_stack)
    all_middle, set_middle = gathered(middle_stack)
    part_own, part_mate, mid1_own, mid1_mate, mid1_turned, out_own, out_mate = call(
        feed_second_kernel,
        [slot, slot, slot, slot, slot_turned, slot, slot],
        x1_own,
        x1_mate,
        part_own,
        part_mate,
        got_own,
        got_mate,
        given_own,
        given_mate,
        gain_feed,
        feed_in,
        feed_out,
        vmem=36,
        loads=(feed_in, feed_out),
        name="feed_second",
        after=(all_given,),
    )
    got_own, got_mate = send(part_mate, 1, high), send(part_own, 1, high)
    middle1_own, middle1_mate, grad1_turned = call(
        middle_second_back_kernel,
        [slot, slot, pair_turned],
        mid1_own,
        mid1_mate,
        given_own,
        given_mate,
        part_own,
        part_mate,
        got_own,
        got_mate,
        gain_feed,
        free=(got_own, got_mate),
        name="middle_second_back",
    )

    def attn_back(which, grad, x, first, *mixed, after=()):
        outs = [slot] + [half_turned if which else pair_half_turned] * bool(mixed)
        return call(
            functools.partial(attn_back_kernel, bool(mixed), which),
            outs,
            ends,
            grad,
            x,
            gain_attn,
            inward,
            outward,
            first,
            *mixed,
            smem=1,
            name="attn_back",
            after=after,
            free=(first,),
        )

    part_mate, dfirst_mate = attn_back(1, middle1_mate, x1_mate, first_over, mix)
    got_own = send(part_mate, 1, high)
    part_own, dfirst_both = attn_back(0, middle1_own, x1_own, first_over, mix, dfirst_mate)
    dfirst = send(dfirst_both, 2, high)
    grad_x1 = call(
        input_back_kernel,
        [slot_turned],
        x1_own,
        middle1_own,
        part_own,
        got_own,
        gain_attn,
        name="input_back",
        free=(got_own,),
    )[0]
    grad_own, grad_mate = send(grad_x1, 2, high), send(grad_x1, 3, high)

    received = (grad_own, grad_mate, dfirst)
    late = call(
        late_kernel, [slot_turned], is_lower, grad_own, mid1_turned, smem=1, name="late", free=received
    )[0]
    part_own, part_mate = call(
        feed_first_back_kernel,
        [slot, slot],
        mid0_own,
        mid0_mate,
        grad_own,
        grad_mate,
        gain_feed,
        feed_in,
        feed_out,
        vmem=36,
        loads=(feed_in, feed_out),
        free=received,
        name="feed_first_back",
        after=(late, all_middle),
    )
    got_own, got_mate = send(part_mate, 1, low), send(part_own, 1, low)
    middle_own, middle_mate, last = call(
        middle_first_back_kernel,
        [slot, slot, shape_of((2 * model + 2 * width, count), BF)],
        is_lower,
        mid0_own,
        mid0_mate,
        grad_own,
        grad_mate,
        part_own,
        part_mate,
        got_own,
        got_mate,
        gain_feed,
        grad1_turned,
        dfirst,
        first_over,
        smem=1,
        free=(got_own, got_mate) + received,
        name="middle_first_back",
    )

    place = jnp.stack([section ^ mask for mask in range(sections)]).astype(jnp.int32)

    late_every, late_mate = own_gathered(late, [middle_own])
    part_mate = attn_back(1, middle_mate, given_mate, dfirst, after=(late_every,))[0]
    part_own = attn_back(0, middle_own, given_own, dfirst, after=(part_mate,))[0]

    all_ends = all_given[:, :, model, : ends.shape[1]].reshape(2 * group, -1).astype(jnp.int32)
    core_at = core.astype(jnp.int32)[None]
    half = (section % 2).astype(jnp.int32)[None]
    pick = jnp.concatenate([1 - is_lower, core_at, core_at, half])
    squares = pl.pallas_call(
        square_sum_kernel,
        grid_spec=pltpu.PrefetchScalarGridSpec(
            num_scalar_prefetch=1,
            grid=(1,),
            in_specs=[pl.BlockSpec((group, 1, 16, count), lambda i, unused: (0, 0, model // 16, 0))],
            out_specs=pl.BlockSpec((1, 128), lambda i, unused: (0, 0)),
        ),
        out_shape=pltpu.HBM((1, 128), F32),
        compiler_params=pltpu.CompilerParams(vmem_limit_bytes=4 * MIB),
        name="square_sum",
    )(is_lower, in_hbm(all_middle))

    pieces = call(
        split_kernel,
        [shape_of((4 * count + 16, piece), BF)] * sections,
        place,
        part_own,
        part_mate,
        out_own,
        out_mate,
        squares,
        smem=1,
        name="split",
    )
    scores = attn_scores(
        (pick, all_ends),
        (set_given, set_middle),
        gain_attn,
        inward_turned,
        model,
        (late_every,),
    )
    set_late = own_blocks(late_every, gate(late_mate, [pieces[0], scores[2]]))
    all_last = everywhere(last)
    set_last = [(all_last, (d,), at, None) for d in range(group) for at in (0, model)]
    set_first = [(all_last, (d,), 2 * model + at, None) for d in range(group) for at in (0, width)]
    d_feed_in, d_feed_out, low_in, low_out, dots_feed = weight_call(
        feed_weights_kernel,
        (pick,),
        ((set_middle, set_late), (set_late, set_given)),
        (),
        (gain_feed,),
        (feed_in_turned, feed_out, feed_in),
        "feed_weights",
        after=(pieces[0], scores[2]),
    )
    received = [send(pieces[mask], mask) for mask in range(1, sections)]
    dinput, out, squares = call(
        join_kernel,
        [shape_of((2 * count, piece), F32), shape_of((2 * count, piece), BF), shape_of((1, 128), F32)],
        jnp.stack([lower, even]).astype(jnp.int32),
        pieces[0],
        *received,
        smem=1,
        name="join",
        free=received,
        after=(low_in,),
    )
    if dp > group:
        squares = lax.psum(squares, "dp") / group
    norms = squares[0, :2] / (micro * count * dp * 2 * width)
    d_feed_in, d_feed_out = filled(core_at, other_core(low_in), other_core(low_out), d_feed_in, d_feed_out)
    d_in, d_out, low_in, low_out, dots_attn = weight_call(
        attn_weights_kernel,
        (pick, mix_level),
        ((set_last, set_last), (set_first, set_first)),
        scores,
        (),
        (outward, inward),
        "attn_weights",
        after=(dinput,),
    )
    d_in, d_out = filled(core_at, other_core(low_in), other_core(low_out), d_in, d_out, (d_feed_in,))

    mine, sent = jnp.where(even, dots_attn, dots_feed), jnp.where(even, dots_feed, dots_attn)
    both = [(s * dp + i, (s ^ 1) * dp + (i ^ 1)) for s in range(sections) for i in range(dp)]
    d_gain = mine + send(sent, 1) + other_core(mine) + lax.ppermute(sent, ("section", "dp"), both)
    if dp > group:
        d_gain = lax.psum(d_gain, "dp") / group
        across = [list(range(at, dp, group)) for at in range(group)]
        d_in, d_out, d_feed_in, d_feed_out = [
            lax.psum(x.astype(BF), "dp", axis_index_groups=across).astype(F32)
            for x in (d_in, d_out, d_feed_in, d_feed_out)
        ]
    d_gain = d_gain / gains
    return (out, dinput, d_gain, d_in, d_out, d_feed_in, d_feed_out, norms[0], norms[1])


def solution(mesh):
    in_specs = (
        P("dp", "section"),
        P("dp", "section"),
        P("section", None),
        P("section", None, None),
        P("section", None, None),
        P("section", None, None),
        P("section", None, None),
        P(),
        P("dp", None),
    )
    out_specs = (
        P("dp", "section"),
        P("dp", "section"),
        P("section", None),
        P("section", None, None),
        P("section", None, None),
        P("section", None, None),
        P("section", None, None),
        P(),
        P(),
    )
    return jax.shard_map(body, mesh=mesh, in_specs=in_specs, out_specs=out_specs, check_vma=False)
```

```python
import functools

import jax
import jax.numpy as jnp
from jax import lax
from jax.experimental import pallas as pl
from jax.experimental.pallas import tpu as pltpu
from jax.sharding import PartitionSpec as P

HEAD_DIM = 64
EPS = 1e-05
NEG = -1e30
GROUP = 8
BF = jnp.bfloat16
F32 = jnp.float32
MIB = 1024 * 1024
WEIGHTS_FROM = 500_000


TIMES = {
    "turn_weights": 5.9,
    "attn_mate": 3.1,
    "attn_own": 3.5,
    "feed_first": 5.3,
    "sum": 1.8,
    "stack": 1.9,
    "attn_mixed": 3.3,
    "feed_second": 8.5,
    "middle_second_back": 3.1,
    "attn_back": 4.7,
    "input_back": 2.3,
    "late": 2.2,
    "feed_first_back": 6.8,
    "middle_first_back": 3.3,
    "split": 1.9,
    "join": 1.9,
    "add": 1.2,
}


def time_of(microseconds):
    return pl.CostEstimate(flops=int(microseconds * 1.15e9), bytes_accessed=1, transcendentals=0)


def dot_nn(left, right):
    return lax.dot_general(left, right, (((1,), (0,)), ((), ())), preferred_element_type=F32)


def dot_nt(left, right):
    return lax.dot_general(left, right, (((1,), (1,)), ((), ())), preferred_element_type=F32)


def dot_tn(left, right):
    return lax.dot_general(left, right, (((0,), (0,)), ((), ())), preferred_element_type=F32)


def shape_of(shape, dtype):
    return jax.ShapeDtypeStruct(shape, dtype)


def in_hbm(a):
    return pltpu.with_memory_space_constraint(a, pltpu.HBM)


def made_in_hbm(outs):
    return [pltpu.HBM(o.shape, o.dtype) for o in outs]


def normalize(stream, axis):
    rscale = lax.rsqrt(jnp.mean(stream * stream, axis=axis, keepdims=True) + EPS)
    return stream * rscale, rscale


def norm_back(stream, grad_out, dact, gain):
    normed, rscale = normalize(stream, -1)
    dnorm = dact * gain
    mean = jnp.mean(dnorm * normed, axis=-1, keepdims=True)
    return grad_out + rscale * (dnorm - normed * mean)


def column_of(row_ref):
    return jnp.broadcast_to(row_ref[...], (8, row_ref.shape[1])).T[:, 0:1]


def turned(rows):
    return rows.astype(F32).T.astype(BF)


def allowed_keys(ends, count):
    key = lax.broadcasted_iota(jnp.int32, (count, count), 0)
    query = lax.broadcasted_iota(jnp.int32, (count, count), 1)
    segment_key = sum((key >= end).astype(jnp.int32) for end in ends)
    segment_query = sum((query >= end).astype(jnp.int32) for end in ends)
    return (key <= query) & (segment_key == segment_query)


def heads_of(array, first=0):
    return [array[at : at + HEAD_DIM] for at in range(first, array.shape[0], HEAD_DIM)]


def softmax_keys(scores, allowed):
    scores = jnp.where(allowed, scores * HEAD_DIM**-0.5, NEG)
    exponent = jnp.exp(scores - jnp.max(scores, axis=0, keepdims=True))
    return exponent * (1.0 / jnp.sum(exponent, axis=0, keepdims=True))


def attend(query, keys, values, allowed):
    query, keys, values = heads_of(query), heads_of(keys), heads_of(values)
    scores = [dot_tn(k, q) for q, k in zip(query, keys)]
    probs = [softmax_keys(s, allowed).astype(BF) for s in scores]
    return jnp.concatenate([dot_nn(v, p) for v, p in zip(values, probs)], axis=0)


def attend_back(query, keys, values, dattn, allowed):
    scores = [dot_tn(k, q) for q, k in zip(heads_of(query), heads_of(keys))]
    return attend_back_from(query, keys, values, dattn, lambda: [softmax_keys(s, allowed) for s in scores], False)


def attend_back_from(query, keys, values, dattn, probs_of, forward):
    query, keys, values, dattn = [heads_of(a) for a in (query, keys, values, dattn)]
    dprobs = [dot_tn(v, d) for v, d in zip(values, dattn)]
    low_probs, dscores = [], []
    for probs, dprob in zip(probs_of(), dprobs):
        low_probs.append(probs.astype(BF))
        probs = probs.astype(F32)
        dscores.append((probs * (dprob - jnp.sum(dprob * probs, axis=0, keepdims=True))).astype(BF))
    attn = None
    if forward:
        attn = jnp.concatenate([dot_nn(v, p) for v, p in zip(values, low_probs)], axis=0)
    dquery = jnp.concatenate([dot_nn(k, d) for k, d in zip(keys, dscores)], axis=0) * HEAD_DIM**-0.5
    dkeys = jnp.concatenate([dot_nt(q, d) for q, d in zip(query, dscores)], axis=0) * HEAD_DIM**-0.5
    dmixed = jnp.concatenate([dot_nt(d, p) for d, p in zip(dattn, low_probs)], axis=0)
    return dquery, dkeys, dmixed, attn


def swish(gate, up):
    sigmoid = 1.0 / (1.0 + jnp.exp(-gate))
    return sigmoid, gate * sigmoid


def feed_back(gate, up, dhid):
    sigmoid, silu = swish(gate, up)
    hid = (silu * up).astype(BF)
    dgate = dhid * up * (sigmoid * (1.0 + gate * (1.0 - sigmoid)))
    dup = dhid * silu
    return hid, dgate.astype(BF), dup.astype(BF)


def ends_at(ends_ref, slot):
    return [ends_ref[slot, i] for i in range(ends_ref.shape[1])]


def rounded_sum(left, right):
    return left.astype(F32) + right.astype(F32)


def turn_kernel(a_ref, b_ref, a_out, b_out):
    size = 256
    row = lax.broadcasted_iota(jnp.int32, (size, size), 0)
    col = lax.broadcasted_iota(jnp.int32, (size, size), 1)
    identity = jnp.where(row == col, 1.0, 0.0).astype(BF)
    for source, target in ((a_ref, a_out), (b_ref, b_out)):
        for at in range(0, source.shape[1], size):
            target[at : at + size, :] = dot_nt(identity, source[:, at : at + size]).astype(BF)


def attend_forward(slot, ends_ref, x, gain_ref, inward_ref, mix, first):
    width = inward_ref.shape[1] // 3
    normed, unused = normalize(x.astype(F32), -1)
    act = (normed * gain_ref[...]).astype(BF)
    proj = dot_nn(act, inward_ref[...]).T.astype(BF)
    values = proj[2 * width :]
    if mix is not None:
        values = ((1.0 - mix) * values.astype(F32) + mix * first.astype(F32)).astype(BF)
    wide = values.astype(F32)
    square = jnp.sum(wide * wide, axis=0, keepdims=True)
    allowed = allowed_keys(ends_at(ends_ref, slot), x.shape[0])
    attn = attend(proj[:width], proj[width : 2 * width], values, allowed)
    return attn.T.astype(BF), values, square


def ends_rows(ends_ref, slot, shape):
    lane = lax.broadcasted_iota(jnp.int32, shape, 1)
    ends = ends_at(ends_ref, slot)
    return sum(jnp.where(lane == i, end, 0) for i, end in enumerate(ends)).astype(F32).astype(BF)


def square_rows(square, rows):
    parts = []
    for unused in range(3):
        parts.append(square.astype(BF).astype(F32))
        square = square - parts[-1]
    return jnp.concatenate(parts + [jnp.zeros((rows - 3, square.shape[1]), F32)], axis=0).astype(BF)


def attn_mate_kernel(ends_ref, x_ref, gain_ref, inward_ref, outward_ref, part_ref, values_ref, square_ref):
    attn, values, square = attend_forward(1, ends_ref, x_ref[...], gain_ref, inward_ref, None, None)
    values_ref[...] = values
    square_ref[...] = square
    part_ref[...] = dot_nn(attn, outward_ref[...]).astype(BF)


def attn_own_kernel(
    ends_ref,
    x_ref,
    gain_ref,
    inward_ref,
    outward_ref,
    mate_ref,
    values_mate_ref,
    part_ref,
    values_ref,
    square_ref,
    turned_ref,
):
    model = x_ref.shape[1]
    width = outward_ref.shape[0]
    attn, values, square = attend_forward(0, ends_ref, x_ref[...], gain_ref, inward_ref, None, None)
    part_ref[...] = dot_nn(attn, outward_ref[...]).astype(BF)
    values_ref[:width] = values
    values_ref[width:] = values_mate_ref[...]
    square_ref[...] = square
    for slot, ref in enumerate((x_ref, mate_ref)):
        turned_ref[slot, :model] = turned(ref[...])
        turned_ref[slot, model:] = ends_rows(ends_ref, slot, (turned_ref.shape[1] - model, turned_ref.shape[2]))


def attn_mixed_kernel(slot, ends_ref, x_ref, gain_ref, inward_ref, outward_ref, mix_ref, first_ref, *refs):
    part_ref, square_ref = refs[-2:]
    width = outward_ref.shape[0]
    attn, unused, square = attend_forward(
        slot,
        ends_ref,
        x_ref[...],
        gain_ref,
        inward_ref,
        mix_ref[...],
        first_ref[slot * width : (slot + 1) * width],
    )
    part_ref[...] = dot_nn(attn, outward_ref[...]).astype(BF)
    if slot == 0:
        square_ref[...] = square
        return
    lower_ref, low_ref, own_ref, square_own_ref, square_low_own, square_low_mate = refs[:6]
    stack_ref = square_ref
    model = x_ref.shape[1]
    is_lower = lower_ref[0, 0] == 1
    square = jnp.where(is_lower, square_low_own[...] + square_low_mate[...], square + square_own_ref[...])
    rows = square_rows(square, stack_ref.shape[1] - model)
    stack_ref[0, model:] = rows
    stack_ref[1, model:] = jnp.zeros_like(rows)
    stack_ref[0, :model] = jnp.where(is_lower, low_ref[0], turned(own_ref[...]))
    stack_ref[1, :model] = jnp.where(is_lower, low_ref[1], turned(x_ref[...]))


def sum_kernel(a_ref, b_ref, out_ref):
    out_ref[...] = rounded_sum(a_ref[...], b_ref[...]).astype(BF)


def attn_sums(refs):
    own_ref, mate_ref, part_own_ref, part_mate_ref, got_own_ref, got_mate_ref = refs
    own = (own_ref[...].astype(F32) + rounded_sum(part_own_ref[...], got_own_ref[...])).astype(BF)
    mate = (mate_ref[...].astype(F32) + rounded_sum(part_mate_ref[...], got_mate_ref[...])).astype(BF)
    return own, mate


def feed_loads(inward_ref, outward_ref, inward, outward, sems):
    hidden = outward.shape[0]
    copies = [
        pltpu.make_async_copy(inward_ref.at[:, 0:hidden], inward.at[:, 0:hidden], sems.at[0]),
        pltpu.make_async_copy(inward_ref.at[:, hidden : 2 * hidden], inward.at[:, hidden : 2 * hidden], sems.at[1]),
        pltpu.make_async_copy(outward_ref, outward, sems.at[2]),
    ]
    for copy in copies:
        copy.start()
    return copies


def prefetch_kernel(a_ref, b_ref, *refs):
    a_out, b_out, sems = refs[-3:]
    copies = [
        pltpu.make_async_copy(a_ref, a_out, sems.at[0]),
        pltpu.make_async_copy(b_ref, b_out, sems.at[1]),
    ]
    for copy in copies:
        copy.start()
    for copy in copies:
        copy.wait()


def prefetched(a, b, after):
    any_spec, vmem_spec = pl.BlockSpec(memory_space=pl.ANY), pl.BlockSpec(memory_space=pltpu.VMEM)
    return pl.pallas_call(
        prefetch_kernel,
        in_specs=[any_spec] * (2 + len(after)),
        out_specs=[vmem_spec] * 2,
        out_shape=[pltpu.VMEM(a.shape, a.dtype), pltpu.VMEM(b.shape, b.dtype)],
        scratch_shapes=[pltpu.SemaphoreType.DMA((2,))],
        compiler_params=pltpu.CompilerParams(vmem_limit_bytes=MIB),
        cost_estimate=time_of(3.5),
        name="prefetch",
    )(in_hbm(a), in_hbm(b), *map(in_hbm, after))


def feed_first_kernel(*refs):
    gain_ref, inward_ref, outward_ref = refs[6:9]
    mid_own_ref, mid_mate_ref, stack_ref, send_own_ref, send_mate_ref = refs[9:]
    own, mate = attn_sums(refs[:6])
    count = own.shape[0]
    mid_own_ref[...] = own
    mid_mate_ref[...] = mate
    stack_ref[0] = turned(own)
    stack_ref[1] = turned(mate)
    stream = jnp.concatenate([own, mate], axis=0).astype(F32)
    normed, unused = normalize(stream, -1)
    act = (normed * gain_ref[...]).astype(BF)
    hidden = outward_ref.shape[0]
    gate = dot_nn(act, inward_ref[:, :hidden])
    up = dot_nn(act, inward_ref[:, hidden:])
    unused, silu = swish(gate, up)
    part = dot_nn((silu * up).astype(BF), outward_ref[...])
    send_own_ref[...] = (stream[:count] + part[:count]).astype(BF)
    send_mate_ref[...] = part[count:].astype(BF)


def feed_second_kernel(*refs):
    grad_own_ref, grad_mate_ref, gain_ref, inward_hbm, outward_hbm = refs[6:11]
    part_own_ref, part_mate_ref, mid_own_ref, mid_mate_ref, turned_ref, out_own_ref, out_mate_ref = refs[11:18]
    inward_ref, outward_ref, sems = refs[18:]
    loads = feed_loads(inward_hbm, outward_hbm, inward_ref, outward_ref, sems)
    own, mate = attn_sums(refs[:6])
    count = own.shape[0]
    mid_own_ref[...] = own
    mid_mate_ref[...] = mate
    turned_ref[...] = turned(own)
    stream = jnp.concatenate([own, mate], axis=0).astype(F32)
    grad = jnp.concatenate([grad_own_ref[...], grad_mate_ref[...]], axis=0)
    normed, unused = normalize(stream, -1)
    act = (normed * gain_ref[...]).astype(BF)
    hidden = outward_ref.shape[0]
    loads[0].wait()
    gate = dot_nn(act, inward_ref[:, :hidden])
    loads[1].wait()
    up = dot_nn(act, inward_ref[:, hidden:])
    loads[2].wait()
    dhid = dot_nt(grad, outward_ref[...])
    hid, dgate, dup = feed_back(gate, up, dhid)
    dact = dot_nt(dgate, inward_ref[:, :hidden]) + dot_nt(dup, inward_ref[:, hidden:])
    part_own_ref[...] = dact[:count].astype(BF)
    part_mate_ref[...] = dact[count:].astype(BF)
    part = dot_nn(hid, outward_ref[...])
    out_own_ref[...] = (stream[:count] + part[:count]).astype(BF)
    out_mate_ref[...] = part[count:].astype(BF)


def feed_first_back_kernel(
    own_ref,
    mate_ref,
    grad_own_ref,
    grad_mate_ref,
    gain_ref,
    inward_hbm,
    outward_hbm,
    part_own_ref,
    part_mate_ref,
    inward_ref,
    outward_ref,
    sems,
):
    loads = feed_loads(inward_hbm, outward_hbm, inward_ref, outward_ref, sems)
    count = own_ref.shape[0]
    stream = jnp.concatenate([own_ref[...], mate_ref[...]], axis=0).astype(F32)
    grad = jnp.concatenate([turned(grad_own_ref[...]), turned(grad_mate_ref[...])], axis=0)
    normed, unused = normalize(stream, -1)
    act = (normed * gain_ref[...]).astype(BF)
    hidden = outward_ref.shape[0]
    loads[0].wait()
    gate = dot_nn(act, inward_ref[:, :hidden])
    loads[1].wait()
    up = dot_nn(act, inward_ref[:, hidden:])
    loads[2].wait()
    dhid = dot_nt(grad, outward_ref[...])
    unused, dgate, dup = feed_back(gate, up, dhid)
    dact = dot_nt(dgate, inward_ref[:, :hidden]) + dot_nt(dup, inward_ref[:, hidden:])
    part_own_ref[...] = dact[:count].astype(BF)
    part_mate_ref[...] = dact[count:].astype(BF)


def middle_grads(refs, gain_ref, turned_grads):
    for s_ref, g_ref, p_ref, r_ref in zip(*refs):
        grad = g_ref[...].astype(F32)
        grad = norm_back(
            s_ref[...].astype(F32),
            grad.T if turned_grads else grad,
            rounded_sum(p_ref[...], r_ref[...]),
            gain_ref[...],
        )
        yield grad.astype(BF)


def middle_first_back_kernel(lower_ref, *refs):
    gain_ref, grad_high_ref, dfirst_ref, first_ref = refs[8:12]
    out_own_ref, out_mate_ref, last_ref = refs[12:]
    pairs = refs[0:2], refs[2:4], refs[4:6], refs[6:8]
    own, mate = middle_grads(pairs, gain_ref, True)
    out_own_ref[...] = own
    out_mate_ref[...] = mate
    model = own.shape[1]
    is_lower = lower_ref[0] == 1
    last_ref[:model] = jnp.where(is_lower, turned(own), grad_high_ref[0])
    last_ref[model : 2 * model] = jnp.where(is_lower, turned(mate), grad_high_ref[1])
    last_ref[2 * model :] = jnp.where(is_lower, dfirst_ref[...], first_ref[...])


def middle_second_back_kernel(*refs):
    gain_ref, out_own_ref, out_mate_ref, turned_ref = refs[8:]
    pairs = refs[0:2], refs[2:4], refs[4:6], refs[6:8]
    own, mate = middle_grads(pairs, gain_ref, False)
    out_own_ref[...] = own
    out_mate_ref[...] = mate
    turned_ref[0] = turned(own)
    turned_ref[1] = turned(mate)


def attn_back_kernel(mixing, slot, *refs):
    ends_ref, grad_ref, x_ref, gain_ref, inward_ref, outward_ref, first_ref = refs[:7]
    count = x_ref.shape[0]
    width = outward_ref.shape[0]
    first = first_ref[slot * width : (slot + 1) * width].astype(F32)
    normed, unused = normalize(x_ref[...].astype(F32), -1)
    act = (normed * gain_ref[...]).astype(BF)
    allowed = allowed_keys(ends_at(ends_ref, slot), count)
    dattn = dot_nt(grad_ref[...], outward_ref[...]).T.astype(BF)
    proj = dot_nn(act, inward_ref[...]).T.astype(BF)
    values = proj[2 * width :]
    if mixing:
        mix = refs[7][...]
        values = ((1.0 - mix) * values.astype(F32) + mix * first).astype(BF)
    dquery, dkeys, dmixed, unused = attend_back(proj[:width], proj[width : 2 * width], values, dattn, allowed)
    if mixing:
        dfirst = (mix * dmixed).astype(BF)
        dvalues = (1.0 - mix) * dmixed
        if slot == 1:
            refs[-1][...] = dfirst
        else:
            refs[-1][:width] = dfirst
            refs[-1][width:] = refs[8][...]
    else:
        dvalues = dmixed + first
    dproj = jnp.concatenate([dquery, dkeys, dvalues], axis=0).T.astype(BF)
    dact = dot_nt(dproj, inward_ref[...])
    if mixing:
        refs[-2][...] = dact.astype(BF)
    else:
        grad = 0.0 if slot else grad_ref[...].astype(F32)
        refs[-1][...] = norm_back(x_ref[...].astype(F32), grad, dact, gain_ref[...]).astype(BF)


def input_back_kernel(x_ref, grad_ref, part_ref, got_ref, gain_ref, out_ref):
    grad = norm_back(
        x_ref[...].astype(F32),
        grad_ref[...].astype(F32),
        rounded_sum(part_ref[...], got_ref[...]),
        gain_ref[...],
    )
    out_ref[...] = grad.T.astype(BF)


def split_kernel(place_ref, a_own_ref, a_mate_ref, b_own_ref, b_mate_ref, row_ref, *refs):
    count, piece = a_own_ref.shape[0], refs[0].shape[1]
    for mask, ref in enumerate(refs):
        columns = aligned(place_ref[mask] * piece, piece)
        for i, source in enumerate((a_own_ref, a_mate_ref, b_own_ref, b_mate_ref)):
            ref[i * count : (i + 1) * count] = source[:, columns]
        row = jnp.concatenate([row_ref[...], jnp.zeros((1, piece - row_ref.shape[1]), F32)], axis=1)
        ref[4 * count :] = square_rows(row, ref.shape[0] - 4 * count)


def join_kernel(flags_ref, own_ref, beside_ref, over_ref, across_ref, a_ref, b_ref, row_ref):
    count = a_ref.shape[0] // 2
    lower, even = flags_ref[0] == 1, flags_ref[1] == 1
    for first, out_ref, holds in ((0, a_ref, lower), (2 * count, b_ref, jnp.logical_not(lower))):
        rows = slice(first, first + 2 * count)
        same = jnp.where(holds, own_ref[rows], over_ref[rows]).astype(F32)
        other = jnp.where(holds, beside_ref[rows], across_ref[rows]).astype(F32)
        own, mate = same[:count] + other[count:], same[count:] + other[:count]
        out_ref[:count] = jnp.where(even, own, mate).astype(out_ref.dtype)
        out_ref[count:] = jnp.where(even, mate, own).astype(out_ref.dtype)
    lanes = row_ref.shape[1]
    rows = [r[4 * count :, :lanes].astype(F32) for r in (own_ref, beside_ref, over_ref, across_ref)]
    row_ref[...] = jnp.sum(sum(rows), axis=0, keepdims=True)


def late_kernel(lower_ref, low_ref, high_ref, out_ref):
    out_ref[...] = jnp.where(lower_ref[0] == 1, low_ref[...], high_ref[...])


def square_sum_kernel(lower_ref, rows_ref, out_ref):
    total = jnp.sum(rows_ref[...].astype(F32))
    lane = lax.broadcasted_iota(jnp.int32, out_ref.shape, 1)
    out_ref[...] = jnp.where(lane == 1 - lower_ref[0], total, 0.0)


def add_kernel(a_ref, b_ref, out_ref):
    out_ref[...] = a_ref[...] + b_ref[...]


def call(kernel, outs, *args, smem=0, name=None, after=(), vmem=16, loads=(), free=()):
    whole = len(args)
    held = {id(w) for w in loads}
    either = {id(a) for a in free}

    def run(*refs):
        kernel(*refs[:whole], *refs[whole + len(after) :])

    def whole_block(a):
        return pl.BlockSpec(a.shape, lambda i: (0,) * len(a.shape))

    def given_spec(a):
        if id(a) in held:
            return pl.BlockSpec(memory_space=pl.ANY)
        return pl.BlockSpec(memory_space=pltpu.VMEM) if a.size >= WEIGHTS_FROM else whole_block(a)

    return pl.pallas_call(
        run,
        grid=(1,),
        out_shape=made_in_hbm(outs),
        in_specs=[pl.BlockSpec(memory_space=pltpu.SMEM)] * smem
        + [given_spec(a) for a in args[smem:]]
        + [pl.BlockSpec(memory_space=pl.ANY)] * len(after),
        out_specs=[whole_block(o) for o in outs],
        scratch_shapes=[pltpu.VMEM(w.shape, w.dtype) for w in loads]
        + [pltpu.SemaphoreType.DMA((1 + len(loads),))] * bool(loads),
        compiler_params=pltpu.CompilerParams(vmem_limit_bytes=vmem * MIB),
        cost_estimate=time_of(TIMES.get(name, 1.0)),
        name=name,
    )(*args[:smem], *[a if id(a) in either or a.size >= WEIGHTS_FROM and id(a) not in held else in_hbm(a) for a in args[smem:]], *[a if id(a) in either else in_hbm(a) for a in after])


def gate(array, after):
    spec = pl.BlockSpec(memory_space=pl.ANY)
    return pl.pallas_call(
        lambda *refs: None,
        out_shape=pltpu.HBM(array.shape, array.dtype),
        in_specs=[spec] * (1 + len(after)),
        out_specs=spec,
        input_output_aliases={0: 0},
        compiler_params=pltpu.CompilerParams(vmem_limit_bytes=MIB),
        cost_estimate=time_of(0.1),
        name="gate",
    )(in_hbm(array), *map(in_hbm, after))


class Share:
    def __init__(self, core, segment):
        self.segment = segment
        self.own = -(-segment // 256) * 128
        self.other = segment - self.own
        self.common = 2 * self.own - segment
        self.place = core * (segment - self.own)
        self.other_source = (1 - core) * self.common
        self.other_place = (1 - core) * self.own


def aligned(start, size, unit=128):
    return pl.ds(pl.multiple_of(start, unit), size)


def block_ref(refs, block, rows, shift=0):
    operand, index, first = block[:3]
    ref = refs[operand]
    for i in index:
        ref = ref.at[i]
    return ref.at[aligned(first + shift, rows), :]


def fetch(pick_ref, refs, choices, target, sems, shift=0):
    for which, blocks in enumerate(choices):

        @pl.when(pick_ref[0] == which)
        def _():
            for at, block in enumerate(blocks):
                source = block_ref(refs, block, target.shape[0], shift)
                count = source.shape[1]
                if block[3] is not None:
                    plane, other, slot = block[3]
                    core = 1 - pick_ref[1] if other else pick_ref[1]
                    at = (2 * plane + core) * 2 + slot
                columns = aligned(at * count, count)
                pltpu.make_async_copy(source, target.at[:, columns], sems.at[at]).start()


def arrived(refs, choices, target, sems, at):
    source = block_ref(refs, choices[0][0], target.shape[0])
    count = source.shape[1]
    pltpu.make_async_copy(source, target.at[:, aligned(at * count, count)], sems.at[at]).wait()


def weight_copies(share, inward_ref, outward_ref, plain_ref, inward, outward, plain, sems):
    own = share.own
    first, last = [(outward_ref.at[aligned(share.place, own), :], outward)], []
    for s in range(inward.shape[0] // own):
        place = aligned(s * share.segment + share.place, own)
        here = slice(s * own, (s + 1) * own)
        first.append((inward_ref.at[place, :], inward.at[here, :]))
        last.append((plain_ref.at[:, place], plain.at[:, here]))
    copies = [pltpu.make_async_copy(a, b, sems.at[i]) for i, (a, b) in enumerate(first + last)]
    return copies[: len(first)], copies[len(first) :]


def products(share, core, left, right, plain, refs):
    whole_ref, low_ref, dots_ref, stage, low_stage, dots, dots_row, sems = refs
    size, lanes = stage.shape[2], dots.shape[1]
    each = share.own // size
    steps = right.shape[0] // size

    def copies(step, slot):
        place = lax.div(step, each) * share.segment + share.place + lax.rem(step, each) * size
        columns = aligned(place, size)
        yield pltpu.make_async_copy(stage.at[slot], whole_ref.at[0, :, columns], sems.at[slot, 0])
        yield pltpu.make_async_copy(low_stage.at[slot], low_ref.at[:, aligned(step * size, size)], sems.at[slot, 1])

    dots[...] = jnp.zeros_like(dots)

    def one(step, unused):
        slot = lax.rem(step, 2)
        here = aligned(step * size, size)

        @pl.when(step >= 2)
        def _():
            for copy in copies(step, slot):
                copy.wait()

        value = dot_nt(left[...], right[here, :])
        stage[slot] = value
        low_stage[slot] = value.astype(BF)
        value = value * plain[:, here].astype(F32)
        total = 0.0
        for at in range(0, size, lanes):
            part = value[:, at : at + lanes]
            if at < share.common:
                part = jnp.where((core == 0) | (lax.rem(step, each) > 0), part, 0.0)
            total = total + part
        dots[...] += total
        for copy in copies(step, slot):
            copy.start()
        return 0

    lax.fori_loop(0, steps, one, 0)
    dots_row[...] = jnp.sum(dots[...].T, axis=0, keepdims=True)
    save = pltpu.make_async_copy(dots_row, dots_ref, sems.at[0, 2])
    save.start()
    return [save] + [copy for step in range(max(steps - 2, 0), steps) for copy in copies(step, step % 2)]


def outward_products(share, left, right, refs):
    whole_ref, low_ref, stage, low_stage, sems = refs
    value = dot_nt(left[...], right[...])
    stage[...] = value
    low_stage[...] = value.astype(BF)
    copies = [
        pltpu.make_async_copy(stage, whole_ref.at[0, aligned(share.place, share.own), :], sems.at[0]),
        pltpu.make_async_copy(low_stage, low_ref, sems.at[1]),
    ]
    for copy in copies:
        copy.start()
    return copies


def feed_weights_kernel(layout, *refs):
    (streams, grads), operands = layout
    pick_ref = refs[0]
    blocks_refs = refs[1 : 1 + operands]
    gain_ref, inward_ref, outward_ref, plain_ref = refs[1 + operands : 5 + operands]
    outs, scratch = refs[5 + operands : 10 + operands], refs[10 + operands :]
    act_all, grad_all, hid_all, dboth_all, inward, outward, plain = scratch[:7]
    stage, low_stage, dots, dots_row, out_stage, out_low, sems, weight_sems, out_sems = scratch[7:]
    core = pick_ref[1]
    share = Share(core, outward_ref.shape[0])
    hidden = share.own
    weights, plain_copies = weight_copies(
        share, inward_ref, outward_ref, plain_ref, inward, outward, plain, weight_sems
    )
    for copy in weights:
        copy.start()
    for copy in weights:
        copy.wait()
    fetch(pick_ref, blocks_refs, streams, act_all, sems.at[0])
    fetch(pick_ref, blocks_refs, grads, grad_all, sems.at[1])
    for copy in plain_copies:
        copy.start()
    blocks = len(streams[0])
    wider = 2 * (act_all.shape[1] // blocks)

    gain = column_of(gain_ref)

    def rows(step, unused):
        for at in (2 * step, 2 * step + 1):
            arrived(blocks_refs, streams, act_all, sems.at[0], at)
            arrived(blocks_refs, grads, grad_all, sems.at[1], at)
        here = aligned(step * wider, wider)
        normed, unused = normalize(act_all[:, here].astype(F32), 0)
        act = (normed * gain).astype(BF)
        act_all[:, here] = act
        for at in range(0, hidden, 384):
            to = slice(at, at + 384)
            up_to = slice(hidden + at, hidden + at + 384)
            gate, up = dot_nn(inward[to, :], act), dot_nn(inward[up_to, :], act)
            dhid = dot_nn(outward[to, :], grad_all[:, here])
            hid_all[to, here], dboth_all[to, here], dboth_all[up_to, here] = feed_back(gate, up, dhid)
        return 0

    lax.fori_loop(0, blocks // 2, rows, 0)
    for copy in plain_copies:
        copy.wait()
    copies = outward_products(share, hid_all, grad_all, (outs[1], outs[3], out_stage, out_low, out_sems.at[2]))
    copies += products(
        share, core, act_all, dboth_all, plain, (outs[0], outs[2], outs[4], stage, low_stage, dots, dots_row, out_sems)
    )
    for copy in copies:
        copy.wait()


def attn_scores_kernel(layout, *refs):
    (streams,), operands = layout
    pick_ref, ends_ref = refs[:2]
    blocks_refs = refs[2 : 2 + operands]
    gain_ref, inward_ref = refs[2 + operands : 4 + operands]
    outs, scratch = refs[4 + operands : 7 + operands], refs[7 + operands :]
    act_all, proj_all, probs_all, inward, sems, weight_sems, out_sems = scratch
    own = inward.shape[0] // 3
    share = Share(pick_ref[1], inward_ref.shape[0] // 3)
    copies = []
    for s in range(3):
        place = aligned(s * share.segment + share.place, own)
        copies.append(
            pltpu.make_async_copy(inward_ref.at[place, :], inward.at[s * own : (s + 1) * own, :], weight_sems.at[s])
        )
    for copy in copies:
        copy.start()
    for copy in copies:
        copy.wait()
    fetch(pick_ref, blocks_refs, streams, act_all, sems)
    blocks = len(streams[0])
    count = act_all.shape[1] // blocks
    each = 4
    wider = each * count

    def saves(step):
        here = aligned(step * wider, wider)
        for i, (source, target) in enumerate(zip((act_all, proj_all, probs_all), outs)):
            yield pltpu.make_async_copy(source.at[:, here], target.at[:, here], out_sems.at[i, step])

    gain = column_of(gain_ref)

    def rows(step, unused):
        for at in [each * step + i for i in range(each)]:
            arrived(blocks_refs, streams, act_all, sems, at)
        here = aligned(step * wider, wider)
        normed, unused = normalize(act_all[:, here].astype(F32), 0)
        act = (normed * gain).astype(BF)
        act_all[:, here] = act
        proj = dot_nn(inward[...], act).astype(BF)
        proj_all[:, here] = proj
        for i in range(each):
            cols = slice(i * count, (i + 1) * count)
            allowed = allowed_keys(ends_at(ends_ref, step * each + i), count)
            query, keys = heads_of(proj[:own, cols]), heads_of(proj[own : 2 * own, cols])
            scores = [dot_tn(k, q) for q, k in zip(query, keys)]
            probs = [softmax_keys(s, allowed).astype(BF) for s in scores]
            probs_all[:, aligned(step * wider + i * count, count)] = jnp.concatenate(probs, axis=0)
        for copy in saves(step):
            copy.start()
        return 0

    lax.fori_loop(0, blocks // each, rows, 0)
    for step in range(blocks // each):
        for copy in saves(step):
            copy.wait()


def attn_scores(smem, streams, gain, inward, model, after):
    arrays, layout = gather_layout((streams,))
    segment = inward.shape[0] // 3
    own = Share(0, segment).own
    blocks = len(layout[0][0])
    count = arrays[0].shape[-1]
    total = blocks * count
    shapes = [(model, total), (3 * own, total), (own // HEAD_DIM * count, total)]
    layout = (layout, len(arrays))
    whole = len(smem) + len(arrays) + 2

    def run(*refs):
        attn_scores_kernel(layout, *refs[:whole], *refs[whole + len(after) :])

    any_spec, vmem_spec = pl.BlockSpec(memory_space=pl.ANY), pl.BlockSpec(memory_space=pltpu.VMEM)
    return pl.pallas_call(
        run,
        in_specs=[pl.BlockSpec(memory_space=pltpu.SMEM)] * len(smem)
        + [any_spec] * len(arrays)
        + [vmem_spec, any_spec]
        + [any_spec] * len(after),
        out_specs=[any_spec] * 3,
        out_shape=made_in_hbm([shape_of(s, BF) for s in shapes]),
        scratch_shapes=[pltpu.VMEM(s, BF) for s in shapes]
        + [
            pltpu.VMEM((3 * own, model), BF),
            pltpu.SemaphoreType.DMA((blocks,)),
            pltpu.SemaphoreType.DMA((3,)),
            pltpu.SemaphoreType.DMA((3, blocks // 4)),
        ],
        compiler_params=pltpu.CompilerParams(vmem_limit_bytes=24 * MIB),
        cost_estimate=time_of(14.0),
        name="attn_scores",
    )(*smem, *map(in_hbm, arrays), gain, in_hbm(inward), *map(in_hbm, after))


def attn_weights_kernel(layout, *refs):
    (grads, firsts), operands = layout
    pick_ref, level_ref = refs[:2]
    blocks_refs = refs[2 : 2 + operands]
    act_ref, proj_ref, probs_ref, outward_ref, plain_ref = refs[2 + operands : 7 + operands]
    outs, scratch = refs[7 + operands : 12 + operands], refs[12 + operands :]
    act_all, grad_all, attn_all, dproj_all, outward, plain = scratch[:6]
    stage, low_stage, dots, dots_row, out_stage, out_low, first_all, proj_all, probs_all = scratch[6:15]
    sems, weight_sems, kept_sems, out_sems = scratch[15:]
    core = pick_ref[1]
    share = Share(core, outward_ref.shape[0])
    width = share.own
    load = pltpu.make_async_copy(outward_ref.at[aligned(share.place, width), :], outward, weight_sems.at[0])
    load.start()
    fetch(pick_ref, blocks_refs, grads, grad_all, sems.at[0])
    fetch(pick_ref, blocks_refs, firsts, first_all, sems.at[1], share.place)
    blocks = len(grads[0])
    count = act_all.shape[1] // blocks
    each = 4
    wider = each * count

    def kept(step):
        here = aligned(step * wider, wider)
        for i, (source, target) in enumerate(((proj_ref, proj_all), (probs_ref, probs_all), (act_ref, act_all))):
            yield pltpu.make_async_copy(source.at[:, here], target.at[:, here], kept_sems.at[i, step])

    for step in range(blocks // each):
        for copy in kept(step):
            copy.start()
    plain_copies = []
    for s in range(3):
        place = aligned(s * share.segment + share.place, width)
        here = slice(s * width, (s + 1) * width)
        plain_copies.append(
            pltpu.make_async_copy(plain_ref.at[:, place], plain.at[:, here], weight_sems.at[1 + s])
        )
    for copy in plain_copies:
        copy.start()
    load.wait()

    upper = pick_ref[0].astype(F32)
    heads = width // HEAD_DIM
    first_head = pick_ref[3] * (share.segment // HEAD_DIM) + core * (share.segment - width) // HEAD_DIM
    levels = [level_ref[first_head + i].astype(F32) / 8.0 * upper for i in range(heads)]
    mix = jnp.concatenate([jnp.full((HEAD_DIM, 1), level, F32) for level in levels], axis=0)

    def rows(step, unused):
        for at in [each * step + i for i in range(each)]:
            arrived(blocks_refs, grads, grad_all, sems.at[0], at)
            arrived(blocks_refs, firsts, first_all, sems.at[1], at)
        for copy in kept(step):
            copy.wait()
        here = aligned(step * wider, wider)
        proj = proj_all[:, here]
        dattn = dot_nn(outward[...], grad_all[:, here]).astype(BF)
        first = first_all[:, here].astype(F32)
        values = ((1.0 - mix) * proj[2 * width :].astype(F32) + mix * first).astype(BF)
        for i in range(each):
            cols = slice(i * count, (i + 1) * count)
            place = aligned(step * wider + i * count, count)
            probs = probs_all[:, place]
            dquery, dkeys, dmixed, attn = attend_back_from(
                proj[:width, cols],
                proj[width : 2 * width, cols],
                values[:, cols],
                dattn[:, cols],
                lambda: [probs[at : at + count] for at in range(0, probs.shape[0], count)],
                True,
            )
            dvalues = (1.0 - mix) * dmixed + (1.0 - upper) * first[:, cols]
            attn_all[:, place] = attn.astype(BF)
            dproj_all[:, place] = jnp.concatenate([dquery, dkeys, dvalues], axis=0).astype(BF)
        return 0

    lax.fori_loop(0, blocks // each, rows, 0)
    for copy in plain_copies:
        copy.wait()
    copies = outward_products(share, attn_all, grad_all, (outs[1], outs[3], out_stage, out_low, out_sems.at[2]))
    copies += products(
        share, core, act_all, dproj_all, plain, (outs[0], outs[2], outs[4], stage, low_stage, dots, dots_row, out_sems)
    )
    for copy in copies:
        copy.wait()


def gather_layout(sets):
    arrays, layout = [], []
    for choices in sets:
        placed = []
        for blocks in choices:
            row = []
            for array, index, first, where in blocks:
                at = next((i for i, a in enumerate(arrays) if a is array), None)
                if at is None:
                    at = len(arrays)
                    arrays.append(array)
                row.append((at, index, first, where))
            placed.append(tuple(row))
        layout.append(tuple(placed))
    return arrays, tuple(layout)


def weight_call(kernel, smem, sets, kept, small, weights, name, after=()):
    arrays, layout = gather_layout(sets)
    *turned_in, outward, plain = weights
    segment, model = outward.shape
    segments = plain.shape[1] // segment
    own = Share(0, segment).own
    blocks = len(layout[0][0])
    total = blocks * arrays[0].shape[-1]
    block = 256
    whole = len(smem) + len(arrays) + len(kept) + len(small) + len(weights)
    layout = (layout, len(arrays))

    def run(*refs):
        kernel(layout, *refs[:whole], *refs[whole + len(after) :])

    any_spec, vmem_spec = pl.BlockSpec(memory_space=pl.ANY), pl.BlockSpec(memory_space=pltpu.VMEM)
    scratch = [
        pltpu.VMEM((model, total), BF),
        pltpu.VMEM((model, total), BF),
        pltpu.VMEM((own, total), BF),
        pltpu.VMEM((segments * own, total), BF),
    ]
    scratch += [pltpu.VMEM((segments * own, model), BF)] * len(turned_in)
    scratch += [
        pltpu.VMEM((own, model), BF),
        pltpu.VMEM((model, segments * own), BF),
        pltpu.VMEM((2, model, block), F32),
        pltpu.VMEM((2, model, block), BF),
        pltpu.VMEM((model, 128), F32),
        pltpu.VMEM((1, model), F32),
        pltpu.VMEM((own, model), F32),
        pltpu.VMEM((own, model), BF),
    ]
    if kept:
        scratch += [pltpu.VMEM((own, total), BF)] + [pltpu.VMEM(a.shape, BF) for a in kept[1:]]
    scratch += [
        pltpu.SemaphoreType.DMA((len(sets), blocks)),
        pltpu.SemaphoreType.DMA((2 * segments + 1,)),
    ]
    if kept:
        scratch += [pltpu.SemaphoreType.DMA((3, blocks // 4))]
    scratch += [pltpu.SemaphoreType.DMA((3, 3))]
    return pl.pallas_call(
        run,
        in_specs=[pl.BlockSpec(memory_space=pltpu.SMEM)] * len(smem)
        + [any_spec] * (len(arrays) + len(kept))
        + [vmem_spec] * len(small)
        + [any_spec] * (len(weights) + len(after)),
        out_specs=[any_spec] * 5,
        out_shape=made_in_hbm(
            [
                shape_of((1, model, segments * segment), F32),
                shape_of((1,) + outward.shape, F32),
                shape_of((model, segments * own), BF),
                shape_of((own, model), BF),
                shape_of((1, model), F32),
            ]
        ),
        scratch_shapes=scratch,
        compiler_params=pltpu.CompilerParams(vmem_limit_bytes=56 * MIB),
        cost_estimate=time_of(27.0),
        name=name,
    )(*smem, *map(in_hbm, arrays), *map(in_hbm, kept), *small, *map(in_hbm, weights), *map(in_hbm, after))


def fill_kernel(segment, core_ref, low, out_low, unused_ref, unused_out_ref, *refs):
    whole_ref, whole_out_ref, stage, out_stage, sems = refs
    share = Share(core_ref[0], segment)
    own, other, size = share.own, share.other, stage.shape[1]
    segments = low.shape[1] // own
    writes = []
    for block in range(stage.shape[0]):
        rows = slice(block * size, (block + 1) * size)
        for s in range(segments):
            here = slice(s * other, (s + 1) * other)
            stage[block, :, here] = low[rows, aligned(s * own + share.other_source, other)].astype(F32)
            place = aligned(s * segment + share.other_place, other)
            copy = pltpu.make_async_copy(
                stage.at[block, :, here], whole_ref.at[0, rows, place], sems.at[block, s]
            )
            copy.start()
            writes.append(copy)
    out_stage[...] = out_low[aligned(share.other_source, other), :].astype(F32)
    copy = pltpu.make_async_copy(
        out_stage, whole_out_ref.at[0, aligned(share.other_place, other), :], sems.at[0, segments]
    )
    copy.start()
    for copy in writes + [copy]:
        copy.wait()


def filled(core, low, out_low, whole, whole_out, after=()):
    segment, model = whole_out.shape[1:]
    segments = whole.shape[2] // segment
    share = Share(0, segment)
    steps = 4
    any_spec = pl.BlockSpec(memory_space=pl.ANY)

    def run(*refs):
        fill_kernel(segment, *refs[:5], *refs[5 + len(after) :])

    return pl.pallas_call(
        run,
        in_specs=[pl.BlockSpec(memory_space=pltpu.SMEM)]
        + [pl.BlockSpec(memory_space=pltpu.VMEM)] * 2
        + [any_spec] * (2 + len(after)),
        out_specs=[any_spec] * 2,
        out_shape=made_in_hbm([whole, whole_out]),
        input_output_aliases={3: 0, 4: 1},
        scratch_shapes=[
            pltpu.VMEM((steps, model // steps, segments * share.other), F32),
            pltpu.VMEM((share.other, model), F32),
            pltpu.SemaphoreType.DMA((steps, segments + 1)),
        ],
        compiler_params=pltpu.CompilerParams(vmem_limit_bytes=32 * MIB),
        cost_estimate=time_of(5.0),
        name="fill",
    )(core, low, out_low, in_hbm(whole), in_hbm(whole_out), *map(in_hbm, after))


def body(tokens, cotangent, gains, attn_in, attn_out, ffn_in, ffn_out, mix_level, seq_lengths):
    section = lax.axis_index("section")
    core = lax.axis_index("dp") % 2
    lower = section < 2
    even = section % 2 == 0
    sections = lax.axis_size("section")
    dp = lax.axis_size("dp")
    group = min(dp, GROUP)
    planes = group // 2
    micro = seq_lengths.shape[0]
    count = tokens.shape[0] // micro
    piece = tokens.shape[1]
    inward, outward, feed_in, feed_out = attn_in[0], attn_out[0], ffn_in[0], ffn_out[0]
    model = inward.shape[0]
    width = outward.shape[0]

    low, high = (0, 1), (2, 3)
    everyone = low + high

    def send(x, mask, sources=everyone):
        return lax.ppermute(x, "section", [(i, i ^ mask) for i in sources])

    def planes_of(x, sources=everyone):
        def plane(by):
            pairs = [
                (s * dp + i, s * dp + i // group * group + (i % group // 2 + by) % planes * 2 + i % 2)
                for s in sources
                for i in range(dp)
            ]
            return lax.ppermute(x, ("section", "dp"), pairs)

        return [plane(by) for by in range(1, planes)]

    def other_core(x, sources=everyone):
        pairs = [(s * dp + i, s * dp + (i ^ 1)) for s in sources for i in range(dp)]
        return lax.ppermute(x, ("section", "dp"), pairs)

    near = jnp.where(lower, tokens, cotangent)
    far = jnp.where(lower, cotangent, tokens)
    got_far, got_across, got_near = send(far, 2), send(far, 3), send(near, 1)
    got_gains = send(gains, 1)
    ends = jnp.cumsum(seq_lengths, axis=1)
    ends = jnp.where(even, ends, ends[::-1])

    def by_half(mine, other):
        return [jnp.where(even, mine, other), jnp.where(even, other, mine)]

    ours, theirs = by_half(near, got_near), by_half(got_far, got_across)
    given = jnp.concatenate(
        [jnp.where(lower, a, b) for a, b in zip(ours + theirs, theirs + ours)], axis=1
    )
    top, bottom = given[:count], given[count:]
    given_own, given_mate = jnp.where(even, top, bottom), jnp.where(even, bottom, top)

    gain_attn = jnp.where(even, gains, got_gains)
    gain_feed = jnp.where(even, got_gains, gains)
    mix_all = jnp.repeat(mix_level.astype(F32) / 8.0, HEAD_DIM)
    mix_low, mix_high = mix_all[:width, None], mix_all[width:, None]
    mix = jnp.where(even, mix_low, mix_high)

    slot = shape_of((count, model), BF)
    half_turned = shape_of((width, count), BF)
    pair_half_turned = shape_of((2 * width, count), BF)
    slot_turned = shape_of((model, count), BF)
    pair_turned = shape_of((2, model, count), BF)
    pair_and_rows = shape_of((2, model + 16, count), BF)
    square_row = shape_of((1, count), F32)
    is_lower = lower.astype(jnp.int32)[None]

    attn_call = functools.partial(call, smem=1)
    part_mate, first_mate, square_mate = attn_call(
        attn_mate_kernel,
        [slot, half_turned, square_row],
        ends,
        given_mate,
        gain_attn,
        inward,
        outward,
        name="attn_mate",
    )
    got_own = send(part_mate, 1, low)
    part_own, first_both, square_own, given_stack = attn_call(
        attn_own_kernel,
        [slot, pair_half_turned, square_row, pair_and_rows],
        ends,
        given_own,
        gain_attn,
        inward,
        outward,
        given_mate,
        first_mate,
        name="attn_own",
    )
    got_mate = send(part_own, 1, low)
    first_over = send(first_both, 2, low)
    square0 = square_own, square_mate
    mid0_own, mid0_mate, mid0_stack, send_own, send_mate = call(
        feed_first_kernel,
        [slot, slot, pair_turned, slot, slot],
        given_own,
        given_mate,
        part_own,
        part_mate,
        got_own,
        got_mate,
        gain_feed,
        *prefetched(feed_in, feed_out, (part_own,)),
        vmem=20,
        free=(first_over,),
        name="feed_first",
        after=(first_over,),
    )
    x_a, x_b = send(send_own, 2, low), send(send_mate, 3, low)
    feed_in_turned, inward_turned = call(
        turn_kernel,
        [shape_of(feed_in.shape[::-1], BF), shape_of(inward.shape[::-1], BF)],
        feed_in,
        inward,
        vmem=32,
        name="turn_weights",
        after=(send_own,),
    )

    x1_own = call(sum_kernel, [slot], x_a, x_b, name="sum", after=(inward_turned,), free=(x_a, x_b))[0]
    x1_mate = send(x1_own, 1, high)

    def attn_mixed(which, x, out, *more):
        return attn_call(
            functools.partial(attn_mixed_kernel, which),
            [slot, out],
            ends,
            x,
            gain_attn,
            inward,
            outward,
            mix,
            first_over,
            *more,
            name="attn_mixed",
            free=(first_over,),
        )

    part_own, square_own = attn_mixed(0, x1_own, square_row)
    got_mate = send(part_own, 1, high)
    part_mate, middle_stack = attn_mixed(
        1,
        x1_mate,
        pair_and_rows,
        jnp.full((1, count), is_lower[0], jnp.int32),
        mid0_stack,
        x1_own,
        square_own,
        *square0,
    )
    got_own = send(part_mate, 1, high)
    def everywhere(x):
        groups = [list(range(at, at + group)) for at in range(0, dp, group)]
        return lax.all_gather(x, "dp", axis=0, axis_index_groups=groups)

    def gathered(stack):
        every = everywhere(stack)
        return every, [(every, (d, i), 0, None) for d in range(group) for i in range(2)]

    def own_gathered(own, after):
        same_core = [
            [at + 2 * z + c for z in range(planes)] for at in range(0, dp, group) for c in range(2)
        ]
        every = gate(lax.all_gather(own, "dp", axis=0, axis_index_groups=same_core), after)
        return every, send(every, 1)

    def own_blocks(every, mate):
        arrays = ((every, False, 0), (other_core(every), True, 0), (mate, False, 1), (other_core(mate), True, 1))
        return [(a, (z,), 0, (z, other, i)) for a, other, i in arrays for z in range(planes)]

    all_given, set_given = gathered(given_stack)
    all_middle, set_middle = gathered(middle_stack)
    part_own, part_mate, mid1_own, mid1_mate, mid1_turned, out_own, out_mate = call(
        feed_second_kernel,
        [slot, slot, slot, slot, slot_turned, slot, slot],
        x1_own,
        x1_mate,
        part_own,
        part_mate,
        got_own,
        got_mate,
        given_own,
        given_mate,
        gain_feed,
        feed_in,
        feed_out,
        vmem=36,
        loads=(feed_in, feed_out),
        name="feed_second",
        after=(all_given,),
    )
    got_own, got_mate = send(part_mate, 1, high), send(part_own, 1, high)
    middle1_own, middle1_mate, grad1_turned = call(
        middle_second_back_kernel,
        [slot, slot, pair_turned],
        mid1_own,
        mid1_mate,
        given_own,
        given_mate,
        part_own,
        part_mate,
        got_own,
        got_mate,
        gain_feed,
        free=(got_own, got_mate),
        name="middle_second_back",
    )

    def attn_back(which, grad, x, first, *mixed, after=()):
        outs = [slot] + [half_turned if which else pair_half_turned] * bool(mixed)
        return call(
            functools.partial(attn_back_kernel, bool(mixed), which),
            outs,
            ends,
            grad,
            x,
            gain_attn,
            inward,
            outward,
            first,
            *mixed,
            smem=1,
            name="attn_back",
            after=after,
            free=(first,),
        )

    part_mate, dfirst_mate = attn_back(1, middle1_mate, x1_mate, first_over, mix)
    got_own = send(part_mate, 1, high)
    part_own, dfirst_both = attn_back(0, middle1_own, x1_own, first_over, mix, dfirst_mate)
    dfirst = send(dfirst_both, 2, high)
    grad_x1 = call(
        input_back_kernel,
        [slot_turned],
        x1_own,
        middle1_own,
        part_own,
        got_own,
        gain_attn,
        name="input_back",
        free=(got_own,),
    )[0]
    grad_own, grad_mate = send(grad_x1, 2, high), send(grad_x1, 3, high)

    received = (grad_own, grad_mate, dfirst)
    late = call(
        late_kernel, [slot_turned], is_lower, grad_own, mid1_turned, smem=1, name="late", free=received
    )[0]
    part_own, part_mate = call(
        feed_first_back_kernel,
        [slot, slot],
        mid0_own,
        mid0_mate,
        grad_own,
        grad_mate,
        gain_feed,
        feed_in,
        feed_out,
        vmem=36,
        loads=(feed_in, feed_out),
        free=received,
        name="feed_first_back",
        after=(late, all_middle),
    )
    got_own, got_mate = send(part_mate, 1, low), send(part_own, 1, low)
    middle_own, middle_mate, last = call(
        middle_first_back_kernel,
        [slot, slot, shape_of((2 * model + 2 * width, count), BF)],
        is_lower,
        mid0_own,
        mid0_mate,
        grad_own,
        grad_mate,
        part_own,
        part_mate,
        got_own,
        got_mate,
        gain_feed,
        grad1_turned,
        dfirst,
        first_over,
        smem=1,
        free=(got_own, got_mate) + received,
        name="middle_first_back",
    )

    place = jnp.stack([section ^ mask for mask in range(sections)]).astype(jnp.int32)

    late_every, late_mate = own_gathered(late, [middle_own])
    part_mate = attn_back(1, middle_mate, given_mate, dfirst, after=(late_every,))[0]
    part_own = attn_back(0, middle_own, given_own, dfirst, after=(part_mate,))[0]

    all_ends = all_given[:, :, model, : ends.shape[1]].reshape(2 * group, -1).astype(jnp.int32)
    core_at = core.astype(jnp.int32)[None]
    half = (section % 2).astype(jnp.int32)[None]
    pick = jnp.concatenate([1 - is_lower, core_at, core_at, half])
    squares = pl.pallas_call(
        square_sum_kernel,
        grid_spec=pltpu.PrefetchScalarGridSpec(
            num_scalar_prefetch=1,
            grid=(1,),
            in_specs=[pl.BlockSpec((group, 1, 16, count), lambda i, unused: (0, 0, model // 16, 0))],
            out_specs=pl.BlockSpec((1, 128), lambda i, unused: (0, 0)),
        ),
        out_shape=pltpu.HBM((1, 128), F32),
        compiler_params=pltpu.CompilerParams(vmem_limit_bytes=4 * MIB),
        name="square_sum",
    )(is_lower, in_hbm(all_middle))

    pieces = call(
        split_kernel,
        [shape_of((4 * count + 16, piece), BF)] * sections,
        place,
        part_own,
        part_mate,
        out_own,
        out_mate,
        squares,
        smem=1,
        name="split",
    )
    scores = attn_scores(
        (pick, all_ends),
        (set_given, set_middle),
        gain_attn,
        inward_turned,
        model,
        (late_every,),
    )
    set_late = own_blocks(late_every, gate(late_mate, [pieces[0], scores[2]]))
    all_last = everywhere(last)
    set_last = [(all_last, (d,), at, None) for d in range(group) for at in (0, model)]
    set_first = [(all_last, (d,), 2 * model + at, None) for d in range(group) for at in (0, width)]
    d_feed_in, d_feed_out, low_in, low_out, dots_feed = weight_call(
        feed_weights_kernel,
        (pick,),
        ((set_middle, set_late), (set_late, set_given)),
        (),
        (gain_feed,),
        (feed_in_turned, feed_out, feed_in),
        "feed_weights",
        after=(pieces[0], scores[2]),
    )
    received = [send(pieces[mask], mask) for mask in range(1, sections)]
    dinput, out, squares = call(
        join_kernel,
        [shape_of((2 * count, piece), F32), shape_of((2 * count, piece), BF), shape_of((1, 128), F32)],
        jnp.stack([lower, even]).astype(jnp.int32),
        pieces[0],
        *received,
        smem=1,
        name="join",
        free=received,
        after=(low_in,),
    )
    if dp > group:
        squares = lax.psum(squares, "dp") / group
    norms = squares[0, :2] / (micro * count * dp * 2 * width)
    d_feed_in, d_feed_out = filled(core_at, other_core(low_in), other_core(low_out), d_feed_in, d_feed_out)
    d_in, d_out, low_in, low_out, dots_attn = weight_call(
        attn_weights_kernel,
        (pick, mix_level),
        ((set_last, set_last), (set_first, set_first)),
        scores,
        (),
        (outward, inward),
        "attn_weights",
        after=(dinput,),
    )
    d_in, d_out = filled(core_at, other_core(low_in), other_core(low_out), d_in, d_out, (d_feed_in,))

    mine, sent = jnp.where(even, dots_attn, dots_feed), jnp.where(even, dots_feed, dots_attn)
    both = [(s * dp + i, (s ^ 1) * dp + (i ^ 1)) for s in range(sections) for i in range(dp)]
    d_gain = mine + send(sent, 1) + other_core(mine) + lax.ppermute(sent, ("section", "dp"), both)
    if dp > group:
        d_gain = lax.psum(d_gain, "dp") / group
        across = [list(range(at, dp, group)) for at in range(group)]
        d_in, d_out, d_feed_in, d_feed_out = [
            lax.psum(x.astype(BF), "dp", axis_index_groups=across).astype(F32)
            for x in (d_in, d_out, d_feed_in, d_feed_out)
        ]
    d_gain = d_gain / gains
    return (out, dinput, d_gain, d_in, d_out, d_feed_in, d_feed_out, norms[0], norms[1])


def solution(mesh):
    in_specs = (
        P("dp", "section"),
        P("dp", "section"),
        P("section", None),
        P("section", None, None),
        P("section", None, None),
        P("section", None, None),
        P("section", None, None),
        P(),
        P("dp", None),
    )
    out_specs = (
        P("dp", "section"),
        P("dp", "section"),
        P("section", None),
        P("section", None, None),
        P("section", None, None),
        P("section", None, None),
        P("section", None, None),
        P(),
        P(),
    )
    return jax.shard_map(body, mesh=mesh, in_specs=in_specs, out_specs=out_specs, check_vma=False)
```

```python
import functools

import jax
import jax.numpy as jnp
from jax import lax
from jax.experimental import pallas as pl
from jax.experimental.pallas import tpu as pltpu
from jax.sharding import PartitionSpec as P

HEAD_DIM = 64
EPS = 1e-05
NEG = -1e30
GROUP = 8
BF = jnp.bfloat16
F32 = jnp.float32
MIB = 1024 * 1024
WEIGHTS_FROM = 500_000


TIMES = {
    "turn_weights": 5.9,
    "attn_mate": 3.1,
    "attn_own": 3.5,
    "feed_first": 5.3,
    "sum": 1.8,
    "stack": 1.9,
    "attn_mixed": 3.3,
    "feed_second": 8.5,
    "middle_second_back": 3.1,
    "attn_back": 4.7,
    "input_back": 2.3,
    "late": 2.2,
    "feed_first_back": 6.8,
    "middle_first_back": 3.3,
    "split": 1.9,
    "join": 1.9,
    "add": 1.2,
}


def time_of(microseconds):
    return pl.CostEstimate(flops=int(microseconds * 1.15e9), bytes_accessed=1, transcendentals=0)


def dot_nn(left, right):
    return lax.dot_general(left, right, (((1,), (0,)), ((), ())), preferred_element_type=F32)


def dot_nt(left, right):
    return lax.dot_general(left, right, (((1,), (1,)), ((), ())), preferred_element_type=F32)


def dot_tn(left, right):
    return lax.dot_general(left, right, (((0,), (0,)), ((), ())), preferred_element_type=F32)


def shape_of(shape, dtype):
    return jax.ShapeDtypeStruct(shape, dtype)


def in_hbm(a):
    return pltpu.with_memory_space_constraint(a, pltpu.HBM)


def made_in_hbm(outs):
    return [pltpu.HBM(o.shape, o.dtype) for o in outs]


def normalize(stream, axis):
    rscale = lax.rsqrt(jnp.mean(stream * stream, axis=axis, keepdims=True) + EPS)
    return stream * rscale, rscale


def norm_back(stream, grad_out, dact, gain):
    normed, rscale = normalize(stream, -1)
    dnorm = dact * gain
    mean = jnp.mean(dnorm * normed, axis=-1, keepdims=True)
    return grad_out + rscale * (dnorm - normed * mean)


def column_of(row_ref):
    return jnp.broadcast_to(row_ref[...], (8, row_ref.shape[1])).T[:, 0:1]


def turned(rows):
    return rows.astype(F32).T.astype(BF)


def allowed_keys(ends, count):
    key = lax.broadcasted_iota(jnp.int32, (count, count), 0)
    query = lax.broadcasted_iota(jnp.int32, (count, count), 1)
    segment_key = sum((key >= end).astype(jnp.int32) for end in ends)
    segment_query = sum((query >= end).astype(jnp.int32) for end in ends)
    return (key <= query) & (segment_key == segment_query)


def heads_of(array, first=0):
    return [array[at : at + HEAD_DIM] for at in range(first, array.shape[0], HEAD_DIM)]


def softmax_keys(scores, allowed):
    scores = jnp.where(allowed, scores * HEAD_DIM**-0.5, NEG)
    exponent = jnp.exp(scores - jnp.max(scores, axis=0, keepdims=True))
    return exponent * (1.0 / jnp.sum(exponent, axis=0, keepdims=True))


def attend(query, keys, values, allowed):
    query, keys, values = heads_of(query), heads_of(keys), heads_of(values)
    scores = [dot_tn(k, q) for q, k in zip(query, keys)]
    probs = [softmax_keys(s, allowed).astype(BF) for s in scores]
    return jnp.concatenate([dot_nn(v, p) for v, p in zip(values, probs)], axis=0)


def attend_back(query, keys, values, dattn, allowed):
    scores = [dot_tn(k, q) for q, k in zip(heads_of(query), heads_of(keys))]
    return attend_back_from(query, keys, values, dattn, lambda: [softmax_keys(s, allowed) for s in scores], False)


def attend_back_from(query, keys, values, dattn, probs_of, forward):
    query, keys, values, dattn = [heads_of(a) for a in (query, keys, values, dattn)]
    dprobs = [dot_tn(v, d) for v, d in zip(values, dattn)]
    low_probs, dscores = [], []
    for probs, dprob in zip(probs_of(), dprobs):
        low_probs.append(probs.astype(BF))
        probs = probs.astype(F32)
        dscores.append((probs * (dprob - jnp.sum(dprob * probs, axis=0, keepdims=True))).astype(BF))
    attn = None
    if forward:
        attn = jnp.concatenate([dot_nn(v, p) for v, p in zip(values, low_probs)], axis=0)
    dquery = jnp.concatenate([dot_nn(k, d) for k, d in zip(keys, dscores)], axis=0) * HEAD_DIM**-0.5
    dkeys = jnp.concatenate([dot_nt(q, d) for q, d in zip(query, dscores)], axis=0) * HEAD_DIM**-0.5
    dmixed = jnp.concatenate([dot_nt(d, p) for d, p in zip(dattn, low_probs)], axis=0)
    return dquery, dkeys, dmixed, attn


def swish(gate, up):
    sigmoid = 1.0 / (1.0 + jnp.exp(-gate))
    return sigmoid, gate * sigmoid


def feed_back(gate, up, dhid):
    sigmoid, silu = swish(gate, up)
    hid = (silu * up).astype(BF)
    dgate = dhid * up * (sigmoid * (1.0 + gate * (1.0 - sigmoid)))
    dup = dhid * silu
    return hid, dgate.astype(BF), dup.astype(BF)


def mix_column(levels_ref):
    levels = [levels_ref[i].astype(F32) / 8.0 for i in range(levels_ref.shape[0])]
    return jnp.concatenate([jnp.full((HEAD_DIM, 1), level, F32) for level in levels], axis=0)


def ends_at(ends_ref, slot):
    return [ends_ref[slot, i] for i in range(ends_ref.shape[1])]


def rounded_sum(left, right):
    return left.astype(F32) + right.astype(F32)


def turn_kernel(a_ref, b_ref, a_out, b_out):
    size = 256
    row = lax.broadcasted_iota(jnp.int32, (size, size), 0)
    col = lax.broadcasted_iota(jnp.int32, (size, size), 1)
    identity = jnp.where(row == col, 1.0, 0.0).astype(BF)
    for source, target in ((a_ref, a_out), (b_ref, b_out)):
        for at in range(0, source.shape[1], size):
            target[at : at + size, :] = dot_nt(identity, source[:, at : at + size]).astype(BF)


def attend_forward(slot, ends_ref, x, gain_ref, inward_ref, mix, first):
    width = inward_ref.shape[1] // 3
    normed, unused = normalize(x.astype(F32), -1)
    act = (normed * gain_ref[...]).astype(BF)
    proj = dot_nn(act, inward_ref[...]).T.astype(BF)
    values = proj[2 * width :]
    if mix is not None:
        values = ((1.0 - mix) * values.astype(F32) + mix * first.astype(F32)).astype(BF)
    wide = values.astype(F32)
    square = jnp.sum(wide * wide, axis=0, keepdims=True)
    allowed = allowed_keys(ends_at(ends_ref, slot), x.shape[0])
    attn = attend(proj[:width], proj[width : 2 * width], values, allowed)
    return attn.T.astype(BF), values, square


def ends_rows(ends_ref, slot, shape):
    lane = lax.broadcasted_iota(jnp.int32, shape, 1)
    ends = ends_at(ends_ref, slot)
    return sum(jnp.where(lane == i, end, 0) for i, end in enumerate(ends)).astype(F32).astype(BF)


def square_rows(square, rows):
    parts = []
    for unused in range(3):
        parts.append(square.astype(BF).astype(F32))
        square = square - parts[-1]
    return jnp.concatenate(parts + [jnp.zeros((rows - 3, square.shape[1]), F32)], axis=0).astype(BF)


def attn_mate_kernel(ends_ref, x_ref, gain_ref, inward_ref, outward_ref, part_ref, values_ref, square_ref):
    attn, values, square = attend_forward(1, ends_ref, x_ref[...], gain_ref, inward_ref, None, None)
    values_ref[...] = values
    square_ref[...] = square
    part_ref[...] = dot_nn(attn, outward_ref[...]).astype(BF)


def attn_own_kernel(
    ends_ref,
    x_ref,
    gain_ref,
    inward_ref,
    outward_ref,
    mate_ref,
    values_mate_ref,
    part_ref,
    values_ref,
    square_ref,
    turned_ref,
):
    model = x_ref.shape[1]
    width = outward_ref.shape[0]
    attn, values, square = attend_forward(0, ends_ref, x_ref[...], gain_ref, inward_ref, None, None)
    part_ref[...] = dot_nn(attn, outward_ref[...]).astype(BF)
    values_ref[:width] = values
    values_ref[width:] = values_mate_ref[...]
    square_ref[...] = square
    for slot, ref in enumerate((x_ref, mate_ref)):
        turned_ref[slot, :model] = turned(ref[...])
        turned_ref[slot, model:] = ends_rows(ends_ref, slot, (turned_ref.shape[1] - model, turned_ref.shape[2]))


def attn_mixed_kernel(slot, ends_ref, levels_ref, x_ref, gain_ref, inward_ref, outward_ref, first_ref, *refs):
    part_ref, square_ref = refs[-2:]
    width = outward_ref.shape[0]
    attn, unused, square = attend_forward(
        slot,
        ends_ref,
        x_ref[...],
        gain_ref,
        inward_ref,
        mix_column(levels_ref),
        first_ref[slot * width : (slot + 1) * width],
    )
    part_ref[...] = dot_nn(attn, outward_ref[...]).astype(BF)
    if slot == 0:
        square_ref[...] = square
        return
    lower_ref, low_ref, own_ref, square_own_ref, square_low_own, square_low_mate = refs[:6]
    stack_ref = square_ref
    model = x_ref.shape[1]
    is_lower = lower_ref[0, 0] == 1
    square = jnp.where(is_lower, square_low_own[...] + square_low_mate[...], square + square_own_ref[...])
    rows = square_rows(square, stack_ref.shape[1] - model)
    stack_ref[0, model:] = rows
    stack_ref[1, model:] = jnp.zeros_like(rows)
    stack_ref[0, :model] = jnp.where(is_lower, low_ref[0], turned(own_ref[...]))
    stack_ref[1, :model] = jnp.where(is_lower, low_ref[1], turned(x_ref[...]))


def sum_kernel(a_ref, b_ref, out_ref):
    out_ref[...] = rounded_sum(a_ref[...], b_ref[...]).astype(BF)


def attn_sums(refs):
    own_ref, mate_ref, part_own_ref, part_mate_ref, got_own_ref, got_mate_ref = refs
    own = (own_ref[...].astype(F32) + rounded_sum(part_own_ref[...], got_own_ref[...])).astype(BF)
    mate = (mate_ref[...].astype(F32) + rounded_sum(part_mate_ref[...], got_mate_ref[...])).astype(BF)
    return own, mate


def feed_loads(inward_ref, outward_ref, inward, outward, sems):
    hidden = outward.shape[0]
    copies = [
        pltpu.make_async_copy(inward_ref.at[:, 0:hidden], inward.at[:, 0:hidden], sems.at[0]),
        pltpu.make_async_copy(inward_ref.at[:, hidden : 2 * hidden], inward.at[:, hidden : 2 * hidden], sems.at[1]),
        pltpu.make_async_copy(outward_ref, outward, sems.at[2]),
    ]
    for copy in copies:
        copy.start()
    return copies


def prefetch_kernel(a_ref, b_ref, *refs):
    a_out, b_out, sems = refs[-3:]
    copies = [
        pltpu.make_async_copy(a_ref, a_out, sems.at[0]),
        pltpu.make_async_copy(b_ref, b_out, sems.at[1]),
    ]
    for copy in copies:
        copy.start()
    for copy in copies:
        copy.wait()


def prefetched(a, b, after):
    any_spec, vmem_spec = pl.BlockSpec(memory_space=pl.ANY), pl.BlockSpec(memory_space=pltpu.VMEM)
    return pl.pallas_call(
        prefetch_kernel,
        in_specs=[any_spec] * (2 + len(after)),
        out_specs=[vmem_spec] * 2,
        out_shape=[pltpu.VMEM(a.shape, a.dtype), pltpu.VMEM(b.shape, b.dtype)],
        scratch_shapes=[pltpu.SemaphoreType.DMA((2,))],
        compiler_params=pltpu.CompilerParams(vmem_limit_bytes=MIB),
        cost_estimate=time_of(3.5),
        name="prefetch",
    )(in_hbm(a), in_hbm(b), *map(in_hbm, after))


def feed_first_kernel(*refs):
    gain_ref, inward_ref, outward_ref = refs[6:9]
    mid_own_ref, mid_mate_ref, stack_ref, send_own_ref, send_mate_ref = refs[9:]
    own, mate = attn_sums(refs[:6])
    count = own.shape[0]
    mid_own_ref[...] = own
    mid_mate_ref[...] = mate
    stack_ref[0] = turned(own)
    stack_ref[1] = turned(mate)
    stream = jnp.concatenate([own, mate], axis=0).astype(F32)
    normed, unused = normalize(stream, -1)
    act = (normed * gain_ref[...]).astype(BF)
    hidden = outward_ref.shape[0]
    gate = dot_nn(act, inward_ref[:, :hidden])
    up = dot_nn(act, inward_ref[:, hidden:])
    unused, silu = swish(gate, up)
    part = dot_nn((silu * up).astype(BF), outward_ref[...])
    send_own_ref[...] = (stream[:count] + part[:count]).astype(BF)
    send_mate_ref[...] = part[count:].astype(BF)


def feed_second_kernel(*refs):
    grad_own_ref, grad_mate_ref, gain_ref, inward_hbm, outward_hbm = refs[6:11]
    part_own_ref, part_mate_ref, mid_own_ref, mid_mate_ref, turned_ref, out_own_ref, out_mate_ref = refs[11:18]
    inward_ref, outward_ref, sems = refs[18:]
    loads = feed_loads(inward_hbm, outward_hbm, inward_ref, outward_ref, sems)
    own, mate = attn_sums(refs[:6])
    count = own.shape[0]
    mid_own_ref[...] = own
    mid_mate_ref[...] = mate
    turned_ref[...] = turned(own)
    stream = jnp.concatenate([own, mate], axis=0).astype(F32)
    grad = jnp.concatenate([grad_own_ref[...], grad_mate_ref[...]], axis=0)
    normed, unused = normalize(stream, -1)
    act = (normed * gain_ref[...]).astype(BF)
    hidden = outward_ref.shape[0]
    loads[0].wait()
    gate = dot_nn(act, inward_ref[:, :hidden])
    loads[1].wait()
    up = dot_nn(act, inward_ref[:, hidden:])
    loads[2].wait()
    dhid = dot_nt(grad, outward_ref[...])
    hid, dgate, dup = feed_back(gate, up, dhid)
    dact = dot_nt(dgate, inward_ref[:, :hidden]) + dot_nt(dup, inward_ref[:, hidden:])
    part_own_ref[...] = dact[:count].astype(BF)
    part_mate_ref[...] = dact[count:].astype(BF)
    part = dot_nn(hid, outward_ref[...])
    out_own_ref[...] = (stream[:count] + part[:count]).astype(BF)
    out_mate_ref[...] = part[count:].astype(BF)


def feed_first_back_kernel(
    own_ref,
    mate_ref,
    grad_own_ref,
    grad_mate_ref,
    gain_ref,
    inward_hbm,
    outward_hbm,
    part_own_ref,
    part_mate_ref,
    inward_ref,
    outward_ref,
    sems,
):
    loads = feed_loads(inward_hbm, outward_hbm, inward_ref, outward_ref, sems)
    count = own_ref.shape[0]
    stream = jnp.concatenate([own_ref[...], mate_ref[...]], axis=0).astype(F32)
    grad = jnp.concatenate([turned(grad_own_ref[...]), turned(grad_mate_ref[...])], axis=0)
    normed, unused = normalize(stream, -1)
    act = (normed * gain_ref[...]).astype(BF)
    hidden = outward_ref.shape[0]
    loads[0].wait()
    gate = dot_nn(act, inward_ref[:, :hidden])
    loads[1].wait()
    up = dot_nn(act, inward_ref[:, hidden:])
    loads[2].wait()
    dhid = dot_nt(grad, outward_ref[...])
    unused, dgate, dup = feed_back(gate, up, dhid)
    dact = dot_nt(dgate, inward_ref[:, :hidden]) + dot_nt(dup, inward_ref[:, hidden:])
    part_own_ref[...] = dact[:count].astype(BF)
    part_mate_ref[...] = dact[count:].astype(BF)


def middle_grads(refs, gain_ref, turned_grads):
    for s_ref, g_ref, p_ref, r_ref in zip(*refs):
        grad = g_ref[...].astype(F32)
        grad = norm_back(
            s_ref[...].astype(F32),
            grad.T if turned_grads else grad,
            rounded_sum(p_ref[...], r_ref[...]),
            gain_ref[...],
        )
        yield grad.astype(BF)


def middle_first_back_kernel(lower_ref, *refs):
    gain_ref, grad_high_ref, dfirst_ref, first_ref = refs[8:12]
    out_own_ref, out_mate_ref, last_ref = refs[12:]
    pairs = refs[0:2], refs[2:4], refs[4:6], refs[6:8]
    own, mate = middle_grads(pairs, gain_ref, True)
    out_own_ref[...] = own
    out_mate_ref[...] = mate
    model = own.shape[1]
    is_lower = lower_ref[0] == 1
    last_ref[:model] = jnp.where(is_lower, turned(own), grad_high_ref[0])
    last_ref[model : 2 * model] = jnp.where(is_lower, turned(mate), grad_high_ref[1])
    last_ref[2 * model :] = jnp.where(is_lower, dfirst_ref[...], first_ref[...])


def middle_second_back_kernel(*refs):
    gain_ref, out_own_ref, out_mate_ref, turned_ref = refs[8:]
    pairs = refs[0:2], refs[2:4], refs[4:6], refs[6:8]
    own, mate = middle_grads(pairs, gain_ref, False)
    out_own_ref[...] = own
    out_mate_ref[...] = mate
    turned_ref[0] = turned(own)
    turned_ref[1] = turned(mate)


def attn_back_kernel(mixing, slot, *refs):
    ends_ref, levels_ref, grad_ref, x_ref, gain_ref, inward_ref, outward_ref, first_ref = refs[:8]
    count = x_ref.shape[0]
    width = outward_ref.shape[0]
    first = first_ref[slot * width : (slot + 1) * width].astype(F32)
    normed, unused = normalize(x_ref[...].astype(F32), -1)
    act = (normed * gain_ref[...]).astype(BF)
    allowed = allowed_keys(ends_at(ends_ref, slot), count)
    dattn = dot_nt(grad_ref[...], outward_ref[...]).T.astype(BF)
    proj = dot_nn(act, inward_ref[...]).T.astype(BF)
    values = proj[2 * width :]
    if mixing:
        mix = mix_column(levels_ref)
        values = ((1.0 - mix) * values.astype(F32) + mix * first).astype(BF)
    dquery, dkeys, dmixed, unused = attend_back(proj[:width], proj[width : 2 * width], values, dattn, allowed)
    if mixing:
        dfirst = (mix * dmixed).astype(BF)
        dvalues = (1.0 - mix) * dmixed
        if slot == 1:
            refs[-1][...] = dfirst
        else:
            refs[-1][:width] = dfirst
            refs[-1][width:] = refs[8][...]
    else:
        dvalues = dmixed + first
    dproj = jnp.concatenate([dquery, dkeys, dvalues], axis=0).T.astype(BF)
    dact = dot_nt(dproj, inward_ref[...])
    if mixing:
        refs[-2][...] = dact.astype(BF)
    else:
        grad = 0.0 if slot else grad_ref[...].astype(F32)
        refs[-1][...] = norm_back(x_ref[...].astype(F32), grad, dact, gain_ref[...]).astype(BF)


def input_back_kernel(x_ref, grad_ref, part_ref, got_ref, gain_ref, out_ref):
    grad = norm_back(
        x_ref[...].astype(F32),
        grad_ref[...].astype(F32),
        rounded_sum(part_ref[...], got_ref[...]),
        gain_ref[...],
    )
    out_ref[...] = grad.T.astype(BF)


def split_kernel(place_ref, a_own_ref, a_mate_ref, b_own_ref, b_mate_ref, row_ref, *refs):
    count, piece = a_own_ref.shape[0], refs[0].shape[1]
    for mask, ref in enumerate(refs):
        columns = aligned(place_ref[mask] * piece, piece)
        for i, source in enumerate((a_own_ref, a_mate_ref, b_own_ref, b_mate_ref)):
            ref[i * count : (i + 1) * count] = source[:, columns]
        row = jnp.concatenate([row_ref[...], jnp.zeros((1, piece - row_ref.shape[1]), F32)], axis=1)
        ref[4 * count :] = square_rows(row, ref.shape[0] - 4 * count)


def join_kernel(flags_ref, own_ref, beside_ref, over_ref, across_ref, a_ref, b_ref, row_ref):
    count = a_ref.shape[0] // 2
    lower, even = flags_ref[0] == 1, flags_ref[1] == 1
    for first, out_ref, holds in ((0, a_ref, lower), (2 * count, b_ref, jnp.logical_not(lower))):
        rows = slice(first, first + 2 * count)
        same = jnp.where(holds, own_ref[rows], over_ref[rows]).astype(F32)
        other = jnp.where(holds, beside_ref[rows], across_ref[rows]).astype(F32)
        own, mate = same[:count] + other[count:], same[count:] + other[:count]
        out_ref[:count] = jnp.where(even, own, mate).astype(out_ref.dtype)
        out_ref[count:] = jnp.where(even, mate, own).astype(out_ref.dtype)
    lanes = row_ref.shape[1]
    rows = [r[4 * count :, :lanes].astype(F32) for r in (own_ref, beside_ref, over_ref, across_ref)]
    row_ref[...] = jnp.sum(sum(rows), axis=0, keepdims=True)


def late_kernel(lower_ref, low_ref, high_ref, out_ref):
    out_ref[...] = jnp.where(lower_ref[0] == 1, low_ref[...], high_ref[...])


def square_sum_kernel(lower_ref, rows_ref, out_ref):
    total = jnp.sum(rows_ref[...].astype(F32))
    lane = lax.broadcasted_iota(jnp.int32, out_ref.shape, 1)
    out_ref[...] = jnp.where(lane == 1 - lower_ref[0], total, 0.0)


def add_kernel(a_ref, b_ref, out_ref):
    out_ref[...] = a_ref[...] + b_ref[...]


def call(kernel, outs, *args, smem=0, name=None, after=(), vmem=16, loads=(), free=()):
    whole = len(args)
    held = {id(w) for w in loads}
    either = {id(a) for a in free}

    def run(*refs):
        kernel(*refs[:whole], *refs[whole + len(after) :])

    def whole_block(a):
        return pl.BlockSpec(a.shape, lambda i: (0,) * len(a.shape))

    def given_spec(a):
        if id(a) in held:
            return pl.BlockSpec(memory_space=pl.ANY)
        return pl.BlockSpec(memory_space=pltpu.VMEM) if a.size >= WEIGHTS_FROM else whole_block(a)

    return pl.pallas_call(
        run,
        grid=(1,),
        out_shape=made_in_hbm(outs),
        in_specs=[pl.BlockSpec(memory_space=pltpu.SMEM)] * smem
        + [given_spec(a) for a in args[smem:]]
        + [pl.BlockSpec(memory_space=pl.ANY)] * len(after),
        out_specs=[whole_block(o) for o in outs],
        scratch_shapes=[pltpu.VMEM(w.shape, w.dtype) for w in loads]
        + [pltpu.SemaphoreType.DMA((1 + len(loads),))] * bool(loads),
        compiler_params=pltpu.CompilerParams(vmem_limit_bytes=vmem * MIB),
        cost_estimate=time_of(TIMES.get(name, 1.0)),
        name=name,
    )(*args[:smem], *[a if id(a) in either or a.size >= WEIGHTS_FROM and id(a) not in held else in_hbm(a) for a in args[smem:]], *[a if id(a) in either else in_hbm(a) for a in after])


def gate(array, after):
    spec = pl.BlockSpec(memory_space=pl.ANY)
    return pl.pallas_call(
        lambda *refs: None,
        out_shape=pltpu.HBM(array.shape, array.dtype),
        in_specs=[spec] * (1 + len(after)),
        out_specs=spec,
        input_output_aliases={0: 0},
        compiler_params=pltpu.CompilerParams(vmem_limit_bytes=MIB),
        cost_estimate=time_of(0.1),
        name="gate",
    )(in_hbm(array), *map(in_hbm, after))


class Share:
    def __init__(self, core, segment):
        self.segment = segment
        self.own = -(-segment // 256) * 128
        self.other = segment - self.own
        self.common = 2 * self.own - segment
        self.place = core * (segment - self.own)
        self.other_source = (1 - core) * self.common
        self.other_place = (1 - core) * self.own


def aligned(start, size, unit=128):
    return pl.ds(pl.multiple_of(start, unit), size)


def block_ref(refs, block, rows, shift=0):
    operand, index, first = block[:3]
    ref = refs[operand]
    for i in index:
        ref = ref.at[i]
    return ref.at[aligned(first + shift, rows), :]


def fetch(pick_ref, refs, choices, target, sems, shift=0):
    for which, blocks in enumerate(choices):

        @pl.when(pick_ref[0] == which)
        def _():
            for at, block in enumerate(blocks):
                source = block_ref(refs, block, target.shape[0], shift)
                count = source.shape[1]
                if block[3] is not None:
                    plane, other, slot = block[3]
                    core = 1 - pick_ref[1] if other else pick_ref[1]
                    at = (2 * plane + core) * 2 + slot
                columns = aligned(at * count, count)
                pltpu.make_async_copy(source, target.at[:, columns], sems.at[at]).start()


def arrived(refs, choices, target, sems, at):
    source = block_ref(refs, choices[0][0], target.shape[0])
    count = source.shape[1]
    pltpu.make_async_copy(source, target.at[:, aligned(at * count, count)], sems.at[at]).wait()


def weight_copies(share, inward_ref, outward_ref, plain_ref, inward, outward, plain, sems):
    own = share.own
    first, last = [(outward_ref.at[aligned(share.place, own), :], outward)], []
    for s in range(inward.shape[0] // own):
        place = aligned(s * share.segment + share.place, own)
        here = slice(s * own, (s + 1) * own)
        first.append((inward_ref.at[place, :], inward.at[here, :]))
        last.append((plain_ref.at[:, place], plain.at[:, here]))
    copies = [pltpu.make_async_copy(a, b, sems.at[i]) for i, (a, b) in enumerate(first + last)]
    return copies[: len(first)], copies[len(first) :]


def products(share, core, left, right, plain, refs):
    whole_ref, low_ref, dots_ref, stage, low_stage, dots, dots_row, sems = refs
    size, lanes = stage.shape[2], dots.shape[1]
    each = share.own // size
    steps = right.shape[0] // size

    def copies(step, slot):
        place = lax.div(step, each) * share.segment + share.place + lax.rem(step, each) * size
        columns = aligned(place, size)
        yield pltpu.make_async_copy(stage.at[slot], whole_ref.at[0, :, columns], sems.at[slot, 0])
        yield pltpu.make_async_copy(low_stage.at[slot], low_ref.at[:, aligned(step * size, size)], sems.at[slot, 1])

    dots[...] = jnp.zeros_like(dots)

    def one(step, unused):
        slot = lax.rem(step, 2)
        here = aligned(step * size, size)

        @pl.when(step >= 2)
        def _():
            for copy in copies(step, slot):
                copy.wait()

        value = dot_nt(left[...], right[here, :])
        stage[slot] = value
        low_stage[slot] = value.astype(BF)
        value = value * plain[:, here].astype(F32)
        total = 0.0
        for at in range(0, size, lanes):
            part = value[:, at : at + lanes]
            if at < share.common:
                part = jnp.where((core == 0) | (lax.rem(step, each) > 0), part, 0.0)
            total = total + part
        dots[...] += total
        for copy in copies(step, slot):
            copy.start()
        return 0

    lax.fori_loop(0, steps, one, 0)
    dots_row[...] = jnp.sum(dots[...].T, axis=0, keepdims=True)
    save = pltpu.make_async_copy(dots_row, dots_ref, sems.at[0, 2])
    save.start()
    return [save] + [copy for step in range(max(steps - 2, 0), steps) for copy in copies(step, step % 2)]


def outward_products(share, left, right, refs):
    whole_ref, low_ref, stage, low_stage, sems = refs
    value = dot_nt(left[...], right[...])
    stage[...] = value
    low_stage[...] = value.astype(BF)
    copies = [
        pltpu.make_async_copy(stage, whole_ref.at[0, aligned(share.place, share.own), :], sems.at[0]),
        pltpu.make_async_copy(low_stage, low_ref, sems.at[1]),
    ]
    for copy in copies:
        copy.start()
    return copies


def feed_weights_kernel(layout, *refs):
    (streams, grads), operands = layout
    pick_ref = refs[0]
    blocks_refs = refs[1 : 1 + operands]
    gain_ref, inward_ref, outward_ref, plain_ref = refs[1 + operands : 5 + operands]
    outs, scratch = refs[5 + operands : 10 + operands], refs[10 + operands :]
    act_all, grad_all, hid_all, dboth_all, inward, outward, plain = scratch[:7]
    stage, low_stage, dots, dots_row, out_stage, out_low, sems, weight_sems, out_sems = scratch[7:]
    core = pick_ref[1]
    share = Share(core, outward_ref.shape[0])
    hidden = share.own
    weights, plain_copies = weight_copies(
        share, inward_ref, outward_ref, plain_ref, inward, outward, plain, weight_sems
    )
    for copy in weights:
        copy.start()
    for copy in weights:
        copy.wait()
    fetch(pick_ref, blocks_refs, streams, act_all, sems.at[0])
    fetch(pick_ref, blocks_refs, grads, grad_all, sems.at[1])
    for copy in plain_copies:
        copy.start()
    blocks = len(streams[0])
    wider = 2 * (act_all.shape[1] // blocks)

    gain = column_of(gain_ref)

    def rows(step, unused):
        for at in (2 * step, 2 * step + 1):
            arrived(blocks_refs, streams, act_all, sems.at[0], at)
            arrived(blocks_refs, grads, grad_all, sems.at[1], at)
        here = aligned(step * wider, wider)
        normed, unused = normalize(act_all[:, here].astype(F32), 0)
        act = (normed * gain).astype(BF)
        act_all[:, here] = act
        for at in range(0, hidden, 384):
            to = slice(at, at + 384)
            up_to = slice(hidden + at, hidden + at + 384)
            gate, up = dot_nn(inward[to, :], act), dot_nn(inward[up_to, :], act)
            dhid = dot_nn(outward[to, :], grad_all[:, here])
            hid_all[to, here], dboth_all[to, here], dboth_all[up_to, here] = feed_back(gate, up, dhid)
        return 0

    lax.fori_loop(0, blocks // 2, rows, 0)
    for copy in plain_copies:
        copy.wait()
    copies = outward_products(share, hid_all, grad_all, (outs[1], outs[3], out_stage, out_low, out_sems.at[2]))
    copies += products(
        share, core, act_all, dboth_all, plain, (outs[0], outs[2], outs[4], stage, low_stage, dots, dots_row, out_sems)
    )
    for copy in copies:
        copy.wait()


def attn_scores_kernel(layout, *refs):
    (streams,), operands = layout
    pick_ref, ends_ref = refs[:2]
    blocks_refs = refs[2 : 2 + operands]
    gain_ref, inward_ref = refs[2 + operands : 4 + operands]
    outs, scratch = refs[4 + operands : 7 + operands], refs[7 + operands :]
    act_all, proj_all, probs_all, inward, sems, weight_sems, out_sems = scratch
    own = inward.shape[0] // 3
    share = Share(pick_ref[1], inward_ref.shape[0] // 3)
    copies = []
    for s in range(3):
        place = aligned(s * share.segment + share.place, own)
        copies.append(
            pltpu.make_async_copy(inward_ref.at[place, :], inward.at[s * own : (s + 1) * own, :], weight_sems.at[s])
        )
    for copy in copies:
        copy.start()
    for copy in copies:
        copy.wait()
    fetch(pick_ref, blocks_refs, streams, act_all, sems)
    blocks = len(streams[0])
    count = act_all.shape[1] // blocks
    each = 4
    wider = each * count

    def saves(step):
        here = aligned(step * wider, wider)
        for i, (source, target) in enumerate(zip((act_all, proj_all, probs_all), outs)):
            yield pltpu.make_async_copy(source.at[:, here], target.at[:, here], out_sems.at[i, step])

    gain = column_of(gain_ref)

    def rows(step, unused):
        for at in [each * step + i for i in range(each)]:
            arrived(blocks_refs, streams, act_all, sems, at)
        here = aligned(step * wider, wider)
        normed, unused = normalize(act_all[:, here].astype(F32), 0)
        act = (normed * gain).astype(BF)
        act_all[:, here] = act
        proj = dot_nn(inward[...], act).astype(BF)
        proj_all[:, here] = proj
        for i in range(each):
            cols = slice(i * count, (i + 1) * count)
            allowed = allowed_keys(ends_at(ends_ref, step * each + i), count)
            query, keys = heads_of(proj[:own, cols]), heads_of(proj[own : 2 * own, cols])
            scores = [dot_tn(k, q) for q, k in zip(query, keys)]
            probs = [softmax_keys(s, allowed).astype(BF) for s in scores]
            probs_all[:, aligned(step * wider + i * count, count)] = jnp.concatenate(probs, axis=0)
        for copy in saves(step):
            copy.start()
        return 0

    lax.fori_loop(0, blocks // each, rows, 0)
    for step in range(blocks // each):
        for copy in saves(step):
            copy.wait()


def attn_scores(smem, streams, gain, inward, model, after):
    arrays, layout = gather_layout((streams,))
    segment = inward.shape[0] // 3
    own = Share(0, segment).own
    blocks = len(layout[0][0])
    count = arrays[0].shape[-1]
    total = blocks * count
    shapes = [(model, total), (3 * own, total), (own // HEAD_DIM * count, total)]
    layout = (layout, len(arrays))
    whole = len(smem) + len(arrays) + 2

    def run(*refs):
        attn_scores_kernel(layout, *refs[:whole], *refs[whole + len(after) :])

    any_spec, vmem_spec = pl.BlockSpec(memory_space=pl.ANY), pl.BlockSpec(memory_space=pltpu.VMEM)
    return pl.pallas_call(
        run,
        in_specs=[pl.BlockSpec(memory_space=pltpu.SMEM)] * len(smem)
        + [any_spec] * len(arrays)
        + [vmem_spec, any_spec]
        + [any_spec] * len(after),
        out_specs=[any_spec] * 3,
        out_shape=made_in_hbm([shape_of(s, BF) for s in shapes]),
        scratch_shapes=[pltpu.VMEM(s, BF) for s in shapes]
        + [
            pltpu.VMEM((3 * own, model), BF),
            pltpu.SemaphoreType.DMA((blocks,)),
            pltpu.SemaphoreType.DMA((3,)),
            pltpu.SemaphoreType.DMA((3, blocks // 4)),
        ],
        compiler_params=pltpu.CompilerParams(vmem_limit_bytes=24 * MIB),
        cost_estimate=time_of(14.0),
        name="attn_scores",
    )(*smem, *map(in_hbm, arrays), gain, in_hbm(inward), *map(in_hbm, after))


def attn_weights_kernel(layout, *refs):
    (grads, firsts), operands = layout
    pick_ref, level_ref = refs[:2]
    blocks_refs = refs[2 : 2 + operands]
    act_ref, proj_ref, probs_ref, outward_ref, plain_ref = refs[2 + operands : 7 + operands]
    outs, scratch = refs[7 + operands : 12 + operands], refs[12 + operands :]
    act_all, grad_all, attn_all, dproj_all, outward, plain = scratch[:6]
    stage, low_stage, dots, dots_row, out_stage, out_low, first_all, proj_all, probs_all = scratch[6:15]
    sems, weight_sems, kept_sems, out_sems = scratch[15:]
    core = pick_ref[1]
    share = Share(core, outward_ref.shape[0])
    width = share.own
    load = pltpu.make_async_copy(outward_ref.at[aligned(share.place, width), :], outward, weight_sems.at[0])
    load.start()
    fetch(pick_ref, blocks_refs, grads, grad_all, sems.at[0])
    fetch(pick_ref, blocks_refs, firsts, first_all, sems.at[1], share.place)
    blocks = len(grads[0])
    count = act_all.shape[1] // blocks
    each = 4
    wider = each * count

    def kept(step):
        here = aligned(step * wider, wider)
        for i, (source, target) in enumerate(((proj_ref, proj_all), (probs_ref, probs_all), (act_ref, act_all))):
            yield pltpu.make_async_copy(source.at[:, here], target.at[:, here], kept_sems.at[i, step])

    for step in range(blocks // each):
        for copy in kept(step):
            copy.start()
    plain_copies = []
    for s in range(3):
        place = aligned(s * share.segment + share.place, width)
        here = slice(s * width, (s + 1) * width)
        plain_copies.append(
            pltpu.make_async_copy(plain_ref.at[:, place], plain.at[:, here], weight_sems.at[1 + s])
        )
    for copy in plain_copies:
        copy.start()
    load.wait()

    upper = pick_ref[0].astype(F32)
    heads = width // HEAD_DIM
    first_head = pick_ref[3] * (share.segment // HEAD_DIM) + core * (share.segment - width) // HEAD_DIM
    levels = [level_ref[first_head + i].astype(F32) / 8.0 * upper for i in range(heads)]
    mix = jnp.concatenate([jnp.full((HEAD_DIM, 1), level, F32) for level in levels], axis=0)

    def rows(step, unused):
        for at in [each * step + i for i in range(each)]:
            arrived(blocks_refs, grads, grad_all, sems.at[0], at)
            arrived(blocks_refs, firsts, first_all, sems.at[1], at)
        for copy in kept(step):
            copy.wait()
        here = aligned(step * wider, wider)
        proj = proj_all[:, here]
        dattn = dot_nn(outward[...], grad_all[:, here]).astype(BF)
        first = first_all[:, here].astype(F32)
        values = ((1.0 - mix) * proj[2 * width :].astype(F32) + mix * first).astype(BF)
        for i in range(each):
            cols = slice(i * count, (i + 1) * count)
            place = aligned(step * wider + i * count, count)
            probs = probs_all[:, place]
            dquery, dkeys, dmixed, attn = attend_back_from(
                proj[:width, cols],
                proj[width : 2 * width, cols],
                values[:, cols],
                dattn[:, cols],
                lambda: [probs[at : at + count] for at in range(0, probs.shape[0], count)],
                True,
            )
            dvalues = (1.0 - mix) * dmixed + (1.0 - upper) * first[:, cols]
            attn_all[:, place] = attn.astype(BF)
            dproj_all[:, place] = jnp.concatenate([dquery, dkeys, dvalues], axis=0).astype(BF)
        return 0

    lax.fori_loop(0, blocks // each, rows, 0)
    for copy in plain_copies:
        copy.wait()
    copies = outward_products(share, attn_all, grad_all, (outs[1], outs[3], out_stage, out_low, out_sems.at[2]))
    copies += products(
        share, core, act_all, dproj_all, plain, (outs[0], outs[2], outs[4], stage, low_stage, dots, dots_row, out_sems)
    )
    for copy in copies:
        copy.wait()


def gather_layout(sets):
    arrays, layout = [], []
    for choices in sets:
        placed = []
        for blocks in choices:
            row = []
            for array, index, first, where in blocks:
                at = next((i for i, a in enumerate(arrays) if a is array), None)
                if at is None:
                    at = len(arrays)
                    arrays.append(array)
                row.append((at, index, first, where))
            placed.append(tuple(row))
        layout.append(tuple(placed))
    return arrays, tuple(layout)


def weight_call(kernel, smem, sets, kept, small, weights, name, after=()):
    arrays, layout = gather_layout(sets)
    *turned_in, outward, plain = weights
    segment, model = outward.shape
    segments = plain.shape[1] // segment
    own = Share(0, segment).own
    blocks = len(layout[0][0])
    total = blocks * arrays[0].shape[-1]
    block = 256
    whole = len(smem) + len(arrays) + len(kept) + len(small) + len(weights)
    layout = (layout, len(arrays))

    def run(*refs):
        kernel(layout, *refs[:whole], *refs[whole + len(after) :])

    any_spec, vmem_spec = pl.BlockSpec(memory_space=pl.ANY), pl.BlockSpec(memory_space=pltpu.VMEM)
    scratch = [
        pltpu.VMEM((model, total), BF),
        pltpu.VMEM((model, total), BF),
        pltpu.VMEM((own, total), BF),
        pltpu.VMEM((segments * own, total), BF),
    ]
    scratch += [pltpu.VMEM((segments * own, model), BF)] * len(turned_in)
    scratch += [
        pltpu.VMEM((own, model), BF),
        pltpu.VMEM((model, segments * own), BF),
        pltpu.VMEM((2, model, block), F32),
        pltpu.VMEM((2, model, block), BF),
        pltpu.VMEM((model, 128), F32),
        pltpu.VMEM((1, model), F32),
        pltpu.VMEM((own, model), F32),
        pltpu.VMEM((own, model), BF),
    ]
    if kept:
        scratch += [pltpu.VMEM((own, total), BF)] + [pltpu.VMEM(a.shape, BF) for a in kept[1:]]
    scratch += [
        pltpu.SemaphoreType.DMA((len(sets), blocks)),
        pltpu.SemaphoreType.DMA((2 * segments + 1,)),
    ]
    if kept:
        scratch += [pltpu.SemaphoreType.DMA((3, blocks // 4))]
    scratch += [pltpu.SemaphoreType.DMA((3, 3))]
    return pl.pallas_call(
        run,
        in_specs=[pl.BlockSpec(memory_space=pltpu.SMEM)] * len(smem)
        + [any_spec] * (len(arrays) + len(kept))
        + [vmem_spec] * len(small)
        + [any_spec] * (len(weights) + len(after)),
        out_specs=[any_spec] * 5,
        out_shape=made_in_hbm(
            [
                shape_of((1, model, segments * segment), F32),
                shape_of((1,) + outward.shape, F32),
                shape_of((model, segments * own), BF),
                shape_of((own, model), BF),
                shape_of((1, model), F32),
            ]
        ),
        scratch_shapes=scratch,
        compiler_params=pltpu.CompilerParams(vmem_limit_bytes=56 * MIB),
        cost_estimate=time_of(27.0),
        name=name,
    )(*smem, *map(in_hbm, arrays), *map(in_hbm, kept), *small, *map(in_hbm, weights), *map(in_hbm, after))


def fill_kernel(segment, core_ref, low, out_low, unused_ref, unused_out_ref, *refs):
    whole_ref, whole_out_ref, stage, out_stage, sems = refs
    share = Share(core_ref[0], segment)
    own, other, size = share.own, share.other, stage.shape[1]
    segments = low.shape[1] // own
    writes = []
    for block in range(stage.shape[0]):
        rows = slice(block * size, (block + 1) * size)
        for s in range(segments):
            here = slice(s * other, (s + 1) * other)
            stage[block, :, here] = low[rows, aligned(s * own + share.other_source, other)].astype(F32)
            place = aligned(s * segment + share.other_place, other)
            copy = pltpu.make_async_copy(
                stage.at[block, :, here], whole_ref.at[0, rows, place], sems.at[block, s]
            )
            copy.start()
            writes.append(copy)
    out_stage[...] = out_low[aligned(share.other_source, other), :].astype(F32)
    copy = pltpu.make_async_copy(
        out_stage, whole_out_ref.at[0, aligned(share.other_place, other), :], sems.at[0, segments]
    )
    copy.start()
    for copy in writes + [copy]:
        copy.wait()


def filled(core, low, out_low, whole, whole_out, after=()):
    segment, model = whole_out.shape[1:]
    segments = whole.shape[2] // segment
    share = Share(0, segment)
    steps = 4
    any_spec = pl.BlockSpec(memory_space=pl.ANY)

    def run(*refs):
        fill_kernel(segment, *refs[:5], *refs[5 + len(after) :])

    return pl.pallas_call(
        run,
        in_specs=[pl.BlockSpec(memory_space=pltpu.SMEM)]
        + [pl.BlockSpec(memory_space=pltpu.VMEM)] * 2
        + [any_spec] * (2 + len(after)),
        out_specs=[any_spec] * 2,
        out_shape=made_in_hbm([whole, whole_out]),
        input_output_aliases={3: 0, 4: 1},
        scratch_shapes=[
            pltpu.VMEM((steps, model // steps, segments * share.other), F32),
            pltpu.VMEM((share.other, model), F32),
            pltpu.SemaphoreType.DMA((steps, segments + 1)),
        ],
        compiler_params=pltpu.CompilerParams(vmem_limit_bytes=32 * MIB),
        cost_estimate=time_of(5.0),
        name="fill",
    )(core, low, out_low, in_hbm(whole), in_hbm(whole_out), *map(in_hbm, after))


def body(tokens, cotangent, gains, attn_in, attn_out, ffn_in, ffn_out, mix_level, seq_lengths):
    section = lax.axis_index("section")
    core = lax.axis_index("dp") % 2
    lower = section < 2
    even = section % 2 == 0
    sections = lax.axis_size("section")
    dp = lax.axis_size("dp")
    group = min(dp, GROUP)
    planes = group // 2
    micro = seq_lengths.shape[0]
    count = tokens.shape[0] // micro
    piece = tokens.shape[1]
    inward, outward, feed_in, feed_out = attn_in[0], attn_out[0], ffn_in[0], ffn_out[0]
    model = inward.shape[0]
    width = outward.shape[0]

    low, high = (0, 1), (2, 3)
    everyone = low + high

    def send(x, mask, sources=everyone):
        return lax.ppermute(x, "section", [(i, i ^ mask) for i in sources])

    def planes_of(x, sources=everyone):
        def plane(by):
            pairs = [
                (s * dp + i, s * dp + i // group * group + (i % group // 2 + by) % planes * 2 + i % 2)
                for s in sources
                for i in range(dp)
            ]
            return lax.ppermute(x, ("section", "dp"), pairs)

        return [plane(by) for by in range(1, planes)]

    def other_core(x, sources=everyone):
        pairs = [(s * dp + i, s * dp + (i ^ 1)) for s in sources for i in range(dp)]
        return lax.ppermute(x, ("section", "dp"), pairs)

    near = jnp.where(lower, tokens, cotangent)
    far = jnp.where(lower, cotangent, tokens)
    got_far, got_across, got_near = send(far, 2), send(far, 3), send(near, 1)
    got_gains = send(gains, 1)
    ends = jnp.cumsum(seq_lengths, axis=1)
    ends = jnp.where(even, ends, ends[::-1])

    def by_half(mine, other):
        return [jnp.where(even, mine, other), jnp.where(even, other, mine)]

    ours, theirs = by_half(near, got_near), by_half(got_far, got_across)
    given = jnp.concatenate(
        [jnp.where(lower, a, b) for a, b in zip(ours + theirs, theirs + ours)], axis=1
    )
    top, bottom = given[:count], given[count:]
    given_own, given_mate = jnp.where(even, top, bottom), jnp.where(even, bottom, top)

    gain_attn = jnp.where(even, gains, got_gains)
    gain_feed = jnp.where(even, got_gains, gains)
    own_heads = width // HEAD_DIM
    levels = jnp.where(even, mix_level[:own_heads], mix_level[own_heads:])

    slot = shape_of((count, model), BF)
    half_turned = shape_of((width, count), BF)
    pair_half_turned = shape_of((2 * width, count), BF)
    slot_turned = shape_of((model, count), BF)
    pair_turned = shape_of((2, model, count), BF)
    pair_and_rows = shape_of((2, model + 16, count), BF)
    square_row = shape_of((1, count), F32)
    is_lower = lower.astype(jnp.int32)[None]

    attn_call = functools.partial(call, smem=1)
    attn_weights_early = prefetched(inward, outward, ())
    part_mate, first_mate, square_mate = attn_call(
        attn_mate_kernel,
        [slot, half_turned, square_row],
        ends,
        given_mate,
        gain_attn,
        *attn_weights_early,
        name="attn_mate",
    )
    got_own = send(part_mate, 1, low)
    part_own, first_both, square_own, given_stack = attn_call(
        attn_own_kernel,
        [slot, pair_half_turned, square_row, pair_and_rows],
        ends,
        given_own,
        gain_attn,
        *attn_weights_early,
        given_mate,
        first_mate,
        name="attn_own",
    )
    got_mate = send(part_own, 1, low)
    first_over = send(first_both, 2, low)
    square0 = square_own, square_mate
    mid0_own, mid0_mate, mid0_stack, send_own, send_mate = call(
        feed_first_kernel,
        [slot, slot, pair_turned, slot, slot],
        given_own,
        given_mate,
        part_own,
        part_mate,
        got_own,
        got_mate,
        gain_feed,
        *prefetched(feed_in, feed_out, (part_own,)),
        vmem=20,
        free=(first_over,),
        name="feed_first",
        after=(first_over,),
    )
    x_a, x_b = send(send_own, 2, low), send(send_mate, 3, low)
    feed_in_turned, inward_turned = call(
        turn_kernel,
        [shape_of(feed_in.shape[::-1], BF), shape_of(inward.shape[::-1], BF)],
        feed_in,
        inward,
        vmem=32,
        name="turn_weights",
        after=(send_own,),
    )

    x1_own = call(sum_kernel, [slot], x_a, x_b, name="sum", after=(inward_turned,), free=(x_a, x_b))[0]
    x1_mate = send(x1_own, 1, high)

    def attn_mixed(which, x, out, *more):
        return call(
            functools.partial(attn_mixed_kernel, which),
            [slot, out],
            ends,
            levels,
            x,
            gain_attn,
            inward,
            outward,
            first_over,
            *more,
            smem=2,
            name="attn_mixed",
            free=(first_over,),
        )

    part_own, square_own = attn_mixed(0, x1_own, square_row)
    got_mate = send(part_own, 1, high)
    part_mate, middle_stack = attn_mixed(
        1,
        x1_mate,
        pair_and_rows,
        jnp.full((1, count), is_lower[0], jnp.int32),
        mid0_stack,
        x1_own,
        square_own,
        *square0,
    )
    got_own = send(part_mate, 1, high)
    def everywhere(x):
        groups = [list(range(at, at + group)) for at in range(0, dp, group)]
        return lax.all_gather(x, "dp", axis=0, axis_index_groups=groups)

    def gathered(stack):
        every = everywhere(stack)
        return every, [(every, (d, i), 0, None) for d in range(group) for i in range(2)]

    def own_gathered(own, after):
        same_core = [
            [at + 2 * z + c for z in range(planes)] for at in range(0, dp, group) for c in range(2)
        ]
        every = gate(lax.all_gather(own, "dp", axis=0, axis_index_groups=same_core), after)
        return every, send(every, 1)

    def own_blocks(every, mate):
        arrays = ((every, False, 0), (other_core(every), True, 0), (mate, False, 1), (other_core(mate), True, 1))
        return [(a, (z,), 0, (z, other, i)) for a, other, i in arrays for z in range(planes)]

    all_given, set_given = gathered(given_stack)
    all_middle, set_middle = gathered(middle_stack)
    part_own, part_mate, mid1_own, mid1_mate, mid1_turned, out_own, out_mate = call(
        feed_second_kernel,
        [slot, slot, slot, slot, slot_turned, slot, slot],
        x1_own,
        x1_mate,
        part_own,
        part_mate,
        got_own,
        got_mate,
        given_own,
        given_mate,
        gain_feed,
        feed_in,
        feed_out,
        vmem=36,
        loads=(feed_in, feed_out),
        name="feed_second",
        after=(all_given,),
    )
    got_own, got_mate = send(part_mate, 1, high), send(part_own, 1, high)
    middle1_own, middle1_mate, grad1_turned = call(
        middle_second_back_kernel,
        [slot, slot, pair_turned],
        mid1_own,
        mid1_mate,
        given_own,
        given_mate,
        part_own,
        part_mate,
        got_own,
        got_mate,
        gain_feed,
        free=(got_own, got_mate),
        name="middle_second_back",
    )

    def attn_back(which, grad, x, first, *dfirst, mixing=False, after=()):
        outs = [slot] + [half_turned if which else pair_half_turned] * mixing
        return call(
            functools.partial(attn_back_kernel, mixing, which),
            outs,
            ends,
            levels,
            grad,
            x,
            gain_attn,
            inward,
            outward,
            first,
            *dfirst,
            smem=2,
            name="attn_back",
            after=after,
            free=(first,),
        )

    part_mate, dfirst_mate = attn_back(1, middle1_mate, x1_mate, first_over, mixing=True)
    got_own = send(part_mate, 1, high)
    part_own, dfirst_both = attn_back(0, middle1_own, x1_own, first_over, dfirst_mate, mixing=True)
    dfirst = send(dfirst_both, 2, high)
    grad_x1 = call(
        input_back_kernel,
        [slot_turned],
        x1_own,
        middle1_own,
        part_own,
        got_own,
        gain_attn,
        name="input_back",
        free=(got_own,),
    )[0]
    grad_own, grad_mate = send(grad_x1, 2, high), send(grad_x1, 3, high)

    received = (grad_own, grad_mate, dfirst)
    late = call(
        late_kernel, [slot_turned], is_lower, grad_own, mid1_turned, smem=1, name="late", free=received
    )[0]
    part_own, part_mate = call(
        feed_first_back_kernel,
        [slot, slot],
        mid0_own,
        mid0_mate,
        grad_own,
        grad_mate,
        gain_feed,
        feed_in,
        feed_out,
        vmem=36,
        loads=(feed_in, feed_out),
        free=received,
        name="feed_first_back",
        after=(late, all_middle),
    )
    got_own, got_mate = send(part_mate, 1, low), send(part_own, 1, low)
    middle_own, middle_mate, last = call(
        middle_first_back_kernel,
        [slot, slot, shape_of((2 * model + 2 * width, count), BF)],
        is_lower,
        mid0_own,
        mid0_mate,
        grad_own,
        grad_mate,
        part_own,
        part_mate,
        got_own,
        got_mate,
        gain_feed,
        grad1_turned,
        dfirst,
        first_over,
        smem=1,
        free=(got_own, got_mate) + received,
        name="middle_first_back",
    )

    place = jnp.stack([section ^ mask for mask in range(sections)]).astype(jnp.int32)

    late_every, late_mate = own_gathered(late, [middle_own])
    part_mate = attn_back(1, middle_mate, given_mate, dfirst, after=(late_every,))[0]
    part_own = attn_back(0, middle_own, given_own, dfirst, after=(part_mate,))[0]

    all_ends = all_given[:, :, model, : ends.shape[1]].reshape(2 * group, -1).astype(jnp.int32)
    core_at = core.astype(jnp.int32)[None]
    half = (section % 2).astype(jnp.int32)[None]
    pick = jnp.concatenate([1 - is_lower, core_at, core_at, half])
    squares = pl.pallas_call(
        square_sum_kernel,
        grid_spec=pltpu.PrefetchScalarGridSpec(
            num_scalar_prefetch=1,
            grid=(1,),
            in_specs=[pl.BlockSpec((group, 1, 16, count), lambda i, unused: (0, 0, model // 16, 0))],
            out_specs=pl.BlockSpec((1, 128), lambda i, unused: (0, 0)),
        ),
        out_shape=pltpu.HBM((1, 128), F32),
        compiler_params=pltpu.CompilerParams(vmem_limit_bytes=4 * MIB),
        name="square_sum",
    )(is_lower, in_hbm(all_middle))

    pieces = call(
        split_kernel,
        [shape_of((4 * count + 16, piece), BF)] * sections,
        place,
        part_own,
        part_mate,
        out_own,
        out_mate,
        squares,
        smem=1,
        name="split",
    )
    scores = attn_scores(
        (pick, all_ends),
        (set_given, set_middle),
        gain_attn,
        inward_turned,
        model,
        (late_every,),
    )
    set_late = own_blocks(late_every, gate(late_mate, [pieces[0], scores[2]]))
    all_last = everywhere(last)
    set_last = [(all_last, (d,), at, None) for d in range(group) for at in (0, model)]
    set_first = [(all_last, (d,), 2 * model + at, None) for d in range(group) for at in (0, width)]
    d_feed_in, d_feed_out, low_in, low_out, dots_feed = weight_call(
        feed_weights_kernel,
        (pick,),
        ((set_middle, set_late), (set_late, set_given)),
        (),
        (gain_feed,),
        (feed_in_turned, feed_out, feed_in),
        "feed_weights",
        after=(pieces[0], scores[2]),
    )
    received = [send(pieces[mask], mask) for mask in range(1, sections)]
    dinput, out, squares = call(
        join_kernel,
        [shape_of((2 * count, piece), F32), shape_of((2 * count, piece), BF), shape_of((1, 128), F32)],
        jnp.stack([lower, even]).astype(jnp.int32),
        pieces[0],
        *received,
        smem=1,
        name="join",
        free=received,
        after=(low_in,),
    )
    if dp > group:
        squares = lax.psum(squares, "dp") / group
    norms = squares[0, :2] / (micro * count * dp * 2 * width)
    d_feed_in, d_feed_out = filled(core_at, other_core(low_in), other_core(low_out), d_feed_in, d_feed_out)
    d_in, d_out, low_in, low_out, dots_attn = weight_call(
        attn_weights_kernel,
        (pick, mix_level),
        ((set_last, set_last), (set_first, set_first)),
        scores,
        (),
        (outward, inward),
        "attn_weights",
        after=(dinput,),
    )
    d_in, d_out = filled(core_at, other_core(low_in), other_core(low_out), d_in, d_out, (d_feed_in,))

    mine, sent = jnp.where(even, dots_attn, dots_feed), jnp.where(even, dots_feed, dots_attn)
    both = [(s * dp + i, (s ^ 1) * dp + (i ^ 1)) for s in range(sections) for i in range(dp)]
    d_gain = mine + send(sent, 1) + other_core(mine) + lax.ppermute(sent, ("section", "dp"), both)
    if dp > group:
        d_gain = lax.psum(d_gain, "dp") / group
        across = [list(range(at, dp, group)) for at in range(group)]
        d_in, d_out, d_feed_in, d_feed_out = [
            lax.psum(x.astype(BF), "dp", axis_index_groups=across).astype(F32)
            for x in (d_in, d_out, d_feed_in, d_feed_out)
        ]
    d_gain = d_gain / gains
    return (out, dinput, d_gain, d_in, d_out, d_feed_in, d_feed_out, norms[0], norms[1])


def solution(mesh):
    in_specs = (
        P("dp", "section"),
        P("dp", "section"),
        P("section", None),
        P("section", None, None),
        P("section", None, None),
        P("section", None, None),
        P("section", None, None),
        P(),
        P("dp", None),
    )
    out_specs = (
        P("dp", "section"),
        P("dp", "section"),
        P("section", None),
        P("section", None, None),
        P("section", None, None),
        P("section", None, None),
        P("section", None, None),
        P(),
        P(),
    )
    return jax.shard_map(body, mesh=mesh, in_specs=in_specs, out_specs=out_specs, check_vma=False)
```
